32 devices in a mesh: node: 8 (over z, y), samp: 4 (over x, core).
Axes of the slice: x: 2, y: 2, z: 4, core: 2. Of those that a mesh axis runs over, the one named last changes fastest.
Arguments:
- snapshots: bfloat16 [65536, 2048], P('node', 'samp'), may hold values from -330 to 330
- sketch_matrix: bfloat16 [2048, 160], P('samp'), may hold values from -0.125 to 0.125
Outputs:
- core_rows: float32 [65536, 160], P(('node', 'samp'))
- next_rows: float32 [10240, 32], P('node', 'samp')
The draws below stay inside these ranges and needn't reach their ends.
All inputs are finite; a program needn't handle non-finite values.
Results may differ from the reference program's by a relative error of at most 0.00045.
Values may be sent and summed in bfloat16 or wider, within the bound.
No kernel may reach another device: no remote copies, remote signals or barrier semaphores. Data moves between devices by JAX's collectives and lax.ppermute only.
A program may use at most 64 MiB of HBM per device.

```python
import math
import jax
import jax.numpy as jnp
from jax import lax

ROWS_DEV = 8192
R = 160
P1 = 64
P2 = 32
NODES = 65536
SAMPLES = 2048
N_NODE = 8


def draw_snapshots(key, part):
    key_noise, key_rows, key_cols, key_mode_rows, key_mode_cols = jax.random.split(key, 5)
    position = jnp.arange(NODES, dtype=jnp.float32) / NODES
    noise_part = jax.random.truncated_normal(key_noise, -4.0, 4.0, (NODES, SAMPLES), jnp.float32)
    row_spread = math.log(10.0)
    common = 0.8
    row_scale = jnp.exp(jax.random.uniform(key_rows, (NODES,), jnp.float32, 0.0, row_spread)) * (1.0 + 2.0 * position)
    col_scale = jnp.exp(jax.random.uniform(key_cols, (SAMPLES,), jnp.float32, 0.0, math.log(10.0)))
    mode_rows = jax.random.truncated_normal(key_mode_rows, -3.0, 3.0, (NODES,), jnp.float32)
    mode_cols = jax.random.truncated_normal(key_mode_cols, -3.0, 3.0, (SAMPLES,), jnp.float32)
    values = row_scale[:, None] * col_scale[None, :] * (noise_part + common * mode_rows[:, None] * mode_cols[None, :])
    return (0.05 * values).astype(jnp.bfloat16)


def levels(key, extent, shards, low, top_value):
    loudness = 1.0
    for dim, shards_of in shards:
        heights = jax.random.uniform(jax.random.fold_in(jax.random.fold_in(key, 6), dim), (shards_of,), jnp.float32, low / len(shards), top_value / len(shards))
        loudness = loudness * jnp.repeat(jnp.exp(heights), extent[dim] // shards_of).reshape((-1,) + (1,) * (len(extent) - 1 - dim))
    return loudness


def gaussian(rng, extent, deviation, bound, shards=(), kind=jnp.bfloat16):
    array = deviation * jax.random.normal(rng, extent, jnp.float32)
    if shards:
        array = array * levels(rng, extent, shards, -0.22, 0.18)
    return jnp.clip(array, -bound, bound).astype(kind)


def setup_inputs(seed: int = 0) -> dict:
    key_of = jax.random.split(jax.random.key(seed), 3)
    return {
        "snapshots": draw_snapshots(jax.random.fold_in(key_of[2], 71), 0),
        "sketch_matrix": gaussian(key_of[1], (SAMPLES, R), (P1 * P2) ** -0.5, 0.125, ((0, 4),)),
    }


def reference(snapshots, sketch_matrix):
    row_blocks = snapshots.reshape(N_NODE, ROWS_DEV, P1 * P2)

    def sketch_block(row_block):
        return jnp.dot(row_block.astype(jnp.float32), sketch_matrix.astype(jnp.float32), preferred_element_type=jnp.float32)
    sketched = lax.map(sketch_block, row_blocks).reshape(NODES, R)
    gram_matrix = jnp.dot(sketched.T.astype(jnp.float32), sketched.astype(jnp.float32), precision=lax.Precision.HIGHEST, preferred_element_type=jnp.float32) / NODES
    factor_lower = jnp.linalg.cholesky(gram_matrix)
    identity = jnp.eye(R, dtype=jnp.float32)
    inverse = lax.linalg.triangular_solve(factor_lower, identity, left_side=True, lower=True)
    core_rows = jnp.dot(sketched.astype(jnp.float32), inverse.T.astype(jnp.float32), precision=lax.Precision.HIGHEST, preferred_element_type=jnp.float32)
    basis_rows = core_rows.astype(jnp.bfloat16).reshape(N_NODE, ROWS_DEV, R)

    def project_block(paired):
        return jnp.dot(paired[0].T.astype(jnp.float32), paired[1].astype(jnp.float32), preferred_element_type=jnp.float32)
    partial_sums = lax.map(project_block, (basis_rows, row_blocks))
    coefficients = jnp.sum(partial_sums, axis=0) / NODES
    next_rows = coefficients.reshape(R, P1, P2).transpose(1, 0, 2).reshape(P1 * R, P2)
    return (core_rows, next_rows)
```

```python
import functools
import jax
import jax.numpy as jnp
from jax import lax
from jax.experimental import pallas as pl
from jax.experimental.pallas import tpu as pltpu
from jax.sharding import PartitionSpec as P

P1 = 64
P2 = 32
BAND = 32
F32 = jnp.float32
BF16 = jnp.bfloat16
HI = lax.Precision.HIGHEST
VMEM_LIMIT = 48 * 1024 * 1024


def iota(shape, dim):
    return lax.broadcasted_iota(jnp.int32, shape, dim)


def dot(a, b, dims, precision=None):
    return lax.dot_general(a, b, (dims, ((), ())), precision=precision, preferred_element_type=F32)


def params():
    return pltpu.CompilerParams(vmem_limit_bytes=VMEM_LIMIT)


def cost(flops, moved):
    return pl.CostEstimate(flops=int(flops), bytes_accessed=int(moved), transcendentals=0)


def sketch_kernel(ids_ref, x_ref, w_ref, o_ref):
    o_ref[...] = dot(w_ref[...], x_ref[...], ((1,), (1,)))


def sketch(ids, x, w_t, rows):
    rank, depth = w_t.shape
    steps = ids.shape[0]
    return pl.pallas_call(
        sketch_kernel,
        grid_spec=pltpu.PrefetchScalarGridSpec(
            num_scalar_prefetch=1,
            grid=(steps,),
            in_specs=[
                pl.BlockSpec((rows, depth), lambda i, ids: (ids[i], 0)),
                pl.BlockSpec((rank, depth), lambda i, ids: (0, 0)),
            ],
            out_specs=pl.BlockSpec((rank, rows), lambda i, ids: (0, i)),
        ),
        out_shape=jax.ShapeDtypeStruct((rank, steps * rows), F32),
        compiler_params=params(),
        cost_estimate=cost(2 * rank * depth * rows * steps, steps * rows * (depth * 2 + rank * 4)),
        name="sketch",
    )(ids, x, w_t)


def packing(rank):
    bands = rank // BAND
    pairs = [(i, j) for i in range(bands) for j in range(i, bands)]
    wide = 128 // BAND
    groups = -(-len(pairs) // wide)
    groups += groups % 2
    return pairs, wide, groups


def pack_gram(gram):
    pairs, wide, groups = packing(gram.shape[0])
    out = []
    for g in range(groups):
        chosen = pairs[g * wide:(g + 1) * wide]
        parts = [gram[i * BAND:(i + 1) * BAND, j * BAND:(j + 1) * BAND] for i, j in chosen]
        parts += [jnp.zeros((BAND, BAND), F32)] * (wide - len(chosen))
        out.append(jnp.concatenate(parts, axis=1))
    return jnp.concatenate(out, axis=0)


def gram_kernel(scale, a_ref, b_ref, s_ref, g_ref):
    s = a_ref[...] + b_ref[...]
    s_ref[...] = s
    g_ref[...] = pack_gram(dot(s, s, ((1,), (1,)), HI) * scale)


def own_gram(a, b, scale):
    rank, rows = a.shape
    groups = packing(rank)[2]
    return pl.pallas_call(
        functools.partial(gram_kernel, scale),
        out_shape=(
            jax.ShapeDtypeStruct((rank, rows), F32),
            jax.ShapeDtypeStruct((groups * BAND, 128), F32),
        ),
        compiler_params=params(),
        cost_estimate=cost(12 * rank * rank * rows, 16 * rank * rows),
        name="gram",
    )(a, b)


def wide_lanes(x, n):
    reps = -(-n // 128)
    return jnp.concatenate([x] * reps, axis=1)[:, :n] if reps > 1 else x[:, :n]


def band_rows(block, b):
    n = block.shape[1]
    count = BAND // 8
    part = [block[8 * i:8 * i + 8, :] for i in range(count)]
    sub = iota((8, n), 0)
    lane = iota((8, n), 1)
    for m in range(count):
        c0 = b * BAND + 8 * m
        live = count - m
        col = [
            [jnp.broadcast_to(part[m + i][:, c0 + k:c0 + k + 1], (8, 128)) for i in range(live)]
            for k in range(8)
        ]
        here = (lane >= c0) & (lane < c0 + 8)
        part[m] = jnp.where(here, jnp.where(lane - c0 == sub, 1.0, 0.0), part[m])
        for i in range(1, live):
            part[m + i] = jnp.where(here, 0.0, part[m + i])
        for j in range(8):
            inv_root = lax.rsqrt(jnp.broadcast_to(col[j][0][j:j + 1, :], (8, 128)))
            low = [x * inv_root for x in col[j]]
            for k in range(j + 1, 8):
                t = jnp.broadcast_to(low[0][k:k + 1, :], (8, 128))
                for i in range(live):
                    col[k][i] = col[k][i] - low[i] * t
            row = jnp.broadcast_to(part[m][j:j + 1, :], (8, n)) * wide_lanes(inv_root, n)
            for i in range(live):
                new = part[m + i] - wide_lanes(low[i], n) * row
                if i == 0:
                    new = jnp.where(sub > j, new, jnp.where(sub == j, row, part[m]))
                part[m + i] = new
    return jnp.concatenate(part, axis=0)


def factor_kernel(rank, g_ref, o_ref):
    pairs, wide, _ = packing(rank)
    o_ref[...] = jnp.zeros((rank, rank), F32)
    for at, (i, j) in enumerate(pairs):
        g, k = at // wide, at % wide
        o_ref[i * BAND:(i + 1) * BAND, j * BAND:(j + 1) * BAND] = g_ref[
            g * BAND:(g + 1) * BAND, k * BAND:(k + 1) * BAND]
    for b in range(rank // BAND):
        lo, hi = b * BAND, (b + 1) * BAND
        r = band_rows(o_ref[lo:hi, :], b)
        rows, cols = iota(r.shape, 0), iota(r.shape, 1)
        r = jnp.where((cols >= lo) & (cols < hi) & (cols - lo > rows), 0.0, r)
        o_ref[lo:hi, :] = jnp.where(cols < hi, r, 0.0)
        if hi < rank:
            left = jnp.where(cols >= hi, r, 0.0)
            update = dot(left, r, ((0,), (0,)), HI)
            kept = jnp.where(iota((rank - hi, rank), 1) // BAND == b, 0.0, o_ref[hi:, :])
            o_ref[hi:, :] = kept - update[hi:, :]


def factor_inverse(packed, rank):
    return pl.pallas_call(
        functools.partial(factor_kernel, rank),
        out_shape=jax.ShapeDtypeStruct((rank, rank), F32),
        compiler_params=params(),
        cost_estimate=cost(8e9, 4 * rank * rank),
        name="factor",
    )(packed)


def project_kernel(count, ids_ref, *refs):
    s_refs, x_refs = refs[:count], refs[count:2 * count]
    o_ref = refs[-1]
    rank = o_ref.shape[0]

    @pl.when(pl.program_id(0) == 0)
    def _():
        o_ref[...] = refs[2 * count][...] if len(refs) > 2 * count + 1 else jnp.zeros_like(o_ref)

    for s_ref, x_ref in zip(s_refs, x_refs):
        s = s_ref[...]
        high = s.astype(BF16)
        low = (s - high.astype(F32)).astype(BF16)
        both = dot(jnp.concatenate([high, low], axis=0), x_ref[...], ((1,), (0,)))
        o_ref[...] += both[:rank] + both[rank:]


def project(ids, parts, x, base, rows):
    count = len(parts)
    rank, span = parts[0].shape
    depth = x.shape[1]
    steps = span // rows
    bases = [] if base is None else [base]
    return pl.pallas_call(
        functools.partial(project_kernel, count),
        grid_spec=pltpu.PrefetchScalarGridSpec(
            num_scalar_prefetch=1,
            grid=(steps,),
            in_specs=[pl.BlockSpec((rank, rows), lambda i, ids: (0, i))] * count
            + [
                pl.BlockSpec((rows, depth), lambda i, ids, k=k: (ids[k] * steps + i, 0))
                for k in range(count)
            ]
            + [pl.BlockSpec((rank, depth), lambda i, ids: (0, 0))] * len(bases),
            out_specs=pl.BlockSpec((rank, depth), lambda i, ids: (0, 0)),
        ),
        out_shape=jax.ShapeDtypeStruct((rank, depth), F32),
        compiler_params=params(),
        cost_estimate=cost(4 * rank * depth * span * count, span * count * (depth * 2 + rank * 4)),
        name="project",
    )(ids, *parts, *([x] * count), *bases)


def folding(rank, width):
    best = 1
    for f in range(1, rank + 1):
        if rank % f == 0 and (rank // f) % 8 == 0 and f * width <= 128:
            best = f
    return best


def regroup_kernel(pieces, samp, per_node, width_cols, me_ref, t_ref, *refs):
    outs, hold = refs[:pieces], refs[pieces]
    rank, depth = t_ref.shape
    width = per_node * width_cols
    fold = folding(rank, width)
    tall = rank // fold
    dst = iota((depth, depth), 1)
    src = iota((depth, depth), 0)
    a, rest = dst // (samp * width), dst % (samp * width)
    s, rest = rest // width, rest % width
    want = (a * per_node + rest // width_cols) * (samp * width_cols) + s * width_cols + rest % width_cols
    move = jnp.where(src == want, 1.0, 0.0).astype(BF16)
    t = t_ref[...]
    high = t.astype(BF16)
    mid = (t - high.astype(F32)).astype(BF16)
    low = (t - high.astype(F32) - mid.astype(F32)).astype(BF16)
    moved = dot(jnp.concatenate([high, mid, low], axis=0), move, ((1,), (0,)))
    moved = moved[:rank] + moved[rank:2 * rank] + moved[2 * rank:]
    for i in range(pieces):
        piece = moved[:, i * width:(i + 1) * width]
        hold[i] = jnp.concatenate([piece[f * tall:(f + 1) * tall] for f in range(fold)], axis=1)
    me = me_ref[0]
    for k, out in enumerate(outs):
        out[...] = hold[me ^ k]


def regroup(me, t, samp, node, per_node, width_cols):
    rank, depth = t.shape
    width = per_node * width_cols
    fold = folding(rank, width)
    shape = (rank // fold, fold * width)
    return pl.pallas_call(
        functools.partial(regroup_kernel, node, samp, per_node, width_cols),
        in_specs=[pl.BlockSpec(memory_space=pltpu.SMEM), pl.BlockSpec(memory_space=pltpu.VMEM)],
        out_shape=[jax.ShapeDtypeStruct(shape, F32)] * node,
        scratch_shapes=[pltpu.VMEM((node,) + shape, F32)],
        compiler_params=params(),
        cost_estimate=cost(6 * rank * depth * depth, 8 * rank * depth),
        name="regroup",
    )(me, t)


def core_kernel(inv_ref, s_ref, o_ref):
    o_ref[...] = dot(inv_ref[...], s_ref[...], ((1,), (0,)), HI)


def core_product(inverse, s):
    rank, rows = s.shape
    return pl.pallas_call(
        core_kernel,
        out_shape=jax.ShapeDtypeStruct((rank, rows), F32),
        compiler_params=params(),
        cost_estimate=cost(12 * rank * rank * rows, 8 * rank * rows),
        name="core",
    )(inverse, s)


def coefficient_kernel(scale, per_node, width_cols, inv_ref, *refs):
    pieces, o_ref = refs[:-1], refs[-1]
    rank = inv_ref.shape[0]
    total = pieces[0][...]
    for p in pieces[1:]:
        total = total + p[...]
    width = per_node * width_cols
    fold = total.shape[1] // width
    total = jnp.concatenate([total[:, f * width:(f + 1) * width] for f in range(fold)], axis=0)
    out = dot(total, inv_ref[...], ((0,), (1,)), HI) * scale
    o_ref[...] = jnp.concatenate(
        [out[p * width_cols:(p + 1) * width_cols, :] for p in range(per_node)], axis=1)


def coefficients(inverse, pieces, scale, per_node, width_cols):
    rank = inverse.shape[0]
    return pl.pallas_call(
        functools.partial(coefficient_kernel, scale, per_node, width_cols),
        out_shape=jax.ShapeDtypeStruct((width_cols, per_node * rank), F32),
        compiler_params=params(),
        cost_estimate=cost(12 * rank * rank * per_node * width_cols, 4 * rank * rank),
        name="coefficient",
    )(inverse, *pieces)


def swap(value, axis, size, bit):
    return lax.ppermute(value, axis, [(i, i ^ bit) for i in range(size)])


def body(snapshots, sketch_matrix):
    rows_all = snapshots.shape[0]
    rank = sketch_matrix.shape[1]
    samp = lax.axis_size("samp")
    node = lax.axis_size("node")
    total = rows_all * node
    quarter = rows_all // samp
    rows = min(quarter, 1024)
    steps = quarter // rows
    me_s = lax.axis_index("samp").astype(jnp.int32)
    me_n = lax.axis_index("node").astype(jnp.int32)
    w_t = sketch_matrix.T

    def block_ids(d):
        return jnp.stack([(me_s ^ d) * steps + i for i in range(steps)])

    order = sorted(range(samp), key=lambda d: (-(d // 2), -(d % 2)))
    part = {d: sketch(block_ids(d), snapshots, w_t, rows) for d in order}

    held = dict(part)
    bit = 1
    while bit * 2 < samp:
        got = {d ^ bit: swap(held.pop(d), "samp", samp, bit) for d in order if d in held and d & bit}
        for d in got:
            held[d] = held[d] + got[d]
        bit *= 2
    last = bit
    ours, theirs = held[0], held[last]
    arrived = swap(theirs, "samp", samp, last)
    short = swap(ours.astype(BF16), "samp", samp, last)
    own, gram = own_gram(ours, arrived, 1.0 / total)

    full = {0: own, last: theirs + short.astype(F32)}
    bit = last // 2
    while bit:
        full.update({d ^ bit: swap(full[d], "samp", samp, bit) for d in list(full)})
        bit //= 2

    upper = (me_s & 1) == 1
    halves = jnp.split(gram, 2, axis=0)
    mine = jnp.where(upper, halves[1], halves[0])
    mine = mine + swap(jnp.where(upper, halves[0], halves[1]), "samp", samp, 1)
    bit = 2
    while bit < samp:
        mine = mine + swap(mine, "samp", samp, bit)
        bit *= 2
    bit = 1
    while bit < node:
        mine = mine + swap(mine, "node", node, bit)
        bit *= 2
    other = swap(mine, "samp", samp, 1)
    packed = jnp.concatenate([jnp.where(upper, other, mine), jnp.where(upper, mine, other)], axis=0)
    inverse = factor_inverse(packed, rank)

    def ids(ds):
        return jnp.stack([me_s ^ d for d in ds])

    t = project(ids([0]), [full[0]], snapshots, None, rows)
    t = project(ids([last]), [full[last]], snapshots, t, rows)
    rest = [d for d in full if d not in (0, last)]
    if rest:
        t = project(ids(rest), [full[d] for d in rest], snapshots, t, rows)

    per_node = P1 // node
    width_cols = P2 // samp
    spread = node // samp
    pieces = regroup(me_n[None], t, samp, node, per_node, width_cols)
    landed = []
    for k in range(node):
        pairs = []
        for n in range(node):
            a, s_to = (n ^ k) // samp, (n ^ k) % samp
            for s_from in range(samp):
                pairs.append((n * samp + s_from, (s_from * spread + a) * samp + s_to))
        landed.append(lax.ppermute(pieces[k], ("node", "samp"), pairs))
    core = core_product(inverse, own)
    coef = coefficients(inverse, landed, 1.0 / total, per_node, width_cols)
    return (core.T, coef.T)


def solution(mesh):
    placed = (P("node", "samp"), P("samp", None))
    return jax.shard_map(
        body,
        mesh=mesh,
        in_specs=placed,
        out_specs=(P(("node", "samp"), None), P("node", "samp")),
        check_vma=False,
    )
```

```python
import functools
import jax
import jax.numpy as jnp
from jax import lax
from jax.experimental import pallas as pl
from jax.experimental.pallas import tpu as pltpu
from jax.sharding import PartitionSpec as P

P1 = 64
P2 = 32
BAND = 32
CHUNKS = 2
F32 = jnp.float32
BF16 = jnp.bfloat16
HI = lax.Precision.HIGHEST
VMEM_LIMIT = 48 * 1024 * 1024


def iota(shape, dim):
    return lax.broadcasted_iota(jnp.int32, shape, dim)


def dot(a, b, dims, precision=None):
    return lax.dot_general(a, b, (dims, ((), ())), precision=precision, preferred_element_type=F32)


def params():
    return pltpu.CompilerParams(vmem_limit_bytes=VMEM_LIMIT)


def cost(flops, moved):
    return pl.CostEstimate(flops=int(flops), bytes_accessed=int(moved), transcendentals=0)


def sketch_kernel(ids_ref, x_ref, w_ref, o_ref):
    o_ref[...] = dot(w_ref[...], x_ref[...], ((1,), (1,)))


def sketch(ids, x, w_t, rows):
    rank, depth = w_t.shape
    steps = ids.shape[0]
    return pl.pallas_call(
        sketch_kernel,
        grid_spec=pltpu.PrefetchScalarGridSpec(
            num_scalar_prefetch=1,
            grid=(steps,),
            in_specs=[
                pl.BlockSpec((rows, depth), lambda i, ids: (ids[i], 0)),
                pl.BlockSpec((rank, depth), lambda i, ids: (0, 0)),
            ],
            out_specs=pl.BlockSpec((rank, rows), lambda i, ids: (0, i)),
        ),
        out_shape=jax.ShapeDtypeStruct((rank, steps * rows), F32),
        compiler_params=params(),
        cost_estimate=cost(2 * rank * depth * rows * steps, steps * rows * (depth * 2 + rank * 4)),
        name="sketch",
    )(ids, x, w_t)


def packing(rank):
    bands = rank // BAND
    pairs = [(i, j) for i in range(bands) for j in range(i, bands)]
    wide = 128 // BAND
    groups = -(-len(pairs) // wide)
    groups += groups % 2
    return pairs, wide, groups


def pack_gram(gram):
    pairs, wide, groups = packing(gram.shape[0])
    out = []
    for g in range(groups):
        chosen = pairs[g * wide:(g + 1) * wide]
        parts = [gram[i * BAND:(i + 1) * BAND, j * BAND:(j + 1) * BAND] for i, j in chosen]
        parts += [jnp.zeros((BAND, BAND), F32)] * (wide - len(chosen))
        out.append(jnp.concatenate(parts, axis=1))
    return jnp.concatenate(out, axis=0)


def split_kernel(a_ref, b_ref, both_ref, high_ref):
    rank = a_ref.shape[0]
    s = a_ref[...] + b_ref[...]
    high = s.astype(BF16)
    high_ref[...] = high
    both_ref[:rank, :] = high
    both_ref[rank:, :] = (s - high.astype(F32)).astype(BF16)


def split_sum(a, b):
    rank, rows = a.shape
    return pl.pallas_call(
        split_kernel,
        out_shape=(
            jax.ShapeDtypeStruct((2 * rank, rows), BF16),
            jax.ShapeDtypeStruct((rank, rows), BF16),
        ),
        compiler_params=params(),
        cost_estimate=cost(4 * rank * rows, 14 * rank * rows),
        name="split",
    )(a, b)


def fold_square(x, rank):
    return (x[:rank, :rank] + x[rank:, rank:]) + (x[:rank, rank:] + x[rank:, :rank])


def gram_kernel(*refs):
    o_ref = refs[-1]
    rank = o_ref.shape[0]
    total = None
    for ref in refs[:-1]:
        both = ref[...]
        term = dot(both, both, ((1,), (1,)))
        total = term if total is None else total + term
    o_ref[...] = fold_square(total, rank)


def local_gram(pairs):
    rank, rows = pairs[0].shape[0] // 2, pairs[0].shape[1]
    return pl.pallas_call(
        gram_kernel,
        out_shape=jax.ShapeDtypeStruct((rank, rank), F32),
        compiler_params=params(),
        cost_estimate=cost(8 * rank * rank * rows * len(pairs), 4 * rank * rows * len(pairs)),
        name="gram",
    )(*pairs)


def cross_kernel(scale, count, *refs):
    own, got, far, near = (refs[k * count:(k + 1) * count] for k in range(4))
    g_ref, o_ref = refs[4 * count], refs[4 * count + 1]
    rank = g_ref.shape[0]
    total = None
    for own_ref, got_ref, far_ref, near_ref in zip(own, got, far, near):
        term = dot(own_ref[...], got_ref[...], ((1,), (1,)))
        term = term[:rank] + term[rank:]
        term = term + dot(near_ref[...], far_ref[rank:, :], ((1,), (1,)))
        total = term if total is None else total + term
    o_ref[...] = pack_gram((g_ref[...] + (total + total.T)) * scale)


def cross_gram(own, got, far, near, gram, scale):
    rank = gram.shape[0]
    rows = got[0].shape[1] * len(got)
    groups = packing(rank)[2]
    return pl.pallas_call(
        functools.partial(cross_kernel, scale, len(own)),
        out_shape=jax.ShapeDtypeStruct((groups * BAND, 128), F32),
        compiler_params=params(),
        cost_estimate=cost(6 * rank * rank * rows, 12 * rank * rows),
        name="cross",
    )(*own, *got, *far, *near, gram)


def wide_lanes(x, n):
    reps = -(-n // 128)
    return jnp.concatenate([x] * reps, axis=1)[:, :n] if reps > 1 else x[:, :n]


def band_rows(block, b):
    n = block.shape[1]
    count = BAND // 8
    part = [block[8 * i:8 * i + 8, :] for i in range(count)]
    sub = iota((8, n), 0)
    lane = iota((8, n), 1)
    for m in range(count):
        c0 = b * BAND + 8 * m
        live = count - m
        col = [
            [jnp.broadcast_to(part[m + i][:, c0 + k:c0 + k + 1], (8, 128)) for i in range(live)]
            for k in range(8)
        ]
        here = (lane >= c0) & (lane < c0 + 8)
        part[m] = jnp.where(here, jnp.where(lane - c0 == sub, 1.0, 0.0), part[m])
        for i in range(1, live):
            part[m + i] = jnp.where(here, 0.0, part[m + i])
        for j in range(8):
            inv_root = lax.rsqrt(jnp.broadcast_to(col[j][0][j:j + 1, :], (8, 128)))
            low = [x * inv_root for x in col[j]]
            for k in range(j + 1, 8):
                t = jnp.broadcast_to(low[0][k:k + 1, :], (8, 128))
                for i in range(live):
                    col[k][i] = col[k][i] - low[i] * t
            row = jnp.broadcast_to(part[m][j:j + 1, :], (8, n)) * wide_lanes(inv_root, n)
            for i in range(live):
                new = part[m + i] - wide_lanes(low[i], n) * row
                if i == 0:
                    new = jnp.where(sub > j, new, jnp.where(sub == j, row, part[m]))
                part[m + i] = new
    return jnp.concatenate(part, axis=0)


def factor_kernel(rank, g_ref, o_ref):
    pairs, wide, _ = packing(rank)
    o_ref[...] = jnp.zeros((rank, rank), F32)
    for at, (i, j) in enumerate(pairs):
        g, k = at // wide, at % wide
        o_ref[i * BAND:(i + 1) * BAND, j * BAND:(j + 1) * BAND] = g_ref[
            g * BAND:(g + 1) * BAND, k * BAND:(k + 1) * BAND]
    for b in range(rank // BAND):
        lo, hi = b * BAND, (b + 1) * BAND
        r = band_rows(o_ref[lo:hi, :], b)
        rows, cols = iota(r.shape, 0), iota(r.shape, 1)
        r = jnp.where((cols >= lo) & (cols < hi) & (cols - lo > rows), 0.0, r)
        o_ref[lo:hi, :] = jnp.where(cols < hi, r, 0.0)
        if hi < rank:
            left = jnp.where(cols >= hi, r, 0.0)
            update = dot(left, r, ((0,), (0,)), HI)
            kept = jnp.where(iota((rank - hi, rank), 1) // BAND == b, 0.0, o_ref[hi:, :])
            o_ref[hi:, :] = kept - update[hi:, :]


def factor_inverse(packed, rank):
    return pl.pallas_call(
        functools.partial(factor_kernel, rank),
        out_shape=jax.ShapeDtypeStruct((rank, rank), F32),
        compiler_params=params(),
        cost_estimate=cost(8e9, 4 * rank * rank),
        name="factor",
    )(packed)


def project_kernel(count, has_base, finish, ids_ref, *refs):
    s_refs, x_refs = refs[:count], refs[count:2 * count]
    rest = refs[2 * count + has_base:]
    t_ref = rest[-1]
    rank = t_ref.shape[0]

    @pl.when(pl.program_id(0) == 0)
    def _():
        t_ref[...] = refs[2 * count][...] if has_base else jnp.zeros_like(t_ref)

    total = None
    for s_ref, x_ref in zip(s_refs, x_refs):
        term = dot(s_ref[...], x_ref[...], ((1,), (0,)))
        total = term if total is None else total + term
    t_ref[...] += total if total.shape[0] == rank else total[:rank] + total[rank:]
    if finish is not None:
        @pl.when(pl.program_id(0) == pl.num_programs(0) - 1)
        def _():
            finish(t_ref[...], ids_ref[count], *rest[:-1])


def project(ids, parts, x, rank, base, rows, finish=None, outs=(), scratch=()):
    count = len(parts)
    height, span = parts[0].shape
    depth = x.shape[1]
    steps = span // rows
    bases = [] if base is None else [base]
    whole = pl.BlockSpec((rank, depth), lambda i, ids: (0, 0))
    t_shape = jax.ShapeDtypeStruct((rank, depth), F32)
    if finish is None:
        out_specs, out_shape, scratch_shapes = whole, t_shape, []
    else:
        out_specs = [pl.BlockSpec(o.shape, lambda i, ids: (0, 0, 0)) for o in outs]
        out_shape = list(outs)
        scratch_shapes = list(scratch) + [pltpu.VMEM((rank, depth), F32)]
    return pl.pallas_call(
        functools.partial(project_kernel, count, len(bases), finish),
        grid_spec=pltpu.PrefetchScalarGridSpec(
            num_scalar_prefetch=1,
            grid=(steps,),
            in_specs=[pl.BlockSpec((height, rows), lambda i, ids: (0, i))] * count
            + [
                pl.BlockSpec((rows, depth), lambda i, ids, k=k: (ids[k] * steps + i, 0))
                for k in range(count)
            ]
            + [whole] * len(bases),
            out_specs=out_specs,
            scratch_shapes=scratch_shapes,
        ),
        out_shape=out_shape,
        compiler_params=params(),
        cost_estimate=cost(2 * height * depth * span * count, span * count * (depth + height) * 2),
        name="project",
    )(ids, *parts, *([x] * count), *bases)


def folding(rank, width):
    best = 1
    for f in range(1, rank + 1):
        if rank % f == 0 and (rank // f) % 8 == 0 and f * width <= 128:
            best = f
    return best


def reverse_bits(p, count):
    return sum(1 << (count - 1 - b) for b in range(count) if (p >> b) & 1)


def regroup_tail(pieces, samp, per_node, width_cols, t, me, keep_ref, send_ref, hold):
    rank, depth = t.shape
    width = per_node * width_cols
    fold = folding(rank, width)
    tall = rank // fold
    dst = iota((depth, depth), 1)
    src = iota((depth, depth), 0)
    a, rest = dst // (samp * width), dst % (samp * width)
    s, rest = rest // width, rest % width
    want = (a * per_node + rest // width_cols) * (samp * width_cols) + s * width_cols + rest % width_cols
    move = jnp.where(src == want, 1.0, 0.0).astype(BF16)
    high = t.astype(BF16)
    mid = (t - high.astype(F32)).astype(BF16)
    low = (t - high.astype(F32) - mid.astype(F32)).astype(BF16)
    moved = dot(jnp.concatenate([high, mid, low], axis=0), move, ((1,), (0,)))
    moved = moved[:rank] + moved[rank:2 * rank] + moved[2 * rank:]
    for i in range(pieces):
        piece = moved[:, i * width:(i + 1) * width]
        hold[i] = jnp.concatenate([piece[f * tall:(f + 1) * tall] for f in range(fold)], axis=1)
    bits = pieces.bit_length() - 1
    for p in range(pieces):
        out = send_ref if p >= pieces // 2 else keep_ref
        out[p % (pieces // 2)] = hold[me ^ reverse_bits(p, bits)]


def core_kernel(count, inv_ref, *refs):
    both, high, low = (refs[k * count:(k + 1) * count] for k in range(3))
    o_ref = refs[-1]
    rank = inv_ref.shape[0]
    for c in range(count):
        s = both[c][:rank, :].astype(F32) + both[c][rank:, :].astype(F32)
        s = s + (high[c][...].astype(F32) + low[c][...].astype(F32))
        rows = s.shape[1]
        o_ref[:, c * rows:(c + 1) * rows] = dot(inv_ref[...], s, ((1,), (0,)), HI)


def core_product(inverse, both, high, low):
    rank, rows = high[0].shape
    count = len(both)
    return pl.pallas_call(
        functools.partial(core_kernel, count),
        out_shape=jax.ShapeDtypeStruct((rank, rows * count), F32),
        compiler_params=params(),
        cost_estimate=cost(12 * rank * rank * rows * count, 12 * rank * rows * count),
        name="core",
    )(inverse, *both, *high, *low)


def coefficient_kernel(scale, per_node, width_cols, inv_ref, *refs):
    pieces, o_ref = refs[:-1], refs[-1]
    rank = inv_ref.shape[0]
    total = pieces[0][...]
    for p in pieces[1:]:
        total = total + p[...]
    width = per_node * width_cols
    fold = total.shape[1] // width
    total = jnp.concatenate([total[:, f * width:(f + 1) * width] for f in range(fold)], axis=0)
    out = dot(total, inv_ref[...], ((0,), (1,)), HI) * scale
    o_ref[...] = jnp.concatenate(
        [out[p * width_cols:(p + 1) * width_cols, :] for p in range(per_node)], axis=1)


def coefficients(inverse, pieces, scale, per_node, width_cols):
    rank = inverse.shape[0]
    return pl.pallas_call(
        functools.partial(coefficient_kernel, scale, per_node, width_cols),
        out_shape=jax.ShapeDtypeStruct((width_cols, per_node * rank), F32),
        compiler_params=params(),
        cost_estimate=cost(12 * rank * rank * per_node * width_cols, 4 * rank * rank),
        name="coefficient",
    )(inverse, *pieces)


def swap(value, axis, size, bit):
    return lax.ppermute(value, axis, [(i, i ^ bit) for i in range(size)])


def body(snapshots, sketch_matrix):
    rows_all = snapshots.shape[0]
    rank = sketch_matrix.shape[1]
    samp = lax.axis_size("samp")
    node = lax.axis_size("node")
    total = rows_all * node
    quarter = rows_all // samp
    chunks = CHUNKS
    span = quarter // chunks
    every = range(chunks)
    me_s = lax.axis_index("samp").astype(jnp.int32)
    me_n = lax.axis_index("node").astype(jnp.int32)
    w_t = sketch_matrix.T
    last = samp // 2

    def chip_sum(base, c):
        ds = [base ^ d for d in range(last)]
        held = {}
        for d in sorted(ds, reverse=True):
            ids = ((me_s ^ d) * chunks + c)[None]
            held[d] = sketch(ids, snapshots, w_t, span)
        bit = 1
        while bit < last:
            for d in [d for d in held if d & bit]:
                got = swap(held.pop(d), "samp", samp, bit)
                if bit * 2 < last:
                    held[d ^ bit] = held[d ^ bit] + got
                else:
                    return split_sum(held[d ^ bit], got)
            bit *= 2

    far, far_high, own, own_high = [], [], [], []
    got_high, near_high = [], []
    for c in every:
        both, high = chip_sum(last, c)
        far.append(both)
        got_high.append(swap(high, "samp", samp, last))
    for c in every:
        both, high = chip_sum(0, c)
        own.append(both)
        near_high.append(swap(high, "samp", samp, last))
    got_low = []
    for c in every:
        low, _ = lax.optimization_barrier((far[c][rank:], got_high[c]))
        got_low.append(swap(low, "samp", samp, last))
    gram = local_gram(own + far)

    def spread_over(table):
        bit = last // 2
        while bit:
            table.update({d ^ bit: [swap(v, "samp", samp, bit) for v in table[d]] for d in list(table)})
            bit //= 2
        return table

    def ids_of(ds):
        return [(me_s ^ d) * chunks + c for d in ds for c in every]

    rows = min(span, 256)
    pairs = spread_over({0: own, last: far})
    t = project(jnp.stack(ids_of(pairs)), [v for d in pairs for v in pairs[d]], snapshots, rank, None, rows)

    packed = cross_gram(own, got_high, far, near_high, gram, 1.0 / total)
    upper = (me_s & 1) == 1
    halves = jnp.split(packed, 2, axis=0)
    mine = jnp.where(upper, halves[1], halves[0])
    mine = mine + swap(jnp.where(upper, halves[0], halves[1]), "samp", samp, 1)
    bit = 2
    while bit < samp:
        mine = mine + swap(mine, "samp", samp, bit)
        bit *= 2
    bit = 1
    while bit < node:
        mine = mine + swap(mine, "node", node, bit)
        bit *= 2
    other = swap(mine, "samp", samp, 1)
    packed = jnp.concatenate([jnp.where(upper, other, mine), jnp.where(upper, mine, other)], axis=0)
    inverse = factor_inverse(packed, rank)

    highs = spread_over({0: got_high, last: near_high})
    first = [0, last]
    t = project(jnp.stack(ids_of(first)), [v for d in first for v in highs[d]], snapshots, rank, t, rows)
    then = [d for d in highs if d not in first]
    per_node = P1 // node
    width_cols = P2 // samp
    width = per_node * width_cols
    fold = folding(rank, width)
    piece = (rank // fold, fold * width)
    keep, send = project(
        jnp.stack(ids_of(then) + [me_n]), [v for d in then for v in highs[d]], snapshots, rank, t, rows,
        functools.partial(regroup_tail, node, samp, per_node, width_cols),
        [jax.ShapeDtypeStruct((node // 2,) + piece, F32)] * 2,
        [pltpu.VMEM((node,) + piece, F32)])

    bit = 1
    while keep.shape[0] > 1:
        got = swap(send, "node", node, bit)
        half = keep.shape[0] // 2
        keep, send = keep[:half] + got[:half], keep[half:] + got[half:]
        bit *= 2
    spread = node // samp
    landed = []
    for k, value in ((0, keep), (bit, send)):
        route = []
        for n in range(node):
            a, s_to = (n ^ k) // samp, (n ^ k) % samp
            for s_from in range(samp):
                route.append((n * samp + s_from, (s_from * spread + a) * samp + s_to))
        landed.append(lax.ppermute(value[0], ("node", "samp"), route))
    core = core_product(inverse, own, got_high, got_low)
    coef = coefficients(inverse, landed, 1.0 / total, per_node, width_cols)
    return (core.T, coef.T)


def solution(mesh):
    placed = (P("node", "samp"), P("samp", None))
    return jax.shard_map(
        body,
        mesh=mesh,
        in_specs=placed,
        out_specs=(P(("node", "samp"), None), P("node", "samp")),
        check_vma=False,
    )
```

```python
import functools
import jax
import jax.numpy as jnp
from jax import lax
from jax.experimental import pallas as pl
from jax.experimental.pallas import tpu as pltpu
from jax.sharding import PartitionSpec as P

P1 = 64
P2 = 32
BAND = 32
CHUNKS = 2
COST_CUT = 1
F32 = jnp.float32
BF16 = jnp.bfloat16
HI = lax.Precision.HIGHEST
UNREAD = pl.BlockSpec(memory_space=pl.ANY)
HELD = pl.BlockSpec(memory_space=pltpu.VMEM)
VMEM_LIMIT = 56 * 1024 * 1024


def iota(shape, dim):
    return lax.broadcasted_iota(jnp.int32, shape, dim)


def dot(a, b, dims, precision=None):
    return lax.dot_general(a, b, (dims, ((), ())), precision=precision, preferred_element_type=F32)


def params():
    return pltpu.CompilerParams(vmem_limit_bytes=VMEM_LIMIT)


def cost(flops, moved):
    return pl.CostEstimate(flops=int(flops) // COST_CUT, bytes_accessed=int(moved) // COST_CUT, transcendentals=0)


def sketch_kernel(count, ids_ref, x_ref, *refs):
    w_refs, x_refs = refs[:count], (x_ref,) + refs[count:2 * count - 1]
    both_ref, high_ref = refs[-2:]
    rank = high_ref.shape[0]
    s = None
    for w_ref, ref in zip(w_refs, x_refs):
        term = dot(w_ref[...], ref[...], ((1,), (1,)))
        s = term if s is None else s + term
    high = s.astype(BF16)
    high_ref[...] = high
    both_ref[:rank, :] = high
    both_ref[rank:, :] = (s - high.astype(F32)).astype(BF16)


def sketch(ids, x, ws, extra, rows, after=()):
    rank, depth = ws[0].shape
    count = len(ws)
    return pl.pallas_call(
        functools.partial(sketch_kernel, count),
        grid_spec=pltpu.PrefetchScalarGridSpec(
            num_scalar_prefetch=1,
            grid=(1,),
            in_specs=[pl.BlockSpec((rows, depth), lambda i, ids: (ids[i], 0))]
            + [pl.BlockSpec((rank, depth), lambda i, ids: (0, 0))] * count
            + [pl.BlockSpec((rows, depth), lambda i, ids: (0, 0))] * (count - 1)
            + [UNREAD] * len(after),
            out_specs=[
                pl.BlockSpec((2 * rank, rows), lambda i, ids: (0, 0)),
                pl.BlockSpec((rank, rows), lambda i, ids: (0, 0)),
            ],
        ),
        out_shape=(
            jax.ShapeDtypeStruct((2 * rank, rows), BF16),
            jax.ShapeDtypeStruct((rank, rows), BF16),
        ),
        compiler_params=params(),
        cost_estimate=cost(2 * rank * depth * rows * count, rows * (depth * 2 * count + rank * 6)),
        name="sketch",
    )(ids, x, *ws, *extra, *after)


def packing(rank):
    bands = rank // BAND
    pairs = [(i, j) for i in range(bands) for j in range(i, bands)]
    wide = 128 // BAND
    groups = -(-len(pairs) // wide)
    groups += groups % 2
    return pairs, wide, groups


def pack_gram(gram):
    pairs, wide, groups = packing(gram.shape[0])
    out = []
    for g in range(groups):
        chosen = pairs[g * wide:(g + 1) * wide]
        parts = [gram[i * BAND:(i + 1) * BAND, j * BAND:(j + 1) * BAND] for i, j in chosen]
        parts += [jnp.zeros((BAND, BAND), F32)] * (wide - len(chosen))
        out.append(jnp.concatenate(parts, axis=1))
    return jnp.concatenate(out, axis=0)


def fold_square(x, rank):
    return (x[:rank, :rank] + x[rank:, rank:]) + (x[:rank, rank:] + x[rank:, :rank])


def gram_kernel(*refs):
    o_ref = refs[-1]
    rank = o_ref.shape[0]
    total = None
    for ref in refs[:-1]:
        both = ref[...]
        term = dot(both, both, ((1,), (1,)))
        total = term if total is None else total + term
    o_ref[...] = fold_square(total, rank)


def local_gram(pairs):
    rank, rows = pairs[0].shape[0] // 2, pairs[0].shape[1]
    return pl.pallas_call(
        gram_kernel,
        out_shape=jax.ShapeDtypeStruct((rank, rank), F32),
        compiler_params=params(),
        cost_estimate=cost(8 * rank * rank * rows * len(pairs), 4 * rank * rows * len(pairs)),
        name="gram",
    )(*pairs)


def cross_kernel(scale, count, *refs):
    own, got, far, near = (refs[k * count:(k + 1) * count] for k in range(4))
    g_ref, o_ref = refs[4 * count], refs[-1]
    rank = g_ref.shape[0]
    total = None
    for own_ref, got_ref, far_ref, near_ref in zip(own, got, far, near):
        term = dot(own_ref[...], got_ref[...], ((1,), (1,)))
        term = term[:rank] + term[rank:]
        term = term + dot(near_ref[...], far_ref[rank:, :], ((1,), (1,)))
        total = term if total is None else total + term
    o_ref[...] = pack_gram((g_ref[...] + (total + total.T)) * scale)


def cross_gram(own, got, far, near, gram, scale, after=()):
    rank = gram.shape[0]
    rows = got[0].shape[1] * len(got)
    groups = packing(rank)[2]
    return pl.pallas_call(
        functools.partial(cross_kernel, scale, len(own)),
        in_specs=[HELD] * (4 * len(own) + 1) + [UNREAD] * len(after),
        out_shape=jax.ShapeDtypeStruct((groups * BAND, 128), F32),
        compiler_params=params(),
        cost_estimate=cost(6 * rank * rank * rows, 12 * rank * rows),
        name="cross",
    )(*own, *got, *far, *near, gram, *after)


def wide_lanes(x, n):
    reps = -(-n // 128)
    return jnp.concatenate([x] * reps, axis=1)[:, :n] if reps > 1 else x[:, :n]


def band_rows(block, b):
    n = block.shape[1]
    count = BAND // 8
    part = [block[8 * i:8 * i + 8, :] for i in range(count)]
    sub = iota((8, n), 0)
    lane = iota((8, n), 1)
    for m in range(count):
        c0 = b * BAND + 8 * m
        live = count - m
        col = [
            [jnp.broadcast_to(part[m + i][:, c0 + k:c0 + k + 1], (8, 128)) for i in range(live)]
            for k in range(8)
        ]
        here = (lane >= c0) & (lane < c0 + 8)
        part[m] = jnp.where(here, jnp.where(lane - c0 == sub, 1.0, 0.0), part[m])
        for i in range(1, live):
            part[m + i] = jnp.where(here, 0.0, part[m + i])
        for j in range(8):
            inv_root = lax.rsqrt(jnp.broadcast_to(col[j][0][j:j + 1, :], (8, 128)))
            low = [x * inv_root for x in col[j]]
            for k in range(j + 1, 8):
                t = jnp.broadcast_to(low[0][k:k + 1, :], (8, 128))
                for i in range(live):
                    col[k][i] = col[k][i] - low[i] * t
            row = jnp.broadcast_to(part[m][j:j + 1, :], (8, n)) * wide_lanes(inv_root, n)
            for i in range(live):
                new = part[m + i] - wide_lanes(low[i], n) * row
                if i == 0:
                    new = jnp.where(sub > j, new, jnp.where(sub == j, row, part[m]))
                part[m + i] = new
    return jnp.concatenate(part, axis=0)


def factor_kernel(rank, g_ref, *refs):
    o_ref = refs[-1]
    pairs, wide, _ = packing(rank)
    o_ref[...] = jnp.zeros((rank, rank), F32)
    for at, (i, j) in enumerate(pairs):
        g, k = at // wide, at % wide
        o_ref[i * BAND:(i + 1) * BAND, j * BAND:(j + 1) * BAND] = g_ref[
            g * BAND:(g + 1) * BAND, k * BAND:(k + 1) * BAND]
    for b in range(rank // BAND):
        lo, hi = b * BAND, (b + 1) * BAND
        r = band_rows(o_ref[lo:hi, :], b)
        rows, cols = iota(r.shape, 0), iota(r.shape, 1)
        r = jnp.where((cols >= lo) & (cols < hi) & (cols - lo > rows), 0.0, r)
        o_ref[lo:hi, :] = jnp.where(cols < hi, r, 0.0)
        if hi < rank:
            left = jnp.where(cols >= hi, r, 0.0)
            update = dot(left, r, ((0,), (0,)), HI)
            kept = jnp.where(iota((rank - hi, rank), 1) // BAND == b, 0.0, o_ref[hi:, :])
            o_ref[hi:, :] = kept - update[hi:, :]


def factor_inverse(packed, rank, after=()):
    return pl.pallas_call(
        functools.partial(factor_kernel, rank),
        in_specs=[HELD] + [UNREAD] * len(after),
        out_shape=jax.ShapeDtypeStruct((rank, rank), F32),
        compiler_params=params(),
        cost_estimate=cost(8e9, 4 * rank * rank),
        name="factor",
    )(packed, *after)


def project_kernel(count, wide, has_base, unread, finish, ids_ref, *refs):
    s_refs, x_refs = refs[:count], refs[count:count * (1 + wide)]
    at = count * (1 + wide)
    rest = refs[at + has_base + unread:]
    t_ref = rest[-1]
    rank = t_ref.shape[1]

    @pl.when(pl.program_id(0) == 0)
    def _():
        t_ref[...] = refs[at][...] if has_base else jnp.zeros_like(t_ref)

    for w in range(wide):
        total = None
        for k in range(count):
            term = dot(s_refs[k][...], x_refs[w * count + k][...], ((1,), (0,)))
            total = term if total is None else total + term
        t_ref[w] += total if total.shape[0] == rank else total[:rank] + total[rank:]
    if finish is not None:
        @pl.when(pl.program_id(0) == pl.num_programs(0) - 1)
        def _():
            finish(t_ref, ids_ref[count], *rest[:-1])


def project(ids, parts, x, extra, rank, base, rows, after=(), finish=None, outs=(), scratch=()):
    count = len(parts)
    wide = 1 + len(extra)
    height, span = parts[0].shape
    depth = x.shape[1]
    steps = span // rows
    bases = [] if base is None else [base]
    whole = pl.BlockSpec((wide, rank, depth), lambda i, ids: (0, 0, 0))
    t_shape = jax.ShapeDtypeStruct((wide, rank, depth), F32)
    if finish is None:
        out_specs, out_shape, scratch_shapes = whole, t_shape, []
    else:
        out_specs = [pl.BlockSpec(o.shape, lambda i, ids: (0, 0, 0)) for o in outs]
        out_shape = list(outs)
        scratch_shapes = list(scratch) + [pltpu.VMEM((wide, rank, depth), F32)]
    return pl.pallas_call(
        functools.partial(project_kernel, count, wide, len(bases), len(after), finish),
        grid_spec=pltpu.PrefetchScalarGridSpec(
            num_scalar_prefetch=1,
            grid=(steps,),
            in_specs=[pl.BlockSpec((height, rows), lambda i, ids: (0, i))] * count
            + [
                pl.BlockSpec((rows, depth), lambda i, ids, k=k: (ids[k] * steps + i, 0))
                for k in range(count)
            ]
            + [pl.BlockSpec((rows, depth), lambda i, ids: (i, 0))] * (count * (wide - 1))
            + [whole] * len(bases) + [UNREAD] * len(after),
            out_specs=out_specs,
            scratch_shapes=scratch_shapes,
        ),
        out_shape=out_shape,
        compiler_params=params(),
        cost_estimate=cost(
            2 * height * depth * span * count * wide, span * count * (depth * wide + height) * 2),
        name="project",
    )(ids, *parts, *([x] * count), *[v for values in extra for v in values], *bases, *after)


def folding(rank, width):
    best = 1
    for f in range(1, rank + 1):
        if rank % f == 0 and (rank // f) % 8 == 0 and f * width <= 128:
            best = f
    return best


def reverse_bits(p, count):
    return sum(1 << (count - 1 - b) for b in range(count) if (p >> b) & 1)


def regroup_tail(pieces, samp, per_node, width_cols, t_ref, me, *refs):
    outs, hold = refs[:-1], refs[-1]
    wide, rank, depth = t_ref.shape
    width = per_node * width_cols
    fold = folding(rank, width)
    tall = rank // fold
    dst = iota((depth, depth), 1)
    src = iota((depth, depth), 0)
    a, rest = dst // (samp * width), dst % (samp * width)
    s, rest = rest // width, rest % width
    want = (a * per_node + rest // width_cols) * (samp * width_cols) + s * width_cols + rest % width_cols
    move = jnp.where(src == want, 1.0, 0.0).astype(BF16)
    bits = pieces.bit_length() - 1
    for w in range(wide):
        t = t_ref[w]
        high = t.astype(BF16)
        mid = (t - high.astype(F32)).astype(BF16)
        low = (t - high.astype(F32) - mid.astype(F32)).astype(BF16)
        moved = dot(jnp.concatenate([high, mid, low], axis=0), move, ((1,), (0,)))
        moved = moved[:rank] + moved[rank:2 * rank] + moved[2 * rank:]
        for i in range(pieces):
            piece = moved[:, i * width:(i + 1) * width]
            hold[i] = jnp.concatenate([piece[f * tall:(f + 1) * tall] for f in range(fold)], axis=1)
        for p in range(pieces):
            outs[w][p] = hold[me ^ reverse_bits(p, bits)]


def core_kernel(count, inv_ref, *refs):
    both, high, low = (refs[k * count:(k + 1) * count] for k in range(3))
    o_ref = refs[-1]
    rank = inv_ref.shape[0]
    for c in range(count):
        s = both[c][:rank, :].astype(F32) + both[c][rank:, :].astype(F32)
        s = s + (high[c][...].astype(F32) + low[c][...].astype(F32))
        rows = s.shape[1]
        o_ref[:, c * rows:(c + 1) * rows] = dot(inv_ref[...], s, ((1,), (0,)), HI)


def core_product(inverse, both, high, low):
    rank, rows = high[0].shape
    count = len(both)
    return pl.pallas_call(
        functools.partial(core_kernel, count),
        out_shape=jax.ShapeDtypeStruct((rank, rows * count), F32),
        compiler_params=params(),
        cost_estimate=cost(12 * rank * rank * rows * count, 12 * rank * rows * count),
        name="core",
    )(inverse, *both, *high, *low)


def coefficient_kernel(scale, per_node, width_cols, inv_ref, *refs):
    pieces, o_ref = refs[:-1], refs[-1]
    rank = inv_ref.shape[0]
    total = pieces[0][...]
    for p in pieces[1:]:
        total = total + p[...]
    width = per_node * width_cols
    fold = total.shape[1] // width
    total = jnp.concatenate([total[:, f * width:(f + 1) * width] for f in range(fold)], axis=0)
    out = dot(total, inv_ref[...], ((0,), (1,)), HI) * scale
    o_ref[...] = jnp.concatenate(
        [out[p * width_cols:(p + 1) * width_cols, :] for p in range(per_node)], axis=1)


def coefficients(inverse, pieces, scale, per_node, width_cols):
    rank = inverse.shape[0]
    return pl.pallas_call(
        functools.partial(coefficient_kernel, scale, per_node, width_cols),
        out_shape=jax.ShapeDtypeStruct((width_cols, per_node * rank), F32),
        compiler_params=params(),
        cost_estimate=cost(12 * rank * rank * per_node * width_cols, 4 * rank * rank),
        name="coefficient",
    )(inverse, *pieces)


def swap(value, axis, size, bit):
    return lax.ppermute(value, axis, [(i, i ^ bit) for i in range(size)])


def body(snapshots, sketch_matrix):
    rows_all = snapshots.shape[0]
    rank = sketch_matrix.shape[1]
    samp = lax.axis_size("samp")
    node = lax.axis_size("node")
    total = rows_all * node
    quarter = rows_all // samp
    chunks = CHUNKS
    span = quarter // chunks
    every = range(chunks)
    me_s = lax.axis_index("samp").astype(jnp.int32)
    me_n = lax.axis_index("node").astype(jnp.int32)
    w_t = sketch_matrix.T
    last = samp // 2

    def quarter_of(d, c):
        return (me_s ^ d) * chunks + c

    def take(d, c):
        return lax.dynamic_slice_in_dim(snapshots, quarter_of(d, c) * span, span, 0)

    near = range(1, last)
    ws = [w_t] + [swap(w_t, "samp", samp, d) for d in near]
    blocks = [(base, c) for base in (last, 0) for c in every]
    borrowed = {
        (base, c): [swap(take(base ^ d, c), "samp", samp, d) for d in near] for base, c in blocks
    }
    pairs, arrived, done = {}, {}, ()
    for base, c in blocks:
        both, high = sketch(quarter_of(base, c)[None], snapshots, ws, borrowed[base, c], span, done)
        done = (high,)
        pairs[base, c] = both
        arrived[base ^ last, c] = swap(high, "samp", samp, last)
    gram = local_gram([pairs[b] for b in blocks])
    ids = jnp.stack([quarter_of(*b) for b in blocks] + [me_n])
    extra = [[borrowed[b][d - 1] for b in blocks] for d in near]
    rows = min(span, 512)
    t = project(ids, [pairs[b] for b in blocks], snapshots, extra, rank, None, rows)

    own, far = ([pairs[b, c] for c in every] for b in (0, last))
    got_high, near_high = ([arrived[b, c] for c in every] for b in (0, last))
    packed = cross_gram(own, got_high, far, near_high, gram, 1.0 / total, after=(t,))
    upper = (me_s & 1) == 1
    halves = jnp.split(packed, 2, axis=0)
    mine = jnp.where(upper, halves[1], halves[0])
    mine = mine + swap(jnp.where(upper, halves[0], halves[1]), "samp", samp, 1)
    bit = 2
    while bit < samp:
        mine = mine + swap(mine, "samp", samp, bit)
        bit *= 2
    begun = mine
    bit = 1
    while bit < node:
        mine = mine + swap(mine, "node", node, bit)
        bit *= 2
    other = swap(mine, "samp", samp, 1)
    packed = jnp.concatenate([jnp.where(upper, other, mine), jnp.where(upper, mine, other)], axis=0)

    got_low = []
    for c in every:
        low, _ = lax.optimization_barrier((far[c][rank:], begun))
        got_low.append(swap(low, "samp", samp, last))

    per_node = P1 // node
    width_cols = P2 // samp
    width = per_node * width_cols
    fold = folding(rank, width)
    piece = (rank // fold, fold * width)
    stacks = project(
        ids, [arrived[b] for b in blocks], snapshots, extra, rank, t, rows, (),
        functools.partial(regroup_tail, node, samp, per_node, width_cols),
        [jax.ShapeDtypeStruct((node,) + piece, F32)] * last,
        [pltpu.VMEM((node,) + piece, F32)])
    inverse = factor_inverse(packed, rank, after=(stacks[0],))

    held = stacks[0]
    for d in near:
        held = held + swap(stacks[d], "samp", samp, d)
    bit = 1
    while True:
        half = held.shape[0] // 2
        if half == 1:
            break
        held = held[:half] + swap(held[half:], "node", node, bit)
        bit *= 2
    spread = node // samp
    landed = []
    for k, value in ((0, held[0]), (bit, held[1])):
        route = []
        for n in range(node):
            a, s_to = (n ^ k) // samp, (n ^ k) % samp
            for s_from in range(samp):
                route.append((n * samp + s_from, (s_from * spread + a) * samp + s_to))
        landed.append(lax.ppermute(value, ("node", "samp"), route))
    core = core_product(inverse, own, got_high, got_low)
    coef = coefficients(inverse, landed, 1.0 / total, per_node, width_cols)
    return (core.T, coef.T)


def solution(mesh):
    placed = (P("node", "samp"), P("samp", None))
    return jax.shard_map(
        body,
        mesh=mesh,
        in_specs=placed,
        out_specs=(P(("node", "samp"), None), P("node", "samp")),
        check_vma=False,
    )
```

```python
import functools
import jax
import jax.numpy as jnp
from jax import lax
from jax.experimental import pallas as pl
from jax.experimental.pallas import tpu as pltpu
from jax.sharding import PartitionSpec as P

P1 = 64
P2 = 32
BAND = 32
UNIT = 1024
SKETCH_ROWS = 1024
COST_CUT = 1
F32 = jnp.float32
BF16 = jnp.bfloat16
HI = lax.Precision.HIGHEST
UNREAD = pl.BlockSpec(memory_space=pl.ANY)
HELD = pl.BlockSpec(memory_space=pltpu.VMEM)
VMEM_LIMIT = 48 * 1024 * 1024


def iota(shape, dim):
    return lax.broadcasted_iota(jnp.int32, shape, dim)


def dot(a, b, dims, precision=None):
    return lax.dot_general(a, b, (dims, ((), ())), precision=precision, preferred_element_type=F32)


def params():
    return pltpu.CompilerParams(vmem_limit_bytes=VMEM_LIMIT)


def cost(flops, moved):
    return pl.CostEstimate(flops=int(flops) // COST_CUT, bytes_accessed=int(moved) // COST_CUT, transcendentals=0)


def sketch_kernel(count, ids_ref, x_ref, *refs):
    w_refs, x_refs = refs[:count], (x_ref,) + refs[count:2 * count - 1]
    both_ref, high_ref = refs[-2:]
    rank = high_ref.shape[0]
    s = None
    for w_ref, ref in zip(w_refs, x_refs):
        term = dot(w_ref[...], ref[...], ((1,), (1,)))
        s = term if s is None else s + term
    high = s.astype(BF16)
    high_ref[...] = high
    both_ref[:rank, :] = high
    both_ref[rank:, :] = (s - high.astype(F32)).astype(BF16)


def sketch(ids, x, ws, extra, size, after=()):
    rank, depth = ws[0].shape
    count = len(ws)
    rows = min(size, SKETCH_ROWS)
    return pl.pallas_call(
        functools.partial(sketch_kernel, count),
        grid_spec=pltpu.PrefetchScalarGridSpec(
            num_scalar_prefetch=1,
            grid=(size // rows,),
            in_specs=[pl.BlockSpec((rows, depth), lambda i, ids: (ids[0] + i, 0))]
            + [pl.BlockSpec((rank, depth), lambda i, ids: (0, 0))] * count
            + [pl.BlockSpec((rows, depth), lambda i, ids: (i, 0))] * (count - 1)
            + [UNREAD] * len(after),
            out_specs=[
                pl.BlockSpec((2 * rank, rows), lambda i, ids: (0, i)),
                pl.BlockSpec((rank, rows), lambda i, ids: (0, i)),
            ],
        ),
        out_shape=(
            jax.ShapeDtypeStruct((2 * rank, size), BF16),
            jax.ShapeDtypeStruct((rank, size), BF16),
        ),
        compiler_params=params(),
        cost_estimate=cost(2 * rank * depth * size * count, size * (depth * 2 * count + rank * 6)),
        name="sketch",
    )(ids, x, *ws, *extra, *after)


def packing(rank):
    bands = rank // BAND
    pairs = [(i, j) for i in range(bands) for j in range(i, bands)]
    wide = 128 // BAND
    groups = -(-len(pairs) // wide)
    groups += groups % 2
    return pairs, wide, groups


def pack_gram(gram):
    pairs, wide, groups = packing(gram.shape[0])
    out = []
    for g in range(groups):
        chosen = pairs[g * wide:(g + 1) * wide]
        parts = [gram[i * BAND:(i + 1) * BAND, j * BAND:(j + 1) * BAND] for i, j in chosen]
        parts += [jnp.zeros((BAND, BAND), F32)] * (wide - len(chosen))
        out.append(jnp.concatenate(parts, axis=1))
    return jnp.concatenate(out, axis=0)


def fold_square(x, rank):
    return (x[:rank, :rank] + x[rank:, rank:]) + (x[:rank, rank:] + x[rank:, :rank])


def gram_kernel(*refs):
    o_ref = refs[-1]
    rank = o_ref.shape[0]
    total = None
    for ref in refs[:-1]:
        both = ref[...]
        term = dot(both, both, ((1,), (1,)))
        total = term if total is None else total + term
    o_ref[...] = fold_square(total, rank)


def local_gram(pairs):
    rank = pairs[0].shape[0] // 2
    rows = sum(v.shape[1] for v in pairs)
    return pl.pallas_call(
        gram_kernel,
        out_shape=jax.ShapeDtypeStruct((rank, rank), F32),
        compiler_params=params(),
        cost_estimate=cost(8 * rank * rank * rows, 4 * rank * rows),
        name="gram",
    )(*pairs)


def cross_terms(own, got, far, near):
    rank = (got + near)[0].shape[0]
    total = None
    for own_ref, got_ref in zip(own, got):
        term = dot(own_ref[...], got_ref[...], ((1,), (1,)))
        term = term[:rank] + term[rank:]
        total = term if total is None else total + term
    for far_ref, near_ref in zip(far, near):
        term = dot(near_ref[...], far_ref[rank:, :], ((1,), (1,)))
        total = term if total is None else total + term
    return total + total.T


def cross_kernel(counts, *refs):
    a, b = counts
    groups = refs[:a], refs[a:2 * a], refs[2 * a:2 * a + b], refs[2 * a + b:2 * a + 2 * b]
    refs[-1][...] = refs[2 * a + 2 * b][...] + cross_terms(*groups)


def cross_gram(own, got, far, near, gram, after=()):
    rank = gram.shape[0]
    rows = sum(v.shape[1] for v in got + near)
    counts = (len(own), len(far))
    return pl.pallas_call(
        functools.partial(cross_kernel, counts),
        in_specs=[HELD] * (2 * sum(counts) + 1) + [UNREAD] * len(after),
        out_shape=jax.ShapeDtypeStruct((rank, rank), F32),
        compiler_params=params(),
        cost_estimate=cost(4 * rank * rank * rows, 6 * rank * rows),
        name="cross",
    )(*own, *got, *far, *near, gram, *after)


def wide_lanes(x, n):
    reps = -(-n // 128)
    return jnp.concatenate([x] * reps, axis=1)[:, :n] if reps > 1 else x[:, :n]


def band_rows(block, b):
    n = block.shape[1]
    count = BAND // 8
    part = [block[8 * i:8 * i + 8, :] for i in range(count)]
    sub = iota((8, n), 0)
    lane = iota((8, n), 1)
    for m in range(count):
        c0 = b * BAND + 8 * m
        live = count - m
        col = [
            [jnp.broadcast_to(part[m + i][:, c0 + k:c0 + k + 1], (8, 128)) for i in range(live)]
            for k in range(8)
        ]
        here = (lane >= c0) & (lane < c0 + 8)
        part[m] = jnp.where(here, jnp.where(lane - c0 == sub, 1.0, 0.0), part[m])
        for i in range(1, live):
            part[m + i] = jnp.where(here, 0.0, part[m + i])
        for j in range(8):
            inv_root = lax.rsqrt(jnp.broadcast_to(col[j][0][j:j + 1, :], (8, 128)))
            low = [x * inv_root for x in col[j]]
            for k in range(j + 1, 8):
                t = jnp.broadcast_to(low[0][k:k + 1, :], (8, 128))
                for i in range(live):
                    col[k][i] = col[k][i] - low[i] * t
            row = jnp.broadcast_to(part[m][j:j + 1, :], (8, n)) * wide_lanes(inv_root, n)
            for i in range(live):
                new = part[m + i] - wide_lanes(low[i], n) * row
                if i == 0:
                    new = jnp.where(sub > j, new, jnp.where(sub == j, row, part[m]))
                part[m + i] = new
    return jnp.concatenate(part, axis=0)


def factor_kernel(rank, me_ref, mine_ref, other_ref, *refs):
    o_ref, g_ref = refs[-2:]
    pairs, wide, groups = packing(rank)
    half = groups * BAND // 2
    mine_at = pl.multiple_of((me_ref[0] & 1) * half, half)
    g_ref[pl.ds(mine_at, half), :] = mine_ref[...]
    g_ref[pl.ds(pl.multiple_of(half - mine_at, half), half), :] = other_ref[...]
    o_ref[...] = jnp.zeros((rank, rank), F32)
    for at, (i, j) in enumerate(pairs):
        g, k = at // wide, at % wide
        o_ref[i * BAND:(i + 1) * BAND, j * BAND:(j + 1) * BAND] = g_ref[
            g * BAND:(g + 1) * BAND, k * BAND:(k + 1) * BAND]
    for b in range(rank // BAND):
        lo, hi = b * BAND, (b + 1) * BAND
        r = band_rows(o_ref[lo:hi, :], b)
        rows, cols = iota(r.shape, 0), iota(r.shape, 1)
        r = jnp.where((cols >= lo) & (cols < hi) & (cols - lo > rows), 0.0, r)
        o_ref[lo:hi, :] = jnp.where(cols < hi, r, 0.0)
        if hi < rank:
            left = jnp.where(cols >= hi, r, 0.0)
            update = dot(left, r, ((0,), (0,)), HI)
            kept = jnp.where(iota((rank - hi, rank), 1) // BAND == b, 0.0, o_ref[hi:, :])
            o_ref[hi:, :] = kept - update[hi:, :]


def factor_inverse(me, mine, other, rank, after=()):
    return pl.pallas_call(
        functools.partial(factor_kernel, rank),
        in_specs=[pl.BlockSpec(memory_space=pltpu.SMEM)] + [HELD] * 2 + [UNREAD] * len(after),
        out_shape=jax.ShapeDtypeStruct((rank, rank), F32),
        scratch_shapes=[pltpu.VMEM((2 * mine.shape[0], 128), F32)],
        compiler_params=params(),
        cost_estimate=cost(8e9, 4 * rank * rank),
        name="factor",
    )(me, mine, other, *after)


def project_kernel(count, wide, has_base, aside, finish, ids_ref, *refs):
    s_refs, x_refs = refs[:count], refs[count:count * (1 + wide)]
    at = count * (1 + wide)
    beside = refs[at + has_base:at + has_base + aside]
    rest = refs[at + has_base + aside:]
    t_ref = rest[-1]
    rank = t_ref.shape[1]

    @pl.when(pl.program_id(0) == 0)
    def _():
        t_ref[...] = refs[at][...] if has_base else jnp.zeros_like(t_ref)

    for w in range(wide):
        total = None
        for k in range(count):
            term = dot(s_refs[k][...], x_refs[w * count + k][...], ((1,), (0,)))
            total = term if total is None else total + term
        t_ref[w] += total if total.shape[0] == rank else total[:rank] + total[rank:]
    if finish is not None:
        @pl.when(pl.program_id(0) == pl.num_programs(0) - 1)
        def _():
            finish(t_ref, ids_ref, beside, *rest[:-1])


def project(ids, work, x, rank, base, rows, beside=(), finish=None, outs=(), scratch=(), after=()):
    wide = 1 + len(work[0][2])
    height = work[0][0].shape[0]
    depth = x.shape[1]
    unit = UNIT
    steps = unit // rows
    parts, s_specs, own_specs, more, more_specs = [], [], [], [[] for _ in range(wide - 1)], []
    for array, slot, lent in work:
        for u in range(array.shape[1] // unit):
            parts.append(array)
            s_specs.append(pl.BlockSpec((height, rows), lambda i, ids, u=u: (0, u * steps + i)))
            own_specs.append(pl.BlockSpec(
                (rows, depth), lambda i, ids, u=u, slot=slot: ((ids[slot] + u) * steps + i, 0)))
            more_specs.append(pl.BlockSpec((rows, depth), lambda i, ids, u=u: (u * steps + i, 0)))
            for w in range(wide - 1):
                more[w].append(lent[w])
    count = len(parts)
    bases = [] if base is None else [base]
    whole = pl.BlockSpec((wide, rank, depth), lambda i, ids: (0, 0, 0))
    t_shape = jax.ShapeDtypeStruct((wide, rank, depth), F32)
    if finish is None:
        out_specs, out_shape, scratch_shapes = whole, t_shape, []
    else:
        out_specs = [pl.BlockSpec(o.shape, lambda i, ids: (0, 0)) for o in outs]
        out_shape = list(outs)
        scratch_shapes = list(scratch) + [pltpu.VMEM((wide, rank, depth), F32)]
    return pl.pallas_call(
        functools.partial(
            project_kernel, count, wide, len(bases), len(beside) + len(after), finish),
        grid_spec=pltpu.PrefetchScalarGridSpec(
            num_scalar_prefetch=1,
            grid=(steps,),
            in_specs=s_specs + own_specs + more_specs * (wide - 1) + [whole] * len(bases)
            + [pl.BlockSpec(v.shape, lambda i, ids: (0, 0)) for v in beside] + [UNREAD] * len(after),
            out_specs=out_specs,
            scratch_shapes=scratch_shapes,
        ),
        out_shape=out_shape,
        compiler_params=params(),
        cost_estimate=cost(
            2 * height * depth * unit * count * wide, unit * count * (depth * wide + height) * 2),
        name="project",
    )(ids, *parts, *([x] * count), *[v for values in more for v in values], *bases, *beside, *after)


def folding(rank, width):
    best = 1
    for f in range(1, rank + 1):
        if rank % f == 0 and (rank // f) % 8 == 0 and f * width <= 128:
            best = f
    return best


def reverse_bits(p, count):
    return sum(1 << (count - 1 - b) for b in range(count) if (p >> b) & 1)


def tail(pieces, samp, per_node, width_cols, scale, counts, t_ref, ids_ref, beside, *refs):
    outs, hold, packed_ref = refs[:-2], refs[-2], refs[-1]
    wide, rank, depth = t_ref.shape
    width = per_node * width_cols
    fold = folding(rank, width)
    tall = rank // fold
    me_node, me_samp = ids_ref[ids_ref.shape[0] - 2], ids_ref[ids_ref.shape[0] - 1]
    a, b = counts
    groups = beside[:a], beside[a:2 * a], beside[2 * a:2 * a + b], beside[2 * a + b:2 * a + 2 * b]
    packed_ref[...] = pack_gram((beside[2 * a + 2 * b][...] + cross_terms(*groups)) * scale)
    half = packed_ref.shape[0] // 2
    mine_at = pl.multiple_of((me_samp & 1) * half, half)
    outs[0][pieces * tall:, :] = packed_ref[pl.ds(mine_at, half), :]
    outs[1][pieces * tall:, :] = packed_ref[pl.ds(pl.multiple_of(half - mine_at, half), half), :]
    for out in outs[2:]:
        out[pieces * tall:, :] = jnp.zeros((half, 128), F32)
    dst = iota((depth, depth), 1)
    src = iota((depth, depth), 0)
    a, rest = dst // (samp * width), dst % (samp * width)
    s, rest = rest // width, rest % width
    want = (a * per_node + rest // width_cols) * (samp * width_cols) + s * width_cols + rest % width_cols
    move = jnp.where(src == want, 1.0, 0.0).astype(BF16)
    bits = pieces.bit_length() - 1
    for w in range(wide):
        t = t_ref[w]
        high = t.astype(BF16)
        mid = (t - high.astype(F32)).astype(BF16)
        low = (t - high.astype(F32) - mid.astype(F32)).astype(BF16)
        moved = dot(jnp.concatenate([high, mid, low], axis=0), move, ((1,), (0,)))
        moved = moved[:rank] + moved[rank:2 * rank] + moved[2 * rank:]
        for i in range(pieces):
            piece = moved[:, i * width:(i + 1) * width]
            parts = [piece[f * tall:(f + 1) * tall] for f in range(fold)]
            if fold * width < 128:
                parts.append(jnp.zeros((tall, 128 - fold * width), F32))
            hold[i] = jnp.concatenate(parts, axis=1)
        for p in range(pieces):
            outs[w][p * tall:(p + 1) * tall, :] = hold[me_node ^ reverse_bits(p, bits)]


def finish_kernel(scale, per_node, width_cols, count, inv_ref, piece_ref, *refs):
    both, high, low = (refs[k * count:(k + 1) * count] for k in range(3))
    core_ref, coef_ref = refs[-2:]
    rank = inv_ref.shape[0]
    inverse = inv_ref[...]
    at = 0
    for c in range(count):
        s = both[c][:rank, :].astype(F32) + both[c][rank:, :].astype(F32)
        s = s + (high[c][...].astype(F32) + low[c][...].astype(F32))
        rows = s.shape[1]
        core_ref[:, at:at + rows] = dot(inverse, s, ((1,), (0,)), HI)
        at += rows
    width = per_node * width_cols
    fold = folding(rank, width)
    total = piece_ref[...]
    total = jnp.concatenate([total[:, f * width:(f + 1) * width] for f in range(fold)], axis=0)
    out = dot(total, inverse, ((0,), (1,)), HI) * scale
    coef_ref[...] = jnp.concatenate(
        [out[p * width_cols:(p + 1) * width_cols, :] for p in range(per_node)], axis=1)


def finish(inverse, piece, both, high, low, scale, per_node, width_cols):
    rank = inverse.shape[0]
    count = len(both)
    rows = sum(v.shape[1] for v in high)
    return pl.pallas_call(
        functools.partial(finish_kernel, scale, per_node, width_cols, count),
        out_shape=(
            jax.ShapeDtypeStruct((rank, rows), F32),
            jax.ShapeDtypeStruct((width_cols, per_node * rank), F32),
        ),
        compiler_params=params(),
        cost_estimate=cost(12 * rank * rank * rows, 12 * rank * rows),
        name="finish",
    )(inverse, piece, *both, *high, *low)


def swap(value, axis, size, bit):
    return lax.ppermute(value, axis, [(i, i ^ bit) for i in range(size)])


def body(snapshots, sketch_matrix):
    rows_all = snapshots.shape[0]
    rank = sketch_matrix.shape[1]
    samp = lax.axis_size("samp")
    node = lax.axis_size("node")
    total = rows_all * node
    quarter = rows_all // samp
    me_s = lax.axis_index("samp").astype(jnp.int32)
    me_n = lax.axis_index("node").astype(jnp.int32)
    w_t = sketch_matrix.T
    last = samp // 2
    near = range(1, last)
    starts, sizes = (0, UNIT), (UNIT, quarter - UNIT)
    blocks = [(last, 0), (last, 1), (0, 0), (0, 1)]

    ws = [w_t] + [swap(w_t, "samp", samp, d) for d in near]
    borrowed, made = {}, None
    for base, c in blocks:
        lent = []
        for d in near:
            at = (me_s ^ base ^ d) * quarter + starts[c]
            if made is not None:
                at, _ = lax.optimization_barrier((at, made))
            made = lax.dynamic_slice_in_dim(snapshots, at, sizes[c], 0)
            lent.append(swap(made, "samp", samp, d))
        borrowed[base, c] = lent

    def first_unit(base, c):
        return (me_s ^ base) * (quarter // UNIT) + starts[c] // UNIT

    pairs, arrived, done = {}, {}, ()
    for base, c in blocks:
        both, high = sketch(
            first_unit(base, c)[None], snapshots, ws, borrowed[base, c], sizes[c], done)
        done = (high,)
        pairs[base, c] = both
        arrived[base ^ last, c] = swap(high, "samp", samp, last)
    gram = local_gram([pairs[b] for b in blocks])
    ids = jnp.stack([first_unit(*b) for b in blocks] + [me_n, me_s])
    slot = {b: k for k, b in enumerate(blocks)}
    rows = min(UNIT, 512)
    t = project(ids, [(pairs[b], slot[b], borrowed[b]) for b in blocks], snapshots, rank, None, rows)

    order = [(base ^ last, c) for base, c in blocks]
    early, late = order[:-1], order[-1:]

    def groups(chosen):
        own = [b for b in chosen if b[0] == 0]
        far = [b for b in chosen if b[0] == last]
        return [pairs[b] for b in own], [arrived[b] for b in own], [pairs[b] for b in far], [arrived[b] for b in far]

    gram = cross_gram(*groups(early), gram, after=(t,))
    t = project(
        ids, [(arrived[b], slot[b], borrowed[b]) for b in early], snapshots, rank, t, rows, after=(gram,))
    per_node = P1 // node
    width_cols = P2 // samp
    tall = rank // folding(rank, per_node * width_cols)
    packed_rows = packing(rank)[2] * BAND
    ends = groups(late)
    beside = [v for group in ends for v in group] + [gram]
    message = jax.ShapeDtypeStruct((node * tall + packed_rows // 2, 128), F32)
    messages = project(
        ids, [(arrived[b], slot[b], borrowed[b]) for b in late], snapshots, rank, t, rows, beside,
        functools.partial(
            tail, node, samp, per_node, width_cols, 1.0 / total, (len(ends[0]), len(ends[2]))),
        [message] * last,
        [pltpu.VMEM((node, tall, 128), F32), pltpu.VMEM((packed_rows, 128), F32)])

    held = messages[0]
    for d in near:
        held = held + swap(messages[d], "samp", samp, d)
    edge = node * tall
    pieces, half = held[:edge], held[edge:]
    bit = 2
    while bit < samp:
        half = half + swap(half, "samp", samp, bit)
        bit *= 2
    crossed = half
    bit = 1
    while bit < node:
        edge //= 2
        got = swap(jnp.concatenate([pieces[edge:], half], axis=0), "node", node, bit)
        pieces, half = pieces[:edge] + got[:edge], half + got[edge:]
        bit *= 2
    other = swap(half, "samp", samp, 1)
    spread = node // samp
    route = [
        (n * samp + s, (s * spread + n // samp) * samp + n % samp) for n in range(node) for s in range(samp)
    ]
    piece = lax.ppermute(pieces, ("node", "samp"), route)

    got_low = []
    for c in range(2):
        low, _ = lax.optimization_barrier((pairs[last, c][rank:], crossed))
        got_low.append(swap(low, "samp", samp, last))

    inverse = factor_inverse(me_s[None], half, other, rank)
    core, coef = finish(
        inverse, piece, [pairs[0, c] for c in range(2)], [arrived[0, c] for c in range(2)], got_low,
        1.0 / total, per_node, width_cols)
    return (core.T, coef.T)


def solution(mesh):
    placed = (P("node", "samp"), P("samp", None))
    return jax.shard_map(
        body,
        mesh=mesh,
        in_specs=placed,
        out_specs=(P(("node", "samp"), None), P("node", "samp")),
        check_vma=False,
    )
```

```python
import functools
import jax
import jax.numpy as jnp
from jax import lax
from jax.experimental import pallas as pl
from jax.experimental.pallas import tpu as pltpu
from jax.sharding import PartitionSpec as P

P1 = 64
P2 = 32
BAND = 32
UNIT = 1024
SKETCH_ROWS = 1024
EARLY_STAGE, LATE_STAGE = 1, 4
COST_CUT = 1
F32 = jnp.float32
BF16 = jnp.bfloat16
HI = lax.Precision.HIGHEST
UNREAD = pl.BlockSpec(memory_space=pl.ANY)
HELD = pl.BlockSpec(memory_space=pltpu.VMEM)
VMEM_LIMIT = 48 * 1024 * 1024


def iota(shape, dim):
    return lax.broadcasted_iota(jnp.int32, shape, dim)


def dot(a, b, dims, precision=None):
    return lax.dot_general(a, b, (dims, ((), ())), precision=precision, preferred_element_type=F32)


def params():
    return pltpu.CompilerParams(vmem_limit_bytes=VMEM_LIMIT)


def cost(flops, moved):
    return pl.CostEstimate(flops=int(flops) // COST_CUT, bytes_accessed=int(moved) // COST_CUT, transcendentals=0)


def lend_kernel(size, stride, at, ids_ref, x_ref, *refs):
    count = ids_ref.shape[0]
    extra = 1 if at is not None else 0
    outs, sems = refs[-1 - count:-1], refs[-1]
    copies = []
    for k in range(count):
        first = pl.multiple_of(ids_ref[k] * size, size)
        for part in range(size // stride):
            copies.append(pltpu.make_async_copy(
                x_ref.at[pl.ds(first + part * stride, stride)],
                outs[k].at[pl.ds(part * stride, stride)],
                sems.at[len(copies)]))
    if extra:
        copies.append(pltpu.make_async_copy(
            refs[0], outs[0].at[pl.ds(at, refs[0].shape[0])], sems.at[len(copies)]))
    for copy in copies:
        copy.start()
    for copy in copies:
        copy.wait()


def lend(ids, x, size, w=None, after=()):
    count = ids.shape[0]
    depth = x.shape[1]
    stride = size // 2
    at, height = None, size
    if w is not None:
        rank = w.shape[0]
        at = -(-size // rank) * rank
        height = at + rank
    more = [] if w is None else [w]
    return pl.pallas_call(
        functools.partial(lend_kernel, size, stride, at),
        in_specs=[pl.BlockSpec(memory_space=pltpu.SMEM)] + [UNREAD] * (1 + len(more) + len(after)),
        out_specs=[pl.BlockSpec(memory_space=pl.ANY)] * count,
        out_shape=[jax.ShapeDtypeStruct((height, depth), BF16)] * count,
        scratch_shapes=[pltpu.SemaphoreType.DMA((2 * count + len(more),))],
        compiler_params=params(),
        cost_estimate=cost(0, 4 * count * height * depth),
        name="lend",
    )(ids, x, *more, *after)


def sketch_kernel(count, ids_ref, x_ref, *refs):
    w_refs, x_refs = refs[:count], (x_ref,) + refs[count:2 * count - 1]
    both_ref, high_ref = refs[-2:]
    rank = high_ref.shape[0]
    s = None
    for w_ref, ref in zip(w_refs, x_refs):
        term = dot(w_ref[...], ref[...], ((1,), (1,)))
        s = term if s is None else s + term
    high = s.astype(BF16)
    high_ref[...] = high
    both_ref[:rank, :] = high
    both_ref[rank:, :] = (s - high.astype(F32)).astype(BF16)


def sketch(ids, x, ws, extra, size, w_at, after=()):
    rank, depth = ws[0].shape
    count = len(ws)
    rows = min(size, SKETCH_ROWS)
    return pl.pallas_call(
        functools.partial(sketch_kernel, count),
        grid_spec=pltpu.PrefetchScalarGridSpec(
            num_scalar_prefetch=1,
            grid=(size // rows,),
            in_specs=[pl.BlockSpec((rows, depth), lambda i, ids: (ids[0] + i, 0))]
            + [pl.BlockSpec((rank, depth), lambda i, ids: (0, 0))]
            + [pl.BlockSpec((rank, depth), lambda i, ids: (w_at // rank, 0))] * (count - 1)
            + [pl.BlockSpec((rows, depth), lambda i, ids: (i, 0))] * (count - 1)
            + [UNREAD] * len(after),
            out_specs=[
                pl.BlockSpec((2 * rank, rows), lambda i, ids: (0, i)),
                pl.BlockSpec((rank, rows), lambda i, ids: (0, i)),
            ],
        ),
        out_shape=(
            jax.ShapeDtypeStruct((2 * rank, size), BF16),
            jax.ShapeDtypeStruct((rank, size), BF16),
        ),
        compiler_params=params(),
        cost_estimate=cost(2 * rank * depth * size * count, size * (depth * 2 * count + rank * 6)),
        name="sketch",
    )(ids, x, *ws, *extra, *after)


def packing(rank):
    bands = rank // BAND
    pairs = [(i, j) for i in range(bands) for j in range(i, bands)]
    wide = 128 // BAND
    groups = -(-len(pairs) // wide)
    groups += groups % 2
    return pairs, wide, groups


def pack_gram(gram):
    pairs, wide, groups = packing(gram.shape[0])
    out = []
    for g in range(groups):
        chosen = pairs[g * wide:(g + 1) * wide]
        parts = [gram[i * BAND:(i + 1) * BAND, j * BAND:(j + 1) * BAND] for i, j in chosen]
        parts += [jnp.zeros((BAND, BAND), F32)] * (wide - len(chosen))
        out.append(jnp.concatenate(parts, axis=1))
    return jnp.concatenate(out, axis=0)


def fold_square(x, rank):
    return (x[:rank, :rank] + x[rank:, rank:]) + (x[:rank, rank:] + x[rank:, :rank])


def gram_kernel(scale, count, *refs):
    o_ref = refs[-1]
    rank = refs[count].shape[0]
    total = None
    for own_ref, got_ref in zip(refs[:count], refs[count:2 * count]):
        s = own_ref[:rank, :].astype(F32) + own_ref[rank:, :].astype(F32) + got_ref[...].astype(F32)
        high = s.astype(BF16)
        both = jnp.concatenate([high, (s - high.astype(F32)).astype(BF16)], axis=0)
        term = dot(both, both, ((1,), (1,)))
        total = term if total is None else total + term
    o_ref[...] = pack_gram(fold_square(total, rank) * scale)


def own_gram(own, got, scale, after=()):
    rank = got[0].shape[0]
    rows = sum(v.shape[1] for v in got)
    return pl.pallas_call(
        functools.partial(gram_kernel, scale, len(own)),
        in_specs=[HELD] * (2 * len(own)) + [UNREAD] * len(after),
        out_shape=jax.ShapeDtypeStruct((packing(rank)[2] * BAND, 128), F32),
        compiler_params=params(),
        cost_estimate=cost(8 * rank * rank * rows, 6 * rank * rows),
        name="gram",
    )(*own, *got, *after)


def wide_lanes(x, n):
    reps = -(-n // 128)
    return jnp.concatenate([x] * reps, axis=1)[:, :n] if reps > 1 else x[:, :n]


def band_rows(block, b):
    n = block.shape[1]
    count = BAND // 8
    part = [block[8 * i:8 * i + 8, :] for i in range(count)]
    sub = iota((8, n), 0)
    lane = iota((8, n), 1)
    for m in range(count):
        c0 = b * BAND + 8 * m
        live = count - m
        col = [
            [jnp.broadcast_to(part[m + i][:, c0 + k:c0 + k + 1], (8, 128)) for i in range(live)]
            for k in range(8)
        ]
        here = (lane >= c0) & (lane < c0 + 8)
        part[m] = jnp.where(here, jnp.where(lane - c0 == sub, 1.0, 0.0), part[m])
        for i in range(1, live):
            part[m + i] = jnp.where(here, 0.0, part[m + i])
        for j in range(8):
            inv_root = lax.rsqrt(jnp.broadcast_to(col[j][0][j:j + 1, :], (8, 128)))
            low = [x * inv_root for x in col[j]]
            for k in range(j + 1, 8):
                t = jnp.broadcast_to(low[0][k:k + 1, :], (8, 128))
                for i in range(live):
                    col[k][i] = col[k][i] - low[i] * t
            row = jnp.broadcast_to(part[m][j:j + 1, :], (8, n)) * wide_lanes(inv_root, n)
            for i in range(live):
                new = part[m + i] - wide_lanes(low[i], n) * row
                if i == 0:
                    new = jnp.where(sub > j, new, jnp.where(sub == j, row, part[m]))
                part[m + i] = new
    return jnp.concatenate(part, axis=0)


def factor_kernel(rank, me_ref, mine_ref, other_ref, *refs):
    o_ref, g_ref = refs[-2:]
    pairs, wide, groups = packing(rank)
    half = groups * BAND // 2
    mine_at = pl.multiple_of((me_ref[0] & 1) * half, half)
    g_ref[pl.ds(mine_at, half), :] = mine_ref[...]
    g_ref[pl.ds(pl.multiple_of(half - mine_at, half), half), :] = other_ref[...]
    o_ref[...] = jnp.zeros((rank, rank), F32)
    for at, (i, j) in enumerate(pairs):
        g, k = at // wide, at % wide
        o_ref[i * BAND:(i + 1) * BAND, j * BAND:(j + 1) * BAND] = g_ref[
            g * BAND:(g + 1) * BAND, k * BAND:(k + 1) * BAND]
    for b in range(rank // BAND):
        lo, hi = b * BAND, (b + 1) * BAND
        r = band_rows(o_ref[lo:hi, :], b)
        rows, cols = iota(r.shape, 0), iota(r.shape, 1)
        r = jnp.where((cols >= lo) & (cols < hi) & (cols - lo > rows), 0.0, r)
        o_ref[lo:hi, :] = jnp.where(cols < hi, r, 0.0)
        if hi < rank:
            left = jnp.where(cols >= hi, r, 0.0)
            update = dot(left, r, ((0,), (0,)), HI)
            kept = jnp.where(iota((rank - hi, rank), 1) // BAND == b, 0.0, o_ref[hi:, :])
            o_ref[hi:, :] = kept - update[hi:, :]


def factor_inverse(me, mine, other, rank, after=()):
    return pl.pallas_call(
        functools.partial(factor_kernel, rank),
        in_specs=[pl.BlockSpec(memory_space=pltpu.SMEM)] + [HELD] * 2 + [UNREAD] * len(after),
        out_shape=jax.ShapeDtypeStruct((rank, rank), F32),
        scratch_shapes=[pltpu.VMEM((2 * mine.shape[0], 128), F32)],
        compiler_params=params(),
        cost_estimate=cost(8e9, 4 * rank * rank),
        name="factor",
    )(me, mine, other, *after)


def project_kernel(count, wide, has_base, aside, finish, ids_ref, *refs):
    s_refs, x_refs = refs[:count], refs[count:count * (1 + wide)]
    at = count * (1 + wide)
    beside = refs[at + has_base:at + has_base + aside]
    rest = refs[at + has_base + aside:]
    t_ref = rest[-1]
    rank = t_ref.shape[1]

    @pl.when(pl.program_id(0) == 0)
    def _():
        t_ref[...] = refs[at][...] if has_base else jnp.zeros_like(t_ref)

    for w in range(wide):
        total = None
        for k in range(count):
            term = dot(s_refs[k][...], x_refs[w * count + k][...], ((1,), (0,)))
            total = term if total is None else total + term
        t_ref[w] += total if total.shape[0] == rank else total[:rank] + total[rank:]
    if finish is not None:
        @pl.when(pl.program_id(0) == pl.num_programs(0) - 1)
        def _():
            finish(t_ref, ids_ref, beside, *rest[:-1])


def project(ids, work, x, rank, base, rows, beside=(), finish=None, outs=(), scratch=(), after=()):
    wide = 1 + len(work[0][2])
    height = work[0][0].shape[0]
    depth = x.shape[1]
    unit = UNIT
    steps = unit // rows
    parts, s_specs, own_specs, more, more_specs = [], [], [], [[] for _ in range(wide - 1)], []
    for array, slot, lent in work:
        for u in range(array.shape[1] // unit):
            parts.append(array)
            s_specs.append(pl.BlockSpec((height, rows), lambda i, ids, u=u: (0, u * steps + i)))
            own_specs.append(pl.BlockSpec(
                (rows, depth), lambda i, ids, u=u, slot=slot: ((ids[slot] + u) * steps + i, 0)))
            more_specs.append(pl.BlockSpec((rows, depth), lambda i, ids, u=u: (u * steps + i, 0)))
            for w in range(wide - 1):
                more[w].append(lent[w])
    count = len(parts)
    bases = [] if base is None else [base]
    whole = pl.BlockSpec((wide, rank, depth), lambda i, ids: (0, 0, 0))
    t_shape = jax.ShapeDtypeStruct((wide, rank, depth), F32)
    if finish is None:
        out_specs, out_shape, scratch_shapes = whole, t_shape, []
    else:
        out_specs = [pl.BlockSpec(o.shape, lambda i, ids: (0, 0)) for o in outs]
        out_shape = list(outs)
        scratch_shapes = list(scratch) + [pltpu.VMEM((wide, rank, depth), F32)]
    return pl.pallas_call(
        functools.partial(
            project_kernel, count, wide, len(bases), len(beside) + len(after), finish),
        grid_spec=pltpu.PrefetchScalarGridSpec(
            num_scalar_prefetch=1,
            grid=(steps,),
            in_specs=s_specs + own_specs + more_specs * (wide - 1) + [whole] * len(bases)
            + [pl.BlockSpec(v.shape, lambda i, ids: (0, 0)) for v in beside] + [UNREAD] * len(after),
            out_specs=out_specs,
            scratch_shapes=scratch_shapes,
        ),
        out_shape=out_shape,
        compiler_params=params(),
        cost_estimate=cost(
            2 * height * depth * unit * count * wide, unit * count * (depth * wide + height) * 2),
        name="project",
    )(ids, *parts, *([x] * count), *[v for values in more for v in values], *bases, *beside, *after)


def folding(rank, width):
    best = 1
    for f in range(1, rank + 1):
        if rank % f == 0 and (rank // f) % 8 == 0 and f * width <= 128:
            best = f
    return best


def reverse_bits(p, count):
    return sum(1 << (count - 1 - b) for b in range(count) if (p >> b) & 1)


def tail(pieces, samp, per_node, width_cols, t_ref, ids_ref, beside, *refs):
    outs, hold = refs[:-1], refs[-1]
    wide, rank, depth = t_ref.shape
    width = per_node * width_cols
    fold = folding(rank, width)
    tall = rank // fold
    me_node = ids_ref[ids_ref.shape[0] - 1]
    dst = iota((depth, depth), 1)
    src = iota((depth, depth), 0)
    a, rest = dst // (samp * width), dst % (samp * width)
    s, rest = rest // width, rest % width
    want = (a * per_node + rest // width_cols) * (samp * width_cols) + s * width_cols + rest % width_cols
    move = jnp.where(src == want, 1.0, 0.0).astype(BF16)
    bits = pieces.bit_length() - 1
    for w in range(wide):
        t = t_ref[w]
        high = t.astype(BF16)
        mid = (t - high.astype(F32)).astype(BF16)
        low = (t - high.astype(F32) - mid.astype(F32)).astype(BF16)
        moved = dot(jnp.concatenate([high, mid, low], axis=0), move, ((1,), (0,)))
        moved = moved[:rank] + moved[rank:2 * rank] + moved[2 * rank:]
        for i in range(pieces):
            piece = moved[:, i * width:(i + 1) * width]
            parts = [piece[f * tall:(f + 1) * tall] for f in range(fold)]
            if fold * width < 128:
                parts.append(jnp.zeros((tall, 128 - fold * width), F32))
            hold[i] = jnp.concatenate(parts, axis=1)
        for p in range(pieces):
            outs[w][p * tall:(p + 1) * tall, :] = hold[me_node ^ reverse_bits(p, bits)]


def core_kernel(count, inv_ref, *refs):
    both, high, low = (refs[k * count:(k + 1) * count] for k in range(3))
    core_ref = refs[-1]
    rank = inv_ref.shape[0]
    at = 0
    for c in range(count):
        s = both[c][:rank, :].astype(F32) + both[c][rank:, :].astype(F32)
        s = s + (high[c][...].astype(F32) + low[c][...].astype(F32))
        rows = s.shape[1]
        core_ref[:, at:at + rows] = dot(inv_ref[...], s, ((1,), (0,)), HI)
        at += rows


def core_product(inverse, both, high, low):
    rank = inverse.shape[0]
    count = len(both)
    rows = sum(v.shape[1] for v in high)
    return pl.pallas_call(
        functools.partial(core_kernel, count),
        out_shape=jax.ShapeDtypeStruct((rank, rows), F32),
        compiler_params=params(),
        cost_estimate=cost(12 * rank * rank * rows, 12 * rank * rows),
        name="core",
    )(inverse, *both, *high, *low)


def coefficient_kernel(scale, per_node, width_cols, inv_ref, piece_ref, o_ref):
    rank = inv_ref.shape[0]
    width = per_node * width_cols
    fold = folding(rank, width)
    total = piece_ref[...]
    total = jnp.concatenate([total[:, f * width:(f + 1) * width] for f in range(fold)], axis=0)
    out = dot(total, inv_ref[...], ((0,), (1,)), HI) * scale
    o_ref[...] = jnp.concatenate(
        [out[p * width_cols:(p + 1) * width_cols, :] for p in range(per_node)], axis=1)


def coefficients(inverse, piece, scale, per_node, width_cols):
    rank = inverse.shape[0]
    return pl.pallas_call(
        functools.partial(coefficient_kernel, scale, per_node, width_cols),
        out_shape=jax.ShapeDtypeStruct((width_cols, per_node * rank), F32),
        compiler_params=params(),
        cost_estimate=cost(12 * rank * rank * per_node * width_cols, 4 * rank * rank),
        name="coefficient",
    )(inverse, piece)


def swap(value, axis, size, bit):
    return lax.ppermute(value, axis, [(i, i ^ bit) for i in range(size)])


def body(snapshots, sketch_matrix):
    rows_all = snapshots.shape[0]
    rank = sketch_matrix.shape[1]
    samp = lax.axis_size("samp")
    node = lax.axis_size("node")
    total = rows_all * node
    quarter = rows_all // samp
    me_s = lax.axis_index("samp").astype(jnp.int32)
    me_n = lax.axis_index("node").astype(jnp.int32)
    w_t = sketch_matrix.T
    last = samp // 2
    near = range(1, last)
    starts, sizes = (0, UNIT), (UNIT, quarter - UNIT)
    blocks = [(last, 0), (last, 1), (0, 0), (0, 1)]

    def block_of(base, c):
        return (me_s ^ base) * (quarter // UNIT) + starts[c] // UNIT

    borrowed = {b: [] for b in blocks}
    ws, w_at = [w_t], 0
    for d in near:
        out = lend(jnp.stack([block_of(blocks[0][0] ^ d, blocks[0][1])]), snapshots, UNIT, w_t)
        w_at = out[0].shape[0] - rank
        out += lend(jnp.stack([block_of(base ^ d, c) for base, c in blocks[1:]]), snapshots, UNIT, after=out)
        for b, v in zip(blocks, out):
            borrowed[b].append(swap(v, "samp", samp, d))
        ws.append(borrowed[blocks[0]][-1])

    pairs, arrived, done = {}, {}, ()
    for base, c in blocks:
        both, high = sketch(
            block_of(base, c)[None], snapshots, ws, borrowed[base, c], UNIT, w_at, done)
        done = (high,)
        pairs[base, c] = both
        arrived[base ^ last, c] = swap(high, "samp", samp, last)
    own = [pairs[0, c] for c in range(2)]
    got_high = [arrived[0, c] for c in range(2)]

    ids = jnp.stack([block_of(*b) for b in blocks] + [me_n])
    slot = {b: k for k, b in enumerate(blocks)}
    rows = min(UNIT, 512)
    t = project(ids, [(pairs[b], slot[b], borrowed[b]) for b in blocks], snapshots, rank, None, rows)

    packed = own_gram(own, got_high, 1.0 / total, (t,))
    upper = (me_s & 1) == 1
    halves = jnp.split(packed, 2, axis=0)
    half = jnp.where(upper, halves[1], halves[0])
    stages = []
    half = half + swap(jnp.where(upper, halves[0], halves[1]), "samp", samp, 1)
    stages.append(half)
    bit = 2
    while bit < samp:
        half = half + swap(half, "samp", samp, bit)
        stages.append(half)
        bit *= 2
    bit = 1
    while bit < node:
        half = half + swap(half, "node", node, bit)
        stages.append(half)
        bit *= 2
    other = swap(half, "samp", samp, 1)

    order = [(base ^ last, c) for base, c in blocks]
    early, late = order[:-1], order[-1:]
    t = project(
        ids, [(arrived[b], slot[b], borrowed[b]) for b in early], snapshots, rank, t, rows,
        after=(stages[EARLY_STAGE],))
    per_node = P1 // node
    width_cols = P2 // samp
    tall = rank // folding(rank, per_node * width_cols)
    messages = project(
        ids, [(arrived[b], slot[b], borrowed[b]) for b in late], snapshots, rank, t, rows, (),
        functools.partial(tail, node, samp, per_node, width_cols),
        [jax.ShapeDtypeStruct((node * tall, 128), F32)] * last,
        [pltpu.VMEM((node, tall, 128), F32)], (stages[LATE_STAGE],))
    inverse = factor_inverse(me_s[None], half, other, rank, (messages[0],))

    got_low = []
    for c in range(2):
        low, _ = lax.optimization_barrier((pairs[last, c][rank:], arrived[late[0]]))
        got_low.append(swap(low, "samp", samp, last))

    pieces = messages[0]
    for d in near:
        pieces = pieces + swap(messages[d], "samp", samp, d)
    bit = 1
    while bit < node:
        edge = pieces.shape[0] // 2
        pieces = pieces[:edge] + swap(pieces[edge:], "node", node, bit)
        bit *= 2
    spread = node // samp
    route = [
        (n * samp + s, (s * spread + n // samp) * samp + n % samp) for n in range(node) for s in range(samp)
    ]
    piece = lax.ppermute(pieces, ("node", "samp"), route)
    core = core_product(inverse, own, got_high, got_low)
    coef = coefficients(inverse, piece, 1.0 / total, per_node, width_cols)
    return (core.T, coef.T)


def solution(mesh):
    placed = (P("node", "samp"), P("samp", None))
    return jax.shard_map(
        body,
        mesh=mesh,
        in_specs=placed,
        out_specs=(P(("node", "samp"), None), P("node", "samp")),
        check_vma=False,
    )
```

```python
import functools
import jax
import jax.numpy as jnp
from jax import lax
from jax.experimental import pallas as pl
from jax.experimental.pallas import tpu as pltpu
from jax.sharding import PartitionSpec as P

P1 = 64
P2 = 32
BAND = 32
UNIT = 1024
SKETCH_ROWS = 1024
LEND_PARTS = 4
FACTOR_FIRST = True
FACTOR_COST = 8e5
COST_CUT = 1
F32 = jnp.float32
BF16 = jnp.bfloat16
HI = lax.Precision.HIGHEST
UNREAD = pl.BlockSpec(memory_space=pl.ANY)
HELD = pl.BlockSpec(memory_space=pltpu.VMEM)
VMEM_LIMIT = 48 * 1024 * 1024


def iota(shape, dim):
    return lax.broadcasted_iota(jnp.int32, shape, dim)


def dot(a, b, dims, precision=None):
    return lax.dot_general(a, b, (dims, ((), ())), precision=precision, preferred_element_type=F32)


def params():
    return pltpu.CompilerParams(vmem_limit_bytes=VMEM_LIMIT)


def cost(flops, moved):
    return pl.CostEstimate(flops=int(flops) // COST_CUT, bytes_accessed=int(moved) // COST_CUT, transcendentals=0)


def lend_kernel(size, stride, at, ids_ref, x_ref, *refs):
    count = ids_ref.shape[0]
    extra = 1 if at is not None else 0
    outs, sems = refs[-1 - count:-1], refs[-1]
    copies = []
    for k in range(count):
        first = pl.multiple_of(ids_ref[k] * size, size)
        for part in range(size // stride):
            copies.append(pltpu.make_async_copy(
                x_ref.at[pl.ds(first + part * stride, stride)],
                outs[k].at[pl.ds(part * stride, stride)],
                sems.at[len(copies)]))
    if extra:
        copies.append(pltpu.make_async_copy(
            refs[0], outs[0].at[pl.ds(at, refs[0].shape[0])], sems.at[len(copies)]))
    for copy in copies:
        copy.start()
    for copy in copies:
        copy.wait()


def lend(ids, x, size, w=None, after=()):
    count = ids.shape[0]
    depth = x.shape[1]
    stride = size // LEND_PARTS
    at, height = None, size
    if w is not None:
        rank = w.shape[0]
        at = -(-size // rank) * rank
        height = at + rank
    more = [] if w is None else [w]
    return pl.pallas_call(
        functools.partial(lend_kernel, size, stride, at),
        in_specs=[pl.BlockSpec(memory_space=pltpu.SMEM)] + [UNREAD] * (1 + len(more) + len(after)),
        out_specs=[HELD] * count,
        out_shape=[jax.ShapeDtypeStruct((height, depth), BF16)] * count,
        scratch_shapes=[pltpu.SemaphoreType.DMA((LEND_PARTS * count + len(more),))],
        compiler_params=params(),
        cost_estimate=cost(0, 4 * count * height * depth),
        name="lend",
    )(ids, x, *more, *after)


def sketch_kernel(count, ids_ref, x_ref, *refs):
    w_refs, x_refs = refs[:count], (x_ref,) + refs[count:2 * count - 1]
    both_ref, high_ref = refs[-2:]
    rank = high_ref.shape[0]
    s = None
    for w_ref, ref in zip(w_refs, x_refs):
        term = dot(w_ref[...], ref[...], ((1,), (1,)))
        s = term if s is None else s + term
    high = s.astype(BF16)
    high_ref[...] = high
    both_ref[:rank, :] = high
    both_ref[rank:, :] = (s - high.astype(F32)).astype(BF16)


def sketch(ids, x, ws, extra, size, w_at, after=()):
    rank, depth = ws[0].shape
    count = len(ws)
    rows = min(size, SKETCH_ROWS)
    return pl.pallas_call(
        functools.partial(sketch_kernel, count),
        grid_spec=pltpu.PrefetchScalarGridSpec(
            num_scalar_prefetch=1,
            grid=(size // rows,),
            in_specs=[pl.BlockSpec((rows, depth), lambda i, ids: (ids[0] + i, 0))]
            + [pl.BlockSpec((rank, depth), lambda i, ids: (0, 0))]
            + [pl.BlockSpec((rank, depth), lambda i, ids: (w_at // rank, 0))] * (count - 1)
            + [pl.BlockSpec((rows, depth), lambda i, ids: (i, 0))] * (count - 1)
            + [UNREAD] * len(after),
            out_specs=[
                pl.BlockSpec((2 * rank, rows), lambda i, ids: (0, i)),
                pl.BlockSpec((rank, rows), lambda i, ids: (0, i)),
            ],
        ),
        out_shape=(
            jax.ShapeDtypeStruct((2 * rank, size), BF16),
            jax.ShapeDtypeStruct((rank, size), BF16),
        ),
        compiler_params=params(),
        cost_estimate=cost(2 * rank * depth * size * count, size * (depth * 2 * count + rank * 6)),
        name="sketch",
    )(ids, x, *ws, *extra, *after)


def packing(rank):
    bands = rank // BAND
    pairs = [(i, j) for i in range(bands) for j in range(i, bands)]
    wide = 128 // BAND
    groups = -(-len(pairs) // wide)
    groups += groups % 2
    return pairs, wide, groups


def pack_gram(gram):
    pairs, wide, groups = packing(gram.shape[0])
    out = []
    for g in range(groups):
        chosen = pairs[g * wide:(g + 1) * wide]
        parts = [gram[i * BAND:(i + 1) * BAND, j * BAND:(j + 1) * BAND] for i, j in chosen]
        parts += [jnp.zeros((BAND, BAND), F32)] * (wide - len(chosen))
        out.append(jnp.concatenate(parts, axis=1))
    return jnp.concatenate(out, axis=0)


def fold_square(x, rank):
    return (x[:rank, :rank] + x[rank:, rank:]) + (x[:rank, rank:] + x[rank:, :rank])


def gram_kernel(scale, has_base, own_ref, got_ref, *refs):
    o_ref = refs[-1]
    rank = got_ref.shape[0]
    s = own_ref[:rank, :].astype(F32) + own_ref[rank:, :].astype(F32) + got_ref[...].astype(F32)
    high = s.astype(BF16)
    both = jnp.concatenate([high, (s - high.astype(F32)).astype(BF16)], axis=0)
    total = fold_square(dot(both, both, ((1,), (1,))), rank)
    if has_base:
        total = total + refs[0][...]
    o_ref[...] = total if scale is None else pack_gram(total * scale)


def own_gram(own, got, base, scale, after=()):
    rank, rows = got.shape
    bases = [] if base is None else [base]
    shape = (rank, rank) if scale is None else (packing(rank)[2] * BAND, 128)
    return pl.pallas_call(
        functools.partial(gram_kernel, scale, len(bases)),
        in_specs=[HELD] * (2 + len(bases)) + [UNREAD] * len(after),
        out_shape=jax.ShapeDtypeStruct(shape, F32),
        compiler_params=params(),
        cost_estimate=cost(8 * rank * rank * rows, 6 * rank * rows),
        name="gram",
    )(own, got, *bases, *after)


def wide_lanes(x, n):
    reps = -(-n // 128)
    return jnp.concatenate([x] * reps, axis=1)[:, :n] if reps > 1 else x[:, :n]


def band_rows(block, b):
    n = block.shape[1]
    count = BAND // 8
    part = [block[8 * i:8 * i + 8, :] for i in range(count)]
    sub = iota((8, n), 0)
    lane = iota((8, n), 1)
    for m in range(count):
        c0 = b * BAND + 8 * m
        live = count - m
        col = [
            [jnp.broadcast_to(part[m + i][:, c0 + k:c0 + k + 1], (8, 128)) for i in range(live)]
            for k in range(8)
        ]
        here = (lane >= c0) & (lane < c0 + 8)
        part[m] = jnp.where(here, jnp.where(lane - c0 == sub, 1.0, 0.0), part[m])
        for i in range(1, live):
            part[m + i] = jnp.where(here, 0.0, part[m + i])
        for j in range(8):
            inv_root = lax.rsqrt(jnp.broadcast_to(col[j][0][j:j + 1, :], (8, 128)))
            low = [x * inv_root for x in col[j]]
            for k in range(j + 1, 8):
                t = jnp.broadcast_to(low[0][k:k + 1, :], (8, 128))
                for i in range(live):
                    col[k][i] = col[k][i] - low[i] * t
            row = jnp.broadcast_to(part[m][j:j + 1, :], (8, n)) * wide_lanes(inv_root, n)
            for i in range(live):
                new = part[m + i] - wide_lanes(low[i], n) * row
                if i == 0:
                    new = jnp.where(sub > j, new, jnp.where(sub == j, row, part[m]))
                part[m + i] = new
    return jnp.concatenate(part, axis=0)


def factor_kernel(rank, g_ref, *refs):
    o_ref = refs[-1]
    pairs, wide, _ = packing(rank)
    o_ref[...] = jnp.zeros((rank, rank), F32)
    for at, (i, j) in enumerate(pairs):
        g, k = at // wide, at % wide
        o_ref[i * BAND:(i + 1) * BAND, j * BAND:(j + 1) * BAND] = g_ref[
            g * BAND:(g + 1) * BAND, k * BAND:(k + 1) * BAND]
    for b in range(rank // BAND):
        lo, hi = b * BAND, (b + 1) * BAND
        r = band_rows(o_ref[lo:hi, :], b)
        rows, cols = iota(r.shape, 0), iota(r.shape, 1)
        r = jnp.where((cols >= lo) & (cols < hi) & (cols - lo > rows), 0.0, r)
        o_ref[lo:hi, :] = jnp.where(cols < hi, r, 0.0)
        if hi < rank:
            left = jnp.where(cols >= hi, r, 0.0)
            update = dot(left, r, ((0,), (0,)), HI)
            kept = jnp.where(iota((rank - hi, rank), 1) // BAND == b, 0.0, o_ref[hi:, :])
            o_ref[hi:, :] = kept - update[hi:, :]


def factor_inverse(packed, rank, after=()):
    return pl.pallas_call(
        functools.partial(factor_kernel, rank),
        in_specs=[HELD] + [UNREAD] * len(after),
        out_shape=jax.ShapeDtypeStruct((rank, rank), F32),
        compiler_params=params(),
        cost_estimate=cost(FACTOR_COST, 4 * rank * rank),
        name="factor",
    )(packed, *after)


def project_kernel(count, wide, has_base, aside, finish, ids_ref, *refs):
    s_refs, x_refs = refs[:count], refs[count:count * (1 + wide)]
    at = count * (1 + wide)
    beside = refs[at + has_base:at + has_base + aside]
    rest = refs[at + has_base + aside:]
    t_ref = rest[-1]
    rank = t_ref.shape[1]

    @pl.when(pl.program_id(0) == 0)
    def _():
        t_ref[...] = refs[at][...] if has_base else jnp.zeros_like(t_ref)

    for w in range(wide):
        total = None
        for k in range(count):
            term = dot(s_refs[k][...], x_refs[w * count + k][...], ((1,), (0,)))
            total = term if total is None else total + term
        t_ref[w] += total if total.shape[0] == rank else total[:rank] + total[rank:]
    if finish is not None:
        @pl.when(pl.program_id(0) == pl.num_programs(0) - 1)
        def _():
            finish(t_ref, ids_ref, beside, *rest[:-1])


def project(ids, work, x, rank, base, rows, beside=(), finish=None, outs=(), scratch=(), after=()):
    wide = 1 + len(work[0][2])
    height = work[0][0].shape[0]
    depth = x.shape[1]
    unit = UNIT
    steps = unit // rows
    parts, s_specs, own_specs, more, more_specs = [], [], [], [[] for _ in range(wide - 1)], []
    for array, slot, lent in work:
        for u in range(array.shape[1] // unit):
            parts.append(array)
            s_specs.append(pl.BlockSpec((height, rows), lambda i, ids, u=u: (0, u * steps + i)))
            own_specs.append(pl.BlockSpec(
                (rows, depth), lambda i, ids, u=u, slot=slot: ((ids[slot] + u) * steps + i, 0)))
            more_specs.append(pl.BlockSpec((rows, depth), lambda i, ids, u=u: (u * steps + i, 0)))
            for w in range(wide - 1):
                more[w].append(lent[w])
    count = len(parts)
    bases = [] if base is None else [base]
    whole = pl.BlockSpec((wide, rank, depth), lambda i, ids: (0, 0, 0))
    t_shape = jax.ShapeDtypeStruct((wide, rank, depth), F32)
    if finish is None:
        out_specs, out_shape, scratch_shapes = whole, t_shape, []
    else:
        out_specs = [pl.BlockSpec(o.shape, lambda i, ids: (0, 0)) for o in outs]
        out_shape = list(outs)
        scratch_shapes = list(scratch) + [pltpu.VMEM((wide, rank, depth), F32)]
    return pl.pallas_call(
        functools.partial(
            project_kernel, count, wide, len(bases), len(beside) + len(after), finish),
        grid_spec=pltpu.PrefetchScalarGridSpec(
            num_scalar_prefetch=1,
            grid=(steps,),
            in_specs=s_specs + own_specs + more_specs * (wide - 1) + [whole] * len(bases)
            + [pl.BlockSpec(v.shape, lambda i, ids: (0, 0)) for v in beside] + [UNREAD] * len(after),
            out_specs=out_specs,
            scratch_shapes=scratch_shapes,
        ),
        out_shape=out_shape,
        compiler_params=params(),
        cost_estimate=cost(
            2 * height * depth * unit * count * wide, unit * count * (depth * wide + height) * 2),
        name="project",
    )(ids, *parts, *([x] * count), *[v for values in more for v in values], *bases, *beside, *after)


def folding(rank, width):
    best = 1
    for f in range(1, rank + 1):
        if rank % f == 0 and (rank // f) % 8 == 0 and f * width <= 128:
            best = f
    return best


def reverse_bits(p, count):
    return sum(1 << (count - 1 - b) for b in range(count) if (p >> b) & 1)


def tail(pieces, samp, per_node, width_cols, t_ref, ids_ref, beside, *refs):
    outs, hold = refs[:-1], refs[-1]
    wide, rank, depth = t_ref.shape
    width = per_node * width_cols
    fold = folding(rank, width)
    tall = rank // fold
    me_node = ids_ref[ids_ref.shape[0] - 1]
    dst = iota((depth, depth), 1)
    src = iota((depth, depth), 0)
    a, rest = dst // (samp * width), dst % (samp * width)
    s, rest = rest // width, rest % width
    want = (a * per_node + rest // width_cols) * (samp * width_cols) + s * width_cols + rest % width_cols
    move = jnp.where(src == want, 1.0, 0.0).astype(BF16)
    bits = pieces.bit_length() - 1
    for w in range(wide):
        t = t_ref[w]
        high = t.astype(BF16)
        mid = (t - high.astype(F32)).astype(BF16)
        low = (t - high.astype(F32) - mid.astype(F32)).astype(BF16)
        moved = dot(jnp.concatenate([high, mid, low], axis=0), move, ((1,), (0,)))
        moved = moved[:rank] + moved[rank:2 * rank] + moved[2 * rank:]
        for i in range(pieces):
            piece = moved[:, i * width:(i + 1) * width]
            parts = [piece[f * tall:(f + 1) * tall] for f in range(fold)]
            if fold * width < 128:
                parts.append(jnp.zeros((tall, 128 - fold * width), F32))
            hold[i] = jnp.concatenate(parts, axis=1)
        for p in range(pieces):
            outs[w][p * tall:(p + 1) * tall, :] = hold[me_node ^ reverse_bits(p, bits)]


def core_kernel(count, inv_ref, *refs):
    both, high, low = (refs[k * count:(k + 1) * count] for k in range(3))
    core_ref = refs[-1]
    rank = inv_ref.shape[0]
    at = 0
    for c in range(count):
        s = both[c][:rank, :].astype(F32) + both[c][rank:, :].astype(F32)
        s = s + (high[c][...].astype(F32) + low[c][...].astype(F32))
        rows = s.shape[1]
        core_ref[:, at:at + rows] = dot(inv_ref[...], s, ((1,), (0,)), HI)
        at += rows


def core_product(inverse, both, high, low):
    rank = inverse.shape[0]
    count = len(both)
    rows = sum(v.shape[1] for v in high)
    return pl.pallas_call(
        functools.partial(core_kernel, count),
        out_shape=jax.ShapeDtypeStruct((rank, rows), F32),
        compiler_params=params(),
        cost_estimate=cost(12 * rank * rank * rows, 12 * rank * rows),
        name="core",
    )(inverse, *both, *high, *low)


def coefficient_kernel(scale, per_node, width_cols, inv_ref, piece_ref, o_ref):
    rank = inv_ref.shape[0]
    width = per_node * width_cols
    fold = folding(rank, width)
    total = piece_ref[...]
    total = jnp.concatenate([total[:, f * width:(f + 1) * width] for f in range(fold)], axis=0)
    out = dot(total, inv_ref[...], ((0,), (1,)), HI) * scale
    o_ref[...] = jnp.concatenate(
        [out[p * width_cols:(p + 1) * width_cols, :] for p in range(per_node)], axis=1)


def coefficients(inverse, piece, scale, per_node, width_cols):
    rank = inverse.shape[0]
    return pl.pallas_call(
        functools.partial(coefficient_kernel, scale, per_node, width_cols),
        out_shape=jax.ShapeDtypeStruct((width_cols, per_node * rank), F32),
        compiler_params=params(),
        cost_estimate=cost(12 * rank * rank * per_node * width_cols, 4 * rank * rank),
        name="coefficient",
    )(inverse, piece)


def swap(value, axis, size, bit):
    return lax.ppermute(value, axis, [(i, i ^ bit) for i in range(size)])


def body(snapshots, sketch_matrix):
    rows_all = snapshots.shape[0]
    rank = sketch_matrix.shape[1]
    samp = lax.axis_size("samp")
    node = lax.axis_size("node")
    total = rows_all * node
    quarter = rows_all // samp
    me_s = lax.axis_index("samp").astype(jnp.int32)
    me_n = lax.axis_index("node").astype(jnp.int32)
    w_t = sketch_matrix.T
    last = samp // 2
    near = range(1, last)
    starts, sizes = (0, UNIT), (UNIT, quarter - UNIT)
    blocks = [(last, 0), (last, 1), (0, 0), (0, 1)]

    def block_of(base, c):
        return (me_s ^ base) * (quarter // UNIT) + starts[c] // UNIT

    borrowed = {b: [] for b in blocks}
    ws, w_at = [w_t], 0
    for d in near:
        out = lend(jnp.stack([block_of(blocks[0][0] ^ d, blocks[0][1])]), snapshots, UNIT, w_t)
        w_at = out[0].shape[0] - rank
        out += lend(jnp.stack([block_of(base ^ d, c) for base, c in blocks[1:]]), snapshots, UNIT, after=out)
        for b, v in zip(blocks, out):
            borrowed[b].append(swap(v, "samp", samp, d))
        ws.append(borrowed[blocks[0]][-1])

    pairs, highs, arrived, done = {}, {}, {}, ()

    def cross(b):
        arrived[b[0] ^ last, b[1]] = swap(highs[b], "samp", samp, last)

    ids = jnp.stack([block_of(*b) for b in blocks] + [me_n])
    slot = {b: k for k, b in enumerate(blocks)}
    rows = min(UNIT, 512)
    for b in blocks:
        pairs[b], highs[b] = sketch(block_of(*b)[None], snapshots, ws, borrowed[b], UNIT, w_at, done)
        done = (highs[b],)
        if b[0] == last:
            cross(b)
    own = [pairs[0, c] for c in range(2)]
    got_high = [arrived[0, c] for c in range(2)]
    t = project(ids, [(pairs[b], slot[b], borrowed[b]) for b in blocks], snapshots, rank, None, rows)

    gram = own_gram(own[0], got_high[0], None, None, (t,))
    gram = own_gram(own[1], got_high[1], gram, 1.0 / total)
    gram = gram + swap(gram, "samp", samp, last)
    for b in blocks:
        if b[0] == 0:
            highs[b], _ = lax.optimization_barrier((highs[b], gram))
            cross(b)
    bit = last // 2
    while bit:
        gram = gram + swap(gram, "samp", samp, bit)
        bit //= 2
    stages = [gram]
    bit = 1
    while bit < node:
        gram = gram + swap(gram, "node", node, bit)
        stages.append(gram)
        bit *= 2
    inverse = factor_inverse(gram, rank)

    order = [(base ^ last, c) for base, c in blocks]
    early, late = order[:-1], order[-1:]
    t = project(
        ids, [(arrived[b], slot[b], borrowed[b]) for b in early], snapshots, rank, t, rows,
        after=(stages[0],))
    per_node = P1 // node
    width_cols = P2 // samp
    tall = rank // folding(rank, per_node * width_cols)
    messages = project(
        ids, [(arrived[b], slot[b], borrowed[b]) for b in late], snapshots, rank, t, rows, (),
        functools.partial(tail, node, samp, per_node, width_cols),
        [jax.ShapeDtypeStruct((node * tall, 128), F32)] * last,
        [pltpu.VMEM((node, tall, 128), F32)], (inverse,) if FACTOR_FIRST else ())

    got_low = []
    for c in range(2):
        low, _ = lax.optimization_barrier((pairs[last, c][rank:], arrived[late[0]]))
        got_low.append(swap(low, "samp", samp, last))

    pieces = messages[0]
    for d in near:
        pieces = pieces + swap(messages[d], "samp", samp, d)
    bit = 1
    while bit < node:
        edge = pieces.shape[0] // 2
        pieces = pieces[:edge] + swap(pieces[edge:], "node", node, bit)
        bit *= 2
    spread = node // samp
    route = [
        (n * samp + s, (s * spread + n // samp) * samp + n % samp) for n in range(node) for s in range(samp)
    ]
    piece = lax.ppermute(pieces, ("node", "samp"), route)
    core = core_product(inverse, own, got_high, got_low)
    coef = coefficients(inverse, piece, 1.0 / total, per_node, width_cols)
    return (core.T, coef.T)


def solution(mesh):
    placed = (P("node", "samp"), P("samp", None))
    return jax.shard_map(
        body,
        mesh=mesh,
        in_specs=placed,
        out_specs=(P(("node", "samp"), None), P("node", "samp")),
        check_vma=False,
    )
```

```python
import functools
import jax
import jax.numpy as jnp
from jax import lax
from jax.experimental import pallas as pl
from jax.experimental.pallas import tpu as pltpu
from jax.sharding import PartitionSpec as P

P1 = 64
P2 = 32
BAND = 32
UNIT = 1024
LEND_PARTS = 4
PLACE = (True, 2, True, 1, 2)
PROJECT_ROWS = 512
FACTOR_COST = 6e9
COST_CUT = 1
F32 = jnp.float32
BF16 = jnp.bfloat16
HI = lax.Precision.HIGHEST
UNREAD = pl.BlockSpec(memory_space=pl.ANY)
HELD = pl.BlockSpec(memory_space=pltpu.VMEM)
VMEM_LIMIT = 48 * 1024 * 1024


def iota(shape, dim):
    return lax.broadcasted_iota(jnp.int32, shape, dim)


def dot(a, b, dims, precision=None):
    return lax.dot_general(a, b, (dims, ((), ())), precision=precision, preferred_element_type=F32)


def params():
    return pltpu.CompilerParams(vmem_limit_bytes=VMEM_LIMIT)


def cost(flops, moved):
    return pl.CostEstimate(flops=int(flops) // COST_CUT, bytes_accessed=int(moved) // COST_CUT, transcendentals=0)


def lend_kernel(size, stride, at, ids_ref, x_ref, *refs):
    count = ids_ref.shape[0]
    extra = 1 if at is not None else 0
    outs, sems = refs[-1 - count:-1], refs[-1]
    copies = []
    for k in range(count):
        first = pl.multiple_of(ids_ref[k] * size, size)
        for part in range(size // stride):
            copies.append(pltpu.make_async_copy(
                x_ref.at[pl.ds(first + part * stride, stride)],
                outs[k].at[pl.ds(part * stride, stride)],
                sems.at[len(copies)]))
    if extra:
        copies.append(pltpu.make_async_copy(
            refs[0], outs[0].at[pl.ds(at, refs[0].shape[0])], sems.at[len(copies)]))
    for copy in copies:
        copy.start()
    for copy in copies:
        copy.wait()


def lend(ids, x, size, w=None, after=()):
    count = ids.shape[0]
    depth = x.shape[1]
    stride = size // LEND_PARTS
    at, height = None, size
    if w is not None:
        rank = w.shape[0]
        at = -(-size // rank) * rank
        height = at + rank
    more = [] if w is None else [w]
    return pl.pallas_call(
        functools.partial(lend_kernel, size, stride, at),
        in_specs=[pl.BlockSpec(memory_space=pltpu.SMEM)] + [UNREAD] * (1 + len(more) + len(after)),
        out_specs=[HELD] * count,
        out_shape=[jax.ShapeDtypeStruct((height, depth), BF16)] * count,
        scratch_shapes=[pltpu.SemaphoreType.DMA((LEND_PARTS * count + len(more),))],
        compiler_params=params(),
        cost_estimate=cost(0, 4 * count * height * depth),
        name="lend",
    )(ids, x, *more, *after)


def sketch_kernel(count, lent, ids_ref, x_ref, *refs):
    w_refs, x_refs = refs[:count], (x_ref,) + refs[count:2 * count - 1]
    both_ref, high_ref = refs[len(refs) - lent - 2:len(refs) - lent]
    rank = high_ref.shape[0]
    for k in range(lent):
        refs[len(refs) - lent + k][...] = refs[2 * count - 1 + k][...]
    s = None
    for w_ref, ref in zip(w_refs, x_refs):
        term = dot(w_ref[...], ref[...], ((1,), (1,)))
        s = term if s is None else s + term
    high = s.astype(BF16)
    high_ref[...] = high
    both_ref[:rank, :] = high
    both_ref[rank:, :] = (s - high.astype(F32)).astype(BF16)


def sketch(ids, x, ws, extra, size, w_at, after=()):
    rank, depth = ws[0].shape
    count = len(ws)
    lent = ids.shape[0] - 1
    return pl.pallas_call(
        functools.partial(sketch_kernel, count, lent),
        grid_spec=pltpu.PrefetchScalarGridSpec(
            num_scalar_prefetch=1,
            grid=(1,),
            in_specs=[pl.BlockSpec((size, depth), lambda i, ids: (ids[0], 0))]
            + [pl.BlockSpec((rank, depth), lambda i, ids: (0, 0))]
            + [pl.BlockSpec((rank, depth), lambda i, ids: (w_at // rank, 0))] * (count - 1)
            + [pl.BlockSpec((size, depth), lambda i, ids: (0, 0))] * (count - 1)
            + [pl.BlockSpec((size, depth), lambda i, ids, k=k: (ids[1 + k], 0)) for k in range(lent)]
            + [UNREAD] * len(after),
            out_specs=[
                pl.BlockSpec((2 * rank, size), lambda i, ids: (0, 0)),
                pl.BlockSpec((rank, size), lambda i, ids: (0, 0)),
            ] + [pl.BlockSpec((size, depth), lambda i, ids: (0, 0))] * lent,
        ),
        out_shape=[
            jax.ShapeDtypeStruct((2 * rank, size), BF16),
            jax.ShapeDtypeStruct((rank, size), BF16),
        ] + [jax.ShapeDtypeStruct((size, depth), BF16)] * lent,
        compiler_params=params(),
        cost_estimate=cost(
            2 * rank * depth * size * count, size * (depth * 2 * (count + 2 * lent) + rank * 6)),
        name="sketch",
    )(ids, x, *ws, *extra, *([x] * lent), *after)


def packing(rank):
    bands = rank // BAND
    pairs = [(i, j) for i in range(bands) for j in range(i, bands)]
    wide = 128 // BAND
    groups = -(-len(pairs) // wide)
    groups += groups % 2
    return pairs, wide, groups


def pack_gram(gram):
    pairs, wide, groups = packing(gram.shape[0])
    out = []
    for g in range(groups):
        chosen = pairs[g * wide:(g + 1) * wide]
        parts = [gram[i * BAND:(i + 1) * BAND, j * BAND:(j + 1) * BAND] for i, j in chosen]
        parts += [jnp.zeros((BAND, BAND), F32)] * (wide - len(chosen))
        out.append(jnp.concatenate(parts, axis=1))
    return jnp.concatenate(out, axis=0)


def fold_square(x, rank):
    return (x[:rank, :rank] + x[rank:, rank:]) + (x[:rank, rank:] + x[rank:, :rank])


def gram_kernel(scale, has_base, own_ref, got_ref, *refs):
    o_ref = refs[-1]
    rank = got_ref.shape[0]
    s = own_ref[:rank, :].astype(F32) + own_ref[rank:, :].astype(F32) + got_ref[...].astype(F32)
    high = s.astype(BF16)
    both = jnp.concatenate([high, (s - high.astype(F32)).astype(BF16)], axis=0)
    total = fold_square(dot(both, both, ((1,), (1,))), rank)
    if has_base:
        total = total + refs[0][...]
    o_ref[...] = total if scale is None else pack_gram(total * scale)


def own_gram(own, got, base, scale, after=()):
    rank, rows = got.shape
    bases = [] if base is None else [base]
    shape = (rank, rank) if scale is None else (packing(rank)[2] * BAND, 128)
    return pl.pallas_call(
        functools.partial(gram_kernel, scale, len(bases)),
        in_specs=[HELD] * (2 + len(bases)) + [UNREAD] * len(after),
        out_shape=jax.ShapeDtypeStruct(shape, F32),
        compiler_params=params(),
        cost_estimate=cost(8 * rank * rank * rows, 6 * rank * rows),
        name="gram",
    )(own, got, *bases, *after)


def wide_lanes(x, n):
    reps = -(-n // 128)
    return jnp.concatenate([x] * reps, axis=1)[:, :n] if reps > 1 else x[:, :n]


def band_rows(block, b):
    n = block.shape[1]
    count = BAND // 8
    part = [block[8 * i:8 * i + 8, :] for i in range(count)]
    sub = iota((8, n), 0)
    lane = iota((8, n), 1)
    for m in range(count):
        c0 = b * BAND + 8 * m
        live = count - m
        col = [
            [jnp.broadcast_to(part[m + i][:, c0 + k:c0 + k + 1], (8, 128)) for i in range(live)]
            for k in range(8)
        ]
        here = (lane >= c0) & (lane < c0 + 8)
        part[m] = jnp.where(here, jnp.where(lane - c0 == sub, 1.0, 0.0), part[m])
        for i in range(1, live):
            part[m + i] = jnp.where(here, 0.0, part[m + i])
        for j in range(8):
            inv_root = lax.rsqrt(jnp.broadcast_to(col[j][0][j:j + 1, :], (8, 128)))
            low = [x * inv_root for x in col[j]]
            for k in range(j + 1, 8):
                t = jnp.broadcast_to(low[0][k:k + 1, :], (8, 128))
                for i in range(live):
                    col[k][i] = col[k][i] - low[i] * t
            row = jnp.broadcast_to(part[m][j:j + 1, :], (8, n)) * wide_lanes(inv_root, n)
            for i in range(live):
                new = part[m + i] - wide_lanes(low[i], n) * row
                if i == 0:
                    new = jnp.where(sub > j, new, jnp.where(sub == j, row, part[m]))
                part[m + i] = new
    return jnp.concatenate(part, axis=0)


def factor_kernel(rank, g_ref, *refs):
    o_ref = refs[-1]
    pairs, wide, _ = packing(rank)
    o_ref[...] = jnp.zeros((rank, rank), F32)
    for at, (i, j) in enumerate(pairs):
        g, k = at // wide, at % wide
        o_ref[i * BAND:(i + 1) * BAND, j * BAND:(j + 1) * BAND] = g_ref[
            g * BAND:(g + 1) * BAND, k * BAND:(k + 1) * BAND]
    for b in range(rank // BAND):
        lo, hi = b * BAND, (b + 1) * BAND
        r = band_rows(o_ref[lo:hi, :], b)
        rows, cols = iota(r.shape, 0), iota(r.shape, 1)
        r = jnp.where((cols >= lo) & (cols < hi) & (cols - lo > rows), 0.0, r)
        o_ref[lo:hi, :] = jnp.where(cols < hi, r, 0.0)
        if hi < rank:
            left = jnp.where(cols >= hi, r, 0.0)
            update = dot(left, r, ((0,), (0,)), HI)
            kept = jnp.where(iota((rank - hi, rank), 1) // BAND == b, 0.0, o_ref[hi:, :])
            o_ref[hi:, :] = kept - update[hi:, :]


def factor_inverse(packed, rank, after=()):
    return pl.pallas_call(
        functools.partial(factor_kernel, rank),
        in_specs=[HELD] + [UNREAD] * len(after),
        out_shape=jax.ShapeDtypeStruct((rank, rank), F32),
        compiler_params=params(),
        cost_estimate=cost(FACTOR_COST, 4 * rank * rank),
        name="factor",
    )(packed, *after)


def project_kernel(count, wide, has_base, unread, finish, ids_ref, *refs):
    pair_refs, high_refs, x_refs = refs[:count], refs[count:2 * count], refs[2 * count:count * (2 + wide)]
    at = count * (2 + wide)
    rest = refs[at + has_base + unread:]
    t_ref = rest[-1]
    rank = t_ref.shape[1]

    @pl.when(pl.program_id(0) == 0)
    def _():
        t_ref[...] = refs[at][...] if has_base else jnp.zeros_like(t_ref)

    sums = []
    for pair_ref, high_ref in zip(pair_refs, high_refs):
        s = pair_ref[:rank, :].astype(F32) + pair_ref[rank:, :].astype(F32) + high_ref[...].astype(F32)
        high = s.astype(BF16)
        sums.append(jnp.concatenate([high, (s - high.astype(F32)).astype(BF16)], axis=0))
    for w in range(wide):
        total = None
        for k in range(count):
            term = dot(sums[k], x_refs[w * count + k][...], ((1,), (0,)))
            total = term if total is None else total + term
        t_ref[w] += total[:rank] + total[rank:]
    if finish is not None:
        @pl.when(pl.program_id(0) == pl.num_programs(0) - 1)
        def _():
            finish(t_ref, ids_ref, *rest[:-1])


def project(ids, work, x, base, after=(), finish=None, outs=(), scratch=()):
    count = len(work)
    wide = 1 + len(work[0][3])
    rank, span = work[0][1].shape
    depth = x.shape[1]
    rows = min(span, PROJECT_ROWS)
    steps = span // rows
    bases = [] if base is None else [base]
    whole = pl.BlockSpec((wide, rank, depth), lambda i, ids: (0, 0, 0))
    t_shape = jax.ShapeDtypeStruct((wide, rank, depth), F32)
    if finish is None:
        out_specs, out_shape, scratch_shapes = whole, t_shape, []
    else:
        out_specs = [pl.BlockSpec(o.shape, lambda i, ids: (0, 0)) for o in outs]
        out_shape = list(outs)
        scratch_shapes = list(scratch) + [pltpu.VMEM((wide, rank, depth), F32)]
    return pl.pallas_call(
        functools.partial(project_kernel, count, wide, len(bases), len(after), finish),
        grid_spec=pltpu.PrefetchScalarGridSpec(
            num_scalar_prefetch=1,
            grid=(steps,),
            in_specs=[pl.BlockSpec((2 * rank, rows), lambda i, ids: (0, i))] * count
            + [pl.BlockSpec((rank, rows), lambda i, ids: (0, i))] * count
            + [
                pl.BlockSpec((rows, depth), lambda i, ids, slot=w[2]: (ids[slot] * steps + i, 0))
                for w in work
            ]
            + [pl.BlockSpec((rows, depth), lambda i, ids: (i, 0))] * (count * (wide - 1))
            + [whole] * len(bases) + [UNREAD] * len(after),
            out_specs=out_specs,
            scratch_shapes=scratch_shapes,
        ),
        out_shape=out_shape,
        compiler_params=params(),
        cost_estimate=cost(
            4 * rank * depth * span * count * wide, span * count * (depth * wide + 3 * rank) * 2),
        name="project",
    )(
        ids, *[w[0] for w in work], *[w[1] for w in work], *([x] * count),
        *[w[3][d] for d in range(wide - 1) for w in work], *bases, *after)


def folding(rank, width):
    best = 1
    for f in range(1, rank + 1):
        if rank % f == 0 and (rank // f) % 8 == 0 and f * width <= 128:
            best = f
    return best


def reverse_bits(p, count):
    return sum(1 << (count - 1 - b) for b in range(count) if (p >> b) & 1)


def tail(pieces, samp, per_node, width_cols, t_ref, ids_ref, *refs):
    outs, hold = refs[:-1], refs[-1]
    wide, rank, depth = t_ref.shape
    width = per_node * width_cols
    fold = folding(rank, width)
    tall = rank // fold
    me_node = ids_ref[ids_ref.shape[0] - 1]
    dst = iota((depth, depth), 1)
    src = iota((depth, depth), 0)
    a, rest = dst // (samp * width), dst % (samp * width)
    s, rest = rest // width, rest % width
    want = (a * per_node + rest // width_cols) * (samp * width_cols) + s * width_cols + rest % width_cols
    move = jnp.where(src == want, 1.0, 0.0).astype(BF16)
    bits = pieces.bit_length() - 1
    for w in range(wide):
        t = t_ref[w]
        high = t.astype(BF16)
        mid = (t - high.astype(F32)).astype(BF16)
        low = (t - high.astype(F32) - mid.astype(F32)).astype(BF16)
        moved = dot(jnp.concatenate([high, mid, low], axis=0), move, ((1,), (0,)))
        moved = moved[:rank] + moved[rank:2 * rank] + moved[2 * rank:]
        for i in range(pieces):
            piece = moved[:, i * width:(i + 1) * width]
            parts = [piece[f * tall:(f + 1) * tall] for f in range(fold)]
            if fold * width < 128:
                parts.append(jnp.zeros((tall, 128 - fold * width), F32))
            hold[i] = jnp.concatenate(parts, axis=1)
        for p in range(pieces):
            outs[w][p * tall:(p + 1) * tall, :] = hold[me_node ^ reverse_bits(p, bits)]


def core_kernel(count, inv_ref, *refs):
    both, high = refs[:count], refs[count:2 * count]
    low_ref, core_ref = refs[-2:]
    rank = inv_ref.shape[0]
    at = 0
    for c in range(count):
        s = both[c][:rank, :].astype(F32) + both[c][rank:, :].astype(F32)
        rows = s.shape[1]
        s = s + (high[c][...].astype(F32) + low_ref[:, at:at + rows].astype(F32))
        core_ref[:, at:at + rows] = dot(inv_ref[...], s, ((1,), (0,)), HI)
        at += rows


def core_product(inverse, both, high, low):
    rank = inverse.shape[0]
    count = len(both)
    rows = sum(v.shape[1] for v in high)
    return pl.pallas_call(
        functools.partial(core_kernel, count),
        out_shape=jax.ShapeDtypeStruct((rank, rows), F32),
        compiler_params=params(),
        cost_estimate=cost(12 * rank * rank * rows, 12 * rank * rows),
        name="core",
    )(inverse, *both, *high, low)


def coefficient_kernel(scale, per_node, width_cols, inv_ref, piece_ref, o_ref):
    rank = inv_ref.shape[0]
    width = per_node * width_cols
    fold = folding(rank, width)
    total = piece_ref[...]
    total = jnp.concatenate([total[:, f * width:(f + 1) * width] for f in range(fold)], axis=0)
    out = dot(total, inv_ref[...], ((0,), (1,)), HI) * scale
    o_ref[...] = jnp.concatenate(
        [out[p * width_cols:(p + 1) * width_cols, :] for p in range(per_node)], axis=1)


def coefficients(inverse, piece, scale, per_node, width_cols):
    rank = inverse.shape[0]
    return pl.pallas_call(
        functools.partial(coefficient_kernel, scale, per_node, width_cols),
        out_shape=jax.ShapeDtypeStruct((width_cols, per_node * rank), F32),
        compiler_params=params(),
        cost_estimate=cost(12 * rank * rank * per_node * width_cols, 4 * rank * rank),
        name="coefficient",
    )(inverse, piece)


def swap(value, axis, size, bit):
    return lax.ppermute(value, axis, [(i, i ^ bit) for i in range(size)])


def body(snapshots, sketch_matrix):
    rows_all = snapshots.shape[0]
    rank = sketch_matrix.shape[1]
    samp = lax.axis_size("samp")
    node = lax.axis_size("node")
    total = rows_all * node
    quarter = rows_all // samp
    me_s = lax.axis_index("samp").astype(jnp.int32)
    me_n = lax.axis_index("node").astype(jnp.int32)
    w_t = sketch_matrix.T
    last = samp // 2
    near = range(1, last)
    starts, sizes = (0, UNIT), (UNIT, quarter - UNIT)
    blocks = [(last, 0), (last, 1), (0, 0), (0, 1)]

    def block_of(base, c):
        return (me_s ^ base) * (quarter // UNIT) + starts[c] // UNIT

    borrowed = {b: [] for b in blocks}
    ws, w_at = [w_t], 0

    def borrow(chosen, after, w=None):
        out = ()
        for d in near:
            out = lend(jnp.stack([block_of(b[0] ^ d, b[1]) for b in chosen]), snapshots, UNIT, w, after)
            for b, v in zip(chosen, out):
                borrowed[b].append(swap(v, "samp", samp, d))
            after = tuple(out[:1])
        return after

    done = borrow(blocks[:1], (), w_t)
    for v in borrowed[blocks[0]]:
        w_at = v.shape[0] - rank
        ws.append(v)
    borrow(blocks[1:2], done)

    pairs, highs, arrived, done = {}, {}, {}, ()

    def cross(b):
        arrived[b[0] ^ last, b[1]] = swap(highs[b], "samp", samp, last)

    ids = jnp.stack([block_of(*b) for b in blocks] + [me_n])
    slot = {b: k for k, b in enumerate(blocks)}
    for k, b in enumerate(blocks):
        later = blocks[k + 2:k + 3]
        numbers = [block_of(*b)] + [block_of(o[0] ^ d, o[1]) for o in later for d in near]
        out = sketch(jnp.stack(numbers), snapshots, ws, borrowed[b], UNIT, w_at, done)
        pairs[b], highs[b] = out[:2]
        done = (highs[b],)
        for o in later:
            borrowed[o] = [swap(v, "samp", samp, d) for d, v in zip(near, out[2:])]
        if b[0] == last:
            cross(b)
    own = [pairs[0, c] for c in range(2)]
    got_high = [arrived[0, c] for c in range(2)]

    def parts(chosen):
        return [(pairs[b], arrived[b], slot[b], borrowed[b]) for b in chosen]

    gram = own_gram(own[0], got_high[0], None, None)
    gram = own_gram(own[1], got_high[1], gram, 1.0 / total, done)
    gram = gram + swap(gram, "samp", samp, last)
    for b in blocks:
        if b[0] == 0:
            highs[b], _ = lax.optimization_barrier((highs[b], gram))
            cross(b)
    bit = last // 2
    while bit:
        gram = gram + swap(gram, "samp", samp, bit)
        bit //= 2
    begun = gram
    t = project(ids, parts([(0, 0), (0, 1)]), snapshots, None, (gram,) if PLACE[0] else ())
    rounds = node.bit_length() - 1
    for k in range(rounds):
        if k == rounds - PLACE[1]:
            gram, t = lax.optimization_barrier((gram, t))
        if k == rounds - 1:
            t = project(ids, parts([(last, 0)]), snapshots, t, (gram,))
            if PLACE[2]:
                gram, t = lax.optimization_barrier((gram, t))
        gram = gram + swap(gram, "node", node, 1 << k)
    late = [(last, 1)]

    per_node = P1 // node
    width_cols = P2 // samp
    tall = rank // folding(rank, per_node * width_cols)
    messages = project(
        ids, parts(late), snapshots, t, (),
        functools.partial(tail, node, samp, per_node, width_cols),
        [jax.ShapeDtypeStruct((node * tall, 128), F32)] * last,
        [pltpu.VMEM((node, tall, 128), F32)])

    low = jnp.concatenate([pairs[last, c][rank:] for c in range(2)], axis=1)
    low, _ = lax.optimization_barrier((low, begun))
    got_low = swap(low, "samp", samp, last)

    pieces = messages[0]
    for d in near:
        pieces = pieces + swap(messages[d], "samp", samp, d)
    inverse = factor_inverse(gram, rank, (pieces,))
    for k in range(rounds):
        if k == min(PLACE[3], rounds - 1):
            pieces, inverse = lax.optimization_barrier((pieces, inverse))
        if k == min(PLACE[4], rounds - 1):
            pieces, got_low = lax.optimization_barrier((pieces, got_low))
        edge = pieces.shape[0] // 2
        pieces = pieces[:edge] + swap(pieces[edge:], "node", node, 1 << k)
    spread = node // samp
    route = [
        (n * samp + s, (s * spread + n // samp) * samp + n % samp) for n in range(node) for s in range(samp)
    ]
    piece = lax.ppermute(pieces, ("node", "samp"), route)
    core = core_product(inverse, own, got_high, got_low)
    coef = coefficients(inverse, piece, 1.0 / total, per_node, width_cols)
    return (core.T, coef.T)


def solution(mesh):
    placed = (P("node", "samp"), P("samp", None))
    return jax.shard_map(
        body,
        mesh=mesh,
        in_specs=placed,
        out_specs=(P(("node", "samp"), None), P("node", "samp")),
        check_vma=False,
    )
```

```python
import functools
import jax
import jax.numpy as jnp
from jax import lax
from jax.experimental import pallas as pl
from jax.experimental.pallas import tpu as pltpu
from jax.sharding import PartitionSpec as P

P1 = 64
P2 = 32
BAND = 32
UNIT = 1024
LEND_PARTS = 4
PROJECT_ROWS = 512
SKETCH_STEPS = 1
FACTOR_COST = 6e9
COST_CUT = 1
F32 = jnp.float32
BF16 = jnp.bfloat16
HI = lax.Precision.HIGHEST
UNREAD = pl.BlockSpec(memory_space=pl.ANY)
HELD = pl.BlockSpec(memory_space=pltpu.VMEM)
VMEM_LIMIT = 48 * 1024 * 1024


def iota(shape, dim):
    return lax.broadcasted_iota(jnp.int32, shape, dim)


def dot(a, b, dims, precision=None):
    return lax.dot_general(a, b, (dims, ((), ())), precision=precision, preferred_element_type=F32)


def params():
    return pltpu.CompilerParams(vmem_limit_bytes=VMEM_LIMIT)


def cost(flops, moved):
    return pl.CostEstimate(flops=int(flops) // COST_CUT, bytes_accessed=int(moved) // COST_CUT, transcendentals=0)


def lend_kernel(size, stride, at, ids_ref, x_ref, *refs):
    count = ids_ref.shape[0]
    extra = 1 if at is not None else 0
    outs, sems = refs[-1 - count:-1], refs[-1]
    copies = []
    for k in range(count):
        first = pl.multiple_of(ids_ref[k] * size, size)
        for part in range(size // stride):
            copies.append(pltpu.make_async_copy(
                x_ref.at[pl.ds(first + part * stride, stride)],
                outs[k].at[pl.ds(part * stride, stride)],
                sems.at[len(copies)]))
    if extra:
        copies.append(pltpu.make_async_copy(
            refs[0], outs[0].at[pl.ds(at, refs[0].shape[0])], sems.at[len(copies)]))
    for copy in copies:
        copy.start()
    for copy in copies:
        copy.wait()


def lend(ids, x, size, w=None, after=()):
    count = ids.shape[0]
    depth = x.shape[1]
    stride = size // LEND_PARTS
    at, height = None, size
    if w is not None:
        rank = w.shape[0]
        at = -(-size // rank) * rank
        height = at + rank
    more = [] if w is None else [w]
    return pl.pallas_call(
        functools.partial(lend_kernel, size, stride, at),
        in_specs=[pl.BlockSpec(memory_space=pltpu.SMEM)] + [UNREAD] * (1 + len(more) + len(after)),
        out_specs=[HELD] * count,
        out_shape=[jax.ShapeDtypeStruct((height, depth), BF16)] * count,
        scratch_shapes=[pltpu.SemaphoreType.DMA((LEND_PARTS * count + len(more),))],
        compiler_params=params(),
        cost_estimate=cost(0, 4 * count * height * depth),
        name="lend",
    )(ids, x, *more, *after)


def sketch_kernel(count, lent, ids_ref, x_ref, *refs):
    w_refs, x_refs = refs[:count], (x_ref,) + refs[count:2 * count - 1]
    both_ref, high_ref = refs[len(refs) - lent - 2:len(refs) - lent]
    rank = high_ref.shape[0]
    for k in range(lent):
        refs[len(refs) - lent + k][...] = refs[2 * count - 1 + k][...]
    s = None
    for w_ref, ref in zip(w_refs, x_refs):
        term = dot(w_ref[...], ref[...], ((1,), (1,)))
        s = term if s is None else s + term
    high = s.astype(BF16)
    high_ref[...] = high
    both_ref[:rank, :] = high
    both_ref[rank:, :] = (s - high.astype(F32)).astype(BF16)


def sketch(ids, x, ws, extra, size, w_at, after=()):
    rank, depth = ws[0].shape
    count = len(ws)
    lent = ids.shape[0] - 1
    steps = SKETCH_STEPS
    rows = size // steps
    return pl.pallas_call(
        functools.partial(sketch_kernel, count, lent),
        grid_spec=pltpu.PrefetchScalarGridSpec(
            num_scalar_prefetch=1,
            grid=(steps,),
            in_specs=[pl.BlockSpec((rows, depth), lambda i, ids: (ids[0] * steps + i, 0))]
            + [pl.BlockSpec((rank, depth), lambda i, ids: (0, 0))]
            + [pl.BlockSpec((rank, depth), lambda i, ids: (w_at // rank, 0))] * (count - 1)
            + [pl.BlockSpec((rows, depth), lambda i, ids: (i, 0))] * (count - 1)
            + [pl.BlockSpec((rows, depth), lambda i, ids, k=k: (ids[1 + k] * steps + i, 0)) for k in range(lent)]
            + [UNREAD] * len(after),
            out_specs=[
                pl.BlockSpec((2 * rank, rows), lambda i, ids: (0, i)),
                pl.BlockSpec((rank, rows), lambda i, ids: (0, i)),
            ] + [pl.BlockSpec((rows, depth), lambda i, ids: (i, 0))] * lent,
        ),
        out_shape=[
            jax.ShapeDtypeStruct((2 * rank, size), BF16),
            jax.ShapeDtypeStruct((rank, size), BF16),
        ] + [jax.ShapeDtypeStruct((size, depth), BF16)] * lent,
        compiler_params=params(),
        cost_estimate=cost(
            2 * rank * depth * size * count, size * (depth * 2 * (count + 2 * lent) + rank * 6)),
        name="sketch",
    )(ids, x, *ws, *extra, *([x] * lent), *after)


def packing(rank):
    bands = rank // BAND
    pairs = [(i, j) for i in range(bands) for j in range(i, bands)]
    wide = 128 // BAND
    groups = -(-len(pairs) // wide)
    groups += groups % 2
    return pairs, wide, groups


def pack_gram(gram):
    pairs, wide, groups = packing(gram.shape[0])
    out = []
    for g in range(groups):
        chosen = pairs[g * wide:(g + 1) * wide]
        parts = [gram[i * BAND:(i + 1) * BAND, j * BAND:(j + 1) * BAND] for i, j in chosen]
        parts += [jnp.zeros((BAND, BAND), F32)] * (wide - len(chosen))
        out.append(jnp.concatenate(parts, axis=1))
    return jnp.concatenate(out, axis=0)


def fold_square(x, rank):
    return (x[:rank, :rank] + x[rank:, rank:]) + (x[:rank, rank:] + x[rank:, :rank])


def gram_kernel(scale, has_base, own_ref, got_ref, *refs):
    o_ref = refs[-1]
    rank = got_ref.shape[0]
    s = own_ref[:rank, :].astype(F32) + own_ref[rank:, :].astype(F32) + got_ref[...].astype(F32)
    high = s.astype(BF16)
    both = jnp.concatenate([high, (s - high.astype(F32)).astype(BF16)], axis=0)
    total = fold_square(dot(both, both, ((1,), (1,))), rank)
    if has_base:
        total = total + refs[0][...]
    o_ref[...] = total if scale is None else pack_gram(total * scale)


def own_gram(own, got, base, scale, after=()):
    rank, rows = got.shape
    bases = [] if base is None else [base]
    shape = (rank, rank) if scale is None else (packing(rank)[2] * BAND, 128)
    return pl.pallas_call(
        functools.partial(gram_kernel, scale, len(bases)),
        in_specs=[HELD] * (2 + len(bases)) + [UNREAD] * len(after),
        out_shape=jax.ShapeDtypeStruct(shape, F32),
        compiler_params=params(),
        cost_estimate=cost(8 * rank * rank * rows, 6 * rank * rows),
        name="gram",
    )(own, got, *bases, *after)


def wide_lanes(x, n):
    reps = -(-n // 128)
    return jnp.concatenate([x] * reps, axis=1)[:, :n] if reps > 1 else x[:, :n]


def band_rows(block, b):
    n = block.shape[1]
    count = BAND // 8
    part = [block[8 * i:8 * i + 8, :] for i in range(count)]
    sub = iota((8, n), 0)
    lane = iota((8, n), 1)
    for m in range(count):
        c0 = b * BAND + 8 * m
        live = count - m
        col = [
            [jnp.broadcast_to(part[m + i][:, c0 + k:c0 + k + 1], (8, 128)) for i in range(live)]
            for k in range(8)
        ]
        here = (lane >= c0) & (lane < c0 + 8)
        part[m] = jnp.where(here, jnp.where(lane - c0 == sub, 1.0, 0.0), part[m])
        for i in range(1, live):
            part[m + i] = jnp.where(here, 0.0, part[m + i])
        for j in range(8):
            inv_root = lax.rsqrt(jnp.broadcast_to(col[j][0][j:j + 1, :], (8, 128)))
            low = [x * inv_root for x in col[j]]
            for k in range(j + 1, 8):
                t = jnp.broadcast_to(low[0][k:k + 1, :], (8, 128))
                for i in range(live):
                    col[k][i] = col[k][i] - low[i] * t
            row = jnp.broadcast_to(part[m][j:j + 1, :], (8, n)) * wide_lanes(inv_root, n)
            for i in range(live):
                new = part[m + i] - wide_lanes(low[i], n) * row
                if i == 0:
                    new = jnp.where(sub > j, new, jnp.where(sub == j, row, part[m]))
                part[m + i] = new
    return jnp.concatenate(part, axis=0)


def factor_kernel(rank, g_ref, *refs):
    o_ref = refs[-1]
    pairs, wide, _ = packing(rank)
    o_ref[...] = jnp.zeros((rank, rank), F32)
    for at, (i, j) in enumerate(pairs):
        g, k = at // wide, at % wide
        o_ref[i * BAND:(i + 1) * BAND, j * BAND:(j + 1) * BAND] = g_ref[
            g * BAND:(g + 1) * BAND, k * BAND:(k + 1) * BAND]
    for b in range(rank // BAND):
        lo, hi = b * BAND, (b + 1) * BAND
        r = band_rows(o_ref[lo:hi, :], b)
        rows, cols = iota(r.shape, 0), iota(r.shape, 1)
        r = jnp.where((cols >= lo) & (cols < hi) & (cols - lo > rows), 0.0, r)
        o_ref[lo:hi, :] = jnp.where(cols < hi, r, 0.0)
        if hi < rank:
            left = jnp.where(cols >= hi, r, 0.0)
            update = dot(left, r, ((0,), (0,)), HI)
            kept = jnp.where(iota((rank - hi, rank), 1) // BAND == b, 0.0, o_ref[hi:, :])
            o_ref[hi:, :] = kept - update[hi:, :]


def factor_inverse(packed, rank, after=()):
    return pl.pallas_call(
        functools.partial(factor_kernel, rank),
        in_specs=[HELD] + [UNREAD] * len(after),
        out_shape=jax.ShapeDtypeStruct((rank, rank), F32),
        compiler_params=params(),
        cost_estimate=cost(FACTOR_COST, 4 * rank * rank),
        name="factor",
    )(packed, *after)


def project_kernel(count, wide, has_base, aside, finish, ids_ref, *refs):
    pair_refs, high_refs, x_refs = refs[:count], refs[count:2 * count], refs[2 * count:count * (2 + wide)]
    at = count * (2 + wide)
    beside = refs[at + has_base:at + has_base + aside]
    rest = refs[at + has_base + aside:]
    t_ref = rest[-1]
    rank = t_ref.shape[1]

    @pl.when(pl.program_id(0) == 0)
    def _():
        t_ref[...] = refs[at][...] if has_base else jnp.zeros_like(t_ref)

    sums = []
    for pair_ref, high_ref in zip(pair_refs, high_refs):
        s = pair_ref[:rank, :].astype(F32) + pair_ref[rank:, :].astype(F32) + high_ref[...].astype(F32)
        high = s.astype(BF16)
        sums.append(jnp.concatenate([high, (s - high.astype(F32)).astype(BF16)], axis=0))
    for w in range(wide):
        total = None
        for k in range(count):
            term = dot(sums[k], x_refs[w * count + k][...], ((1,), (0,)))
            total = term if total is None else total + term
        t_ref[w] += total[:rank] + total[rank:]
    if finish is not None:
        @pl.when(pl.program_id(0) == pl.num_programs(0) - 1)
        def _():
            finish(t_ref, ids_ref, beside, *rest[:-1])


def project(ids, work, x, base, beside=(), finish=None, outs=(), scratch=()):
    count = len(work)
    wide = 1 + len(work[0][3])
    rank, span = work[0][1].shape
    depth = x.shape[1]
    rows = min(span, PROJECT_ROWS)
    steps = span // rows
    bases = [] if base is None else [base]
    whole = pl.BlockSpec((wide, rank, depth), lambda i, ids: (0, 0, 0))
    t_shape = jax.ShapeDtypeStruct((wide, rank, depth), F32)
    if finish is None:
        out_specs, out_shape, scratch_shapes = whole, t_shape, []
    else:
        out_specs = [pl.BlockSpec(o.shape, lambda i, ids: (0, 0)) for o in outs]
        out_shape = list(outs)
        scratch_shapes = list(scratch) + [pltpu.VMEM((wide, rank, depth), F32)]
    return pl.pallas_call(
        functools.partial(project_kernel, count, wide, len(bases), len(beside), finish),
        grid_spec=pltpu.PrefetchScalarGridSpec(
            num_scalar_prefetch=1,
            grid=(steps,),
            in_specs=[pl.BlockSpec((2 * rank, rows), lambda i, ids: (0, i))] * count
            + [pl.BlockSpec((rank, rows), lambda i, ids: (0, i))] * count
            + [
                pl.BlockSpec((rows, depth), lambda i, ids, slot=w[2]: (ids[slot] * steps + i, 0))
                for w in work
            ]
            + [pl.BlockSpec((rows, depth), lambda i, ids: (i, 0))] * (count * (wide - 1))
            + [whole] * len(bases) + [pl.BlockSpec(v.shape, lambda i, ids: (0, 0)) for v in beside],
            out_specs=out_specs,
            scratch_shapes=scratch_shapes,
        ),
        out_shape=out_shape,
        compiler_params=params(),
        cost_estimate=cost(
            4 * rank * depth * span * count * wide, span * count * (depth * wide + 3 * rank) * 2),
        name="project",
    )(
        ids, *[w[0] for w in work], *[w[1] for w in work], *([x] * count),
        *[w[3][d] for d in range(wide - 1) for w in work], *bases, *beside)


def folding(rank, width):
    best = 1
    for f in range(1, rank + 1):
        if rank % f == 0 and (rank // f) % 8 == 0 and f * width <= 128:
            best = f
    return best


def reverse_bits(p, count):
    return sum(1 << (count - 1 - b) for b in range(count) if (p >> b) & 1)


def tail(pieces, samp, per_node, width_cols, t_ref, ids_ref, beside, *refs):
    outs, hold = refs[:-1], refs[-1]
    wide, rank, depth = t_ref.shape
    width = per_node * width_cols
    fold = folding(rank, width)
    tall = rank // fold
    me_node = ids_ref[ids_ref.shape[0] - 1]
    gram_ref = beside[0]
    for out in outs[:2]:
        out[pieces * tall:, :] = gram_ref[...]
    for out in outs[2:]:
        out[pieces * tall:, :] = jnp.zeros(gram_ref.shape, F32)
    dst = iota((depth, depth), 1)
    src = iota((depth, depth), 0)
    a, rest = dst // (samp * width), dst % (samp * width)
    s, rest = rest // width, rest % width
    want = (a * per_node + rest // width_cols) * (samp * width_cols) + s * width_cols + rest % width_cols
    move = jnp.where(src == want, 1.0, 0.0).astype(BF16)
    bits = pieces.bit_length() - 1
    for w in range(wide):
        t = t_ref[w]
        high = t.astype(BF16)
        mid = (t - high.astype(F32)).astype(BF16)
        low = (t - high.astype(F32) - mid.astype(F32)).astype(BF16)
        moved = dot(jnp.concatenate([high, mid, low], axis=0), move, ((1,), (0,)))
        moved = moved[:rank] + moved[rank:2 * rank] + moved[2 * rank:]
        for i in range(pieces):
            piece = moved[:, i * width:(i + 1) * width]
            parts = [piece[f * tall:(f + 1) * tall] for f in range(fold)]
            if fold * width < 128:
                parts.append(jnp.zeros((tall, 128 - fold * width), F32))
            hold[i] = jnp.concatenate(parts, axis=1)
        for p in range(pieces):
            outs[w][p * tall:(p + 1) * tall, :] = hold[me_node ^ reverse_bits(p, bits)]


def finish_kernel(scale, per_node, width_cols, count, inv_ref, piece_ref, *refs):
    both, high = refs[:count], refs[count:2 * count]
    low_ref, core_ref, coef_ref = refs[-3:]
    rank = inv_ref.shape[0]
    inverse = inv_ref[...]
    at = 0
    for c in range(count):
        s = both[c][:rank, :].astype(F32) + both[c][rank:, :].astype(F32)
        rows = s.shape[1]
        s = s + (high[c][...].astype(F32) + low_ref[:, at:at + rows].astype(F32))
        core_ref[:, at:at + rows] = dot(inverse, s, ((1,), (0,)), HI)
        at += rows
    width = per_node * width_cols
    fold = folding(rank, width)
    total = piece_ref[...]
    total = jnp.concatenate([total[:, f * width:(f + 1) * width] for f in range(fold)], axis=0)
    out = dot(total, inverse, ((0,), (1,)), HI) * scale
    coef_ref[...] = jnp.concatenate(
        [out[p * width_cols:(p + 1) * width_cols, :] for p in range(per_node)], axis=1)


def finish(inverse, piece, both, high, low, scale, per_node, width_cols):
    rank = inverse.shape[0]
    count = len(both)
    rows = sum(v.shape[1] for v in high)
    return pl.pallas_call(
        functools.partial(finish_kernel, scale, per_node, width_cols, count),
        out_shape=(
            jax.ShapeDtypeStruct((rank, rows), F32),
            jax.ShapeDtypeStruct((width_cols, per_node * rank), F32),
        ),
        compiler_params=params(),
        cost_estimate=cost(12 * rank * rank * rows, 12 * rank * rows),
        name="finish",
    )(inverse, piece, *both, *high, low)


def swap(value, axis, size, bit):
    return lax.ppermute(value, axis, [(i, i ^ bit) for i in range(size)])


def body(snapshots, sketch_matrix):
    rows_all = snapshots.shape[0]
    rank = sketch_matrix.shape[1]
    samp = lax.axis_size("samp")
    node = lax.axis_size("node")
    total = rows_all * node
    quarter = rows_all // samp
    me_s = lax.axis_index("samp").astype(jnp.int32)
    me_n = lax.axis_index("node").astype(jnp.int32)
    w_t = sketch_matrix.T
    last = samp // 2
    near = range(1, last)
    starts, sizes = (0, UNIT), (UNIT, quarter - UNIT)
    blocks = [(last, 0), (last, 1), (0, 0), (0, 1)]

    def block_of(base, c):
        return (me_s ^ base) * (quarter // UNIT) + starts[c] // UNIT

    borrowed = {b: [] for b in blocks}
    ws, w_at = [w_t], 0

    def borrow(chosen, after, w=None):
        out = ()
        for d in near:
            out = lend(jnp.stack([block_of(b[0] ^ d, b[1]) for b in chosen]), snapshots, UNIT, w, after)
            for b, v in zip(chosen, out):
                borrowed[b].append(swap(v, "samp", samp, d))
            after = tuple(out[:1])
        return after

    done = borrow(blocks[:1], (), w_t)
    for v in borrowed[blocks[0]]:
        w_at = v.shape[0] - rank
        ws.append(v)
    borrow(blocks[1:], done)

    pairs, arrived, done = {}, {}, ()
    ids = jnp.stack([block_of(*b) for b in blocks] + [me_n])
    slot = {b: k for k, b in enumerate(blocks)}
    for k, b in enumerate(blocks):
        later = ()
        numbers = [block_of(*b)] + [block_of(o[0] ^ d, o[1]) for o in later for d in near]
        out = sketch(jnp.stack(numbers), snapshots, ws, borrowed[b], UNIT, w_at, done)
        pairs[b], high = out[:2]
        done = (high,)
        arrived[b[0] ^ last, b[1]] = swap(high, "samp", samp, last)
        for o in later:
            borrowed[o] = [swap(v, "samp", samp, d) for d, v in zip(near, out[2:])]
    own = [pairs[0, c] for c in range(2)]
    got_high = [arrived[0, c] for c in range(2)]

    def parts(chosen):
        return [(pairs[b], arrived[b], slot[b], borrowed[b]) for b in chosen]

    gram = own_gram(own[0], got_high[0], None, None)
    gram = own_gram(own[1], got_high[1], gram, 1.0 / total, done)
    gram = gram + swap(gram, "samp", samp, last)

    t = project(ids, parts([(0, 0), (0, 1)]), snapshots, None)
    t = project(ids, parts([(last, 0)]), snapshots, t)
    late = [(last, 1)]
    per_node = P1 // node
    width_cols = P2 // samp
    tall = rank // folding(rank, per_node * width_cols)
    messages = project(
        ids, parts(late), snapshots, t, [gram],
        functools.partial(tail, node, samp, per_node, width_cols),
        [jax.ShapeDtypeStruct((node * tall + gram.shape[0], 128), F32)] * last,
        [pltpu.VMEM((node, tall, 128), F32)])

    low = jnp.concatenate([pairs[last, c][rank:] for c in range(2)], axis=1)
    low, _ = lax.optimization_barrier((low, gram))
    got_low = swap(low, "samp", samp, last)

    held = messages[0]
    for d in near:
        held = held + swap(messages[d], "samp", samp, d)
    edge = node * tall
    pieces, gram = held[:edge], held[edge:]
    rounds = node.bit_length() - 1
    for k in range(rounds):
        if k == rounds - 1:
            pieces, got_low = lax.optimization_barrier((pieces, got_low))
        edge //= 2
        got = swap(jnp.concatenate([pieces[edge:], gram], axis=0), "node", node, 1 << k)
        pieces, gram = pieces[:edge] + got[:edge], gram + got[edge:]
    spread = node // samp
    route = [
        (n * samp + s, (s * spread + n // samp) * samp + n % samp) for n in range(node) for s in range(samp)
    ]
    piece = lax.ppermute(pieces, ("node", "samp"), route)
    inverse = factor_inverse(gram, rank)
    core, coef = finish(inverse, piece, own, got_high, got_low, 1.0 / total, per_node, width_cols)
    return (core.T, coef.T)


def solution(mesh):
    placed = (P("node", "samp"), P("samp", None))
    return jax.shard_map(
        body,
        mesh=mesh,
        in_specs=placed,
        out_specs=(P(("node", "samp"), None), P("node", "samp")),
        check_vma=False,
    )
```

```python
import functools
import jax
import jax.numpy as jnp
from jax import lax
from jax.experimental import pallas as pl
from jax.experimental.pallas import tpu as pltpu
from jax.sharding import PartitionSpec as P

P1 = 64
P2 = 32
BAND = 32
UNIT = 1024
LEND_PARTS = 4
PROJECT_ROWS = 512
PLACE = (1, True, 1, 1, -1)
SKETCH_STEPS = 1
FACTOR_COST = 6e9
COST_CUT = 1
F32 = jnp.float32
BF16 = jnp.bfloat16
HI = lax.Precision.HIGHEST
UNREAD = pl.BlockSpec(memory_space=pl.ANY)
HELD = pl.BlockSpec(memory_space=pltpu.VMEM)
VMEM_LIMIT = 48 * 1024 * 1024


def iota(shape, dim):
    return lax.broadcasted_iota(jnp.int32, shape, dim)


def dot(a, b, dims, precision=None):
    return lax.dot_general(a, b, (dims, ((), ())), precision=precision, preferred_element_type=F32)


def params():
    return pltpu.CompilerParams(vmem_limit_bytes=VMEM_LIMIT)


def cost(flops, moved):
    return pl.CostEstimate(flops=int(flops) // COST_CUT, bytes_accessed=int(moved) // COST_CUT, transcendentals=0)


def lend_kernel(size, stride, at, ids_ref, x_ref, *refs):
    count = ids_ref.shape[0]
    extra = 1 if at is not None else 0
    outs, sems = refs[-1 - count:-1], refs[-1]
    copies = []
    for k in range(count):
        first = pl.multiple_of(ids_ref[k] * size, size)
        for part in range(size // stride):
            copies.append(pltpu.make_async_copy(
                x_ref.at[pl.ds(first + part * stride, stride)],
                outs[k].at[pl.ds(part * stride, stride)],
                sems.at[len(copies)]))
    if extra:
        copies.append(pltpu.make_async_copy(
            refs[0], outs[0].at[pl.ds(at, refs[0].shape[0])], sems.at[len(copies)]))
    for copy in copies:
        copy.start()
    for copy in copies:
        copy.wait()


def lend(ids, x, size, w=None, after=()):
    count = ids.shape[0]
    depth = x.shape[1]
    stride = size // LEND_PARTS
    at, height = None, size
    if w is not None:
        rank = w.shape[0]
        at = -(-size // rank) * rank
        height = at + rank
    more = [] if w is None else [w]
    return pl.pallas_call(
        functools.partial(lend_kernel, size, stride, at),
        in_specs=[pl.BlockSpec(memory_space=pltpu.SMEM)] + [UNREAD] * (1 + len(more) + len(after)),
        out_specs=[HELD] * count,
        out_shape=[jax.ShapeDtypeStruct((height, depth), BF16)] * count,
        scratch_shapes=[pltpu.SemaphoreType.DMA((LEND_PARTS * count + len(more),))],
        compiler_params=params(),
        cost_estimate=cost(0, 4 * count * height * depth),
        name="lend",
    )(ids, x, *more, *after)


def sketch_kernel(count, lent, ids_ref, x_ref, *refs):
    w_refs, x_refs = refs[:count], (x_ref,) + refs[count:2 * count - 1]
    both_ref, high_ref = refs[len(refs) - lent - 2:len(refs) - lent]
    rank = high_ref.shape[0]
    for k in range(lent):
        refs[len(refs) - lent + k][...] = refs[2 * count - 1 + k][...]
    s = None
    for w_ref, ref in zip(w_refs, x_refs):
        term = dot(w_ref[...], ref[...], ((1,), (1,)))
        s = term if s is None else s + term
    high = s.astype(BF16)
    high_ref[...] = high
    both_ref[:rank, :] = high
    both_ref[rank:, :] = (s - high.astype(F32)).astype(BF16)


def sketch(ids, x, ws, extra, size, w_at, after=()):
    rank, depth = ws[0].shape
    count = len(ws)
    lent = ids.shape[0] - 1
    steps = SKETCH_STEPS
    rows = size // steps
    return pl.pallas_call(
        functools.partial(sketch_kernel, count, lent),
        grid_spec=pltpu.PrefetchScalarGridSpec(
            num_scalar_prefetch=1,
            grid=(steps,),
            in_specs=[pl.BlockSpec((rows, depth), lambda i, ids: (ids[0] * steps + i, 0))]
            + [pl.BlockSpec((rank, depth), lambda i, ids: (0, 0))]
            + [pl.BlockSpec((rank, depth), lambda i, ids: (w_at // rank, 0))] * (count - 1)
            + [pl.BlockSpec((rows, depth), lambda i, ids: (i, 0))] * (count - 1)
            + [pl.BlockSpec((rows, depth), lambda i, ids, k=k: (ids[1 + k] * steps + i, 0)) for k in range(lent)]
            + [UNREAD] * len(after),
            out_specs=[
                pl.BlockSpec((2 * rank, rows), lambda i, ids: (0, i)),
                pl.BlockSpec((rank, rows), lambda i, ids: (0, i)),
            ] + [pl.BlockSpec((rows, depth), lambda i, ids: (i, 0))] * lent,
        ),
        out_shape=[
            jax.ShapeDtypeStruct((2 * rank, size), BF16),
            jax.ShapeDtypeStruct((rank, size), BF16),
        ] + [jax.ShapeDtypeStruct((size, depth), BF16)] * lent,
        compiler_params=params(),
        cost_estimate=cost(
            2 * rank * depth * size * count, size * (depth * 2 * (count + 2 * lent) + rank * 6)),
        name="sketch",
    )(ids, x, *ws, *extra, *([x] * lent), *after)


def packing(rank):
    bands = rank // BAND
    pairs = [(i, j) for i in range(bands) for j in range(i, bands)]
    wide = 128 // BAND
    groups = -(-len(pairs) // wide)
    groups += groups % 2
    return pairs, wide, groups


def pack_gram(gram):
    pairs, wide, groups = packing(gram.shape[0])
    out = []
    for g in range(groups):
        chosen = pairs[g * wide:(g + 1) * wide]
        parts = [gram[i * BAND:(i + 1) * BAND, j * BAND:(j + 1) * BAND] for i, j in chosen]
        parts += [jnp.zeros((BAND, BAND), F32)] * (wide - len(chosen))
        out.append(jnp.concatenate(parts, axis=1))
    return jnp.concatenate(out, axis=0)


def fold_square(x, rank):
    return (x[:rank, :rank] + x[rank:, rank:]) + (x[:rank, rank:] + x[rank:, :rank])


def gram_kernel(scale, has_base, own_ref, got_ref, *refs):
    o_ref = refs[-1]
    rank = got_ref.shape[0]
    s = own_ref[:rank, :].astype(F32) + own_ref[rank:, :].astype(F32) + got_ref[...].astype(F32)
    high = s.astype(BF16)
    both = jnp.concatenate([high, (s - high.astype(F32)).astype(BF16)], axis=0)
    total = fold_square(dot(both, both, ((1,), (1,))), rank)
    if has_base:
        total = total + refs[0][...]
    o_ref[...] = total if scale is None else pack_gram(total * scale)


def own_gram(own, got, base, scale, after=()):
    rank, rows = got.shape
    bases = [] if base is None else [base]
    shape = (rank, rank) if scale is None else (packing(rank)[2] * BAND, 128)
    return pl.pallas_call(
        functools.partial(gram_kernel, scale, len(bases)),
        in_specs=[HELD] * (2 + len(bases)) + [UNREAD] * len(after),
        out_shape=jax.ShapeDtypeStruct(shape, F32),
        compiler_params=params(),
        cost_estimate=cost(8 * rank * rank * rows, 6 * rank * rows),
        name="gram",
    )(own, got, *bases, *after)


def wide_lanes(x, n):
    reps = -(-n // 128)
    return jnp.concatenate([x] * reps, axis=1)[:, :n] if reps > 1 else x[:, :n]


def band_rows(block, b):
    n = block.shape[1]
    count = BAND // 8
    part = [block[8 * i:8 * i + 8, :] for i in range(count)]
    sub = iota((8, n), 0)
    lane = iota((8, n), 1)
    for m in range(count):
        c0 = b * BAND + 8 * m
        live = count - m
        col = [
            [jnp.broadcast_to(part[m + i][:, c0 + k:c0 + k + 1], (8, 128)) for i in range(live)]
            for k in range(8)
        ]
        here = (lane >= c0) & (lane < c0 + 8)
        part[m] = jnp.where(here, jnp.where(lane - c0 == sub, 1.0, 0.0), part[m])
        for i in range(1, live):
            part[m + i] = jnp.where(here, 0.0, part[m + i])
        for j in range(8):
            inv_root = lax.rsqrt(jnp.broadcast_to(col[j][0][j:j + 1, :], (8, 128)))
            low = [x * inv_root for x in col[j]]
            for k in range(j + 1, 8):
                t = jnp.broadcast_to(low[0][k:k + 1, :], (8, 128))
                for i in range(live):
                    col[k][i] = col[k][i] - low[i] * t
            row = jnp.broadcast_to(part[m][j:j + 1, :], (8, n)) * wide_lanes(inv_root, n)
            for i in range(live):
                new = part[m + i] - wide_lanes(low[i], n) * row
                if i == 0:
                    new = jnp.where(sub > j, new, jnp.where(sub == j, row, part[m]))
                part[m + i] = new
    return jnp.concatenate(part, axis=0)


def factor_kernel(rank, g_ref, *refs):
    o_ref = refs[-1]
    pairs, wide, _ = packing(rank)
    o_ref[...] = jnp.zeros((rank, rank), F32)
    for at, (i, j) in enumerate(pairs):
        g, k = at // wide, at % wide
        o_ref[i * BAND:(i + 1) * BAND, j * BAND:(j + 1) * BAND] = g_ref[
            g * BAND:(g + 1) * BAND, k * BAND:(k + 1) * BAND]
    for b in range(rank // BAND):
        lo, hi = b * BAND, (b + 1) * BAND
        r = band_rows(o_ref[lo:hi, :], b)
        rows, cols = iota(r.shape, 0), iota(r.shape, 1)
        r = jnp.where((cols >= lo) & (cols < hi) & (cols - lo > rows), 0.0, r)
        o_ref[lo:hi, :] = jnp.where(cols < hi, r, 0.0)
        if hi < rank:
            left = jnp.where(cols >= hi, r, 0.0)
            update = dot(left, r, ((0,), (0,)), HI)
            kept = jnp.where(iota((rank - hi, rank), 1) // BAND == b, 0.0, o_ref[hi:, :])
            o_ref[hi:, :] = kept - update[hi:, :]


def factor_inverse(packed, rank, after=()):
    return pl.pallas_call(
        functools.partial(factor_kernel, rank),
        in_specs=[HELD] + [UNREAD] * len(after),
        out_shape=jax.ShapeDtypeStruct((rank, rank), F32),
        compiler_params=params(),
        cost_estimate=cost(FACTOR_COST, 4 * rank * rank),
        name="factor",
    )(packed, *after)


def project_kernel(count, wide, has_base, aside, finish, ids_ref, *refs):
    pair_refs, high_refs, x_refs = refs[:count], refs[count:2 * count], refs[2 * count:count * (2 + wide)]
    at = count * (2 + wide)
    beside = refs[at + has_base:at + has_base + aside]
    rest = refs[at + has_base + aside:]
    t_ref = rest[-1]
    rank = t_ref.shape[1]

    @pl.when(pl.program_id(0) == 0)
    def _():
        t_ref[...] = refs[at][...] if has_base else jnp.zeros_like(t_ref)

    sums = []
    for pair_ref, high_ref in zip(pair_refs, high_refs):
        s = pair_ref[:rank, :].astype(F32) + pair_ref[rank:, :].astype(F32) + high_ref[...].astype(F32)
        high = s.astype(BF16)
        sums.append(jnp.concatenate([high, (s - high.astype(F32)).astype(BF16)], axis=0))
    for w in range(wide):
        total = None
        for k in range(count):
            term = dot(sums[k], x_refs[w * count + k][...], ((1,), (0,)))
            total = term if total is None else total + term
        t_ref[w] += total[:rank] + total[rank:]
    if finish is not None:
        @pl.when(pl.program_id(0) == pl.num_programs(0) - 1)
        def _():
            finish(t_ref, ids_ref, beside, *rest[:-1])


def project(ids, work, x, base, beside=(), finish=None, outs=(), scratch=()):
    count = len(work)
    wide = 1 + len(work[0][3])
    rank, span = work[0][1].shape
    depth = x.shape[1]
    rows = min(span, PROJECT_ROWS)
    steps = span // rows
    bases = [] if base is None else [base]
    whole = pl.BlockSpec((wide, rank, depth), lambda i, ids: (0, 0, 0))
    t_shape = jax.ShapeDtypeStruct((wide, rank, depth), F32)
    if finish is None:
        out_specs, out_shape, scratch_shapes = whole, t_shape, []
    else:
        out_specs = [pl.BlockSpec(o.shape, lambda i, ids: (0, 0)) for o in outs]
        out_shape = list(outs)
        scratch_shapes = list(scratch) + [pltpu.VMEM((wide, rank, depth), F32)]
    return pl.pallas_call(
        functools.partial(project_kernel, count, wide, len(bases), len(beside), finish),
        grid_spec=pltpu.PrefetchScalarGridSpec(
            num_scalar_prefetch=1,
            grid=(steps,),
            in_specs=[pl.BlockSpec((2 * rank, rows), lambda i, ids: (0, i))] * count
            + [pl.BlockSpec((rank, rows), lambda i, ids: (0, i))] * count
            + [
                pl.BlockSpec((rows, depth), lambda i, ids, slot=w[2]: (ids[slot] * steps + i, 0))
                for w in work
            ]
            + [pl.BlockSpec((rows, depth), lambda i, ids: (i, 0))] * (count * (wide - 1))
            + [whole] * len(bases) + [pl.BlockSpec(v.shape, lambda i, ids: (0, 0)) for v in beside],
            out_specs=out_specs,
            scratch_shapes=scratch_shapes,
        ),
        out_shape=out_shape,
        compiler_params=params(),
        cost_estimate=cost(
            4 * rank * depth * span * count * wide, span * count * (depth * wide + 3 * rank) * 2),
        name="project",
    )(
        ids, *[w[0] for w in work], *[w[1] for w in work], *([x] * count),
        *[w[3][d] for d in range(wide - 1) for w in work], *bases, *beside)


def folding(rank, width):
    best = 1
    for f in range(1, rank + 1):
        if rank % f == 0 and (rank // f) % 8 == 0 and f * width <= 128:
            best = f
    return best


def reverse_bits(p, count):
    return sum(1 << (count - 1 - b) for b in range(count) if (p >> b) & 1)


def tail(pieces, samp, per_node, width_cols, t_ref, ids_ref, beside, *refs):
    outs, hold = refs[:-1], refs[-1]
    wide, rank, depth = t_ref.shape
    width = per_node * width_cols
    fold = folding(rank, width)
    tall = rank // fold
    me_node = ids_ref[ids_ref.shape[0] - 1]
    dst = iota((depth, depth), 1)
    src = iota((depth, depth), 0)
    a, rest = dst // (samp * width), dst % (samp * width)
    s, rest = rest // width, rest % width
    want = (a * per_node + rest // width_cols) * (samp * width_cols) + s * width_cols + rest % width_cols
    move = jnp.where(src == want, 1.0, 0.0).astype(BF16)
    bits = pieces.bit_length() - 1
    for w in range(wide):
        t = t_ref[w]
        high = t.astype(BF16)
        mid = (t - high.astype(F32)).astype(BF16)
        low = (t - high.astype(F32) - mid.astype(F32)).astype(BF16)
        moved = dot(jnp.concatenate([high, mid, low], axis=0), move, ((1,), (0,)))
        moved = moved[:rank] + moved[rank:2 * rank] + moved[2 * rank:]
        for i in range(pieces):
            piece = moved[:, i * width:(i + 1) * width]
            parts = [piece[f * tall:(f + 1) * tall] for f in range(fold)]
            if fold * width < 128:
                parts.append(jnp.zeros((tall, 128 - fold * width), F32))
            hold[i] = jnp.concatenate(parts, axis=1)
        for p in range(pieces):
            outs[w][p * tall:(p + 1) * tall, :] = hold[me_node ^ reverse_bits(p, bits)]


def finish_kernel(scale, per_node, width_cols, count, inv_ref, piece_ref, *refs):
    both, high = refs[:count], refs[count:2 * count]
    low, core_ref, coef_ref = refs[2 * count:3 * count], refs[-2], refs[-1]
    rank = inv_ref.shape[0]
    inverse = inv_ref[...]
    at = 0
    for c in range(count):
        s = both[c][:rank, :].astype(F32) + both[c][rank:, :].astype(F32)
        rows = s.shape[1]
        s = s + (high[c][...].astype(F32) + low[c][...].astype(F32))
        core_ref[:, at:at + rows] = dot(inverse, s, ((1,), (0,)), HI)
        at += rows
    width = per_node * width_cols
    fold = folding(rank, width)
    total = piece_ref[...]
    total = jnp.concatenate([total[:, f * width:(f + 1) * width] for f in range(fold)], axis=0)
    out = dot(total, inverse, ((0,), (1,)), HI) * scale
    coef_ref[...] = jnp.concatenate(
        [out[p * width_cols:(p + 1) * width_cols, :] for p in range(per_node)], axis=1)


def finish(inverse, piece, both, high, low, scale, per_node, width_cols):
    rank = inverse.shape[0]
    count = len(both)
    rows = sum(v.shape[1] for v in high)
    return pl.pallas_call(
        functools.partial(finish_kernel, scale, per_node, width_cols, count),
        out_shape=(
            jax.ShapeDtypeStruct((rank, rows), F32),
            jax.ShapeDtypeStruct((width_cols, per_node * rank), F32),
        ),
        compiler_params=params(),
        cost_estimate=cost(12 * rank * rank * rows, 12 * rank * rows),
        name="finish",
    )(inverse, piece, *both, *high, *low)


def swap(value, axis, size, bit):
    return lax.ppermute(value, axis, [(i, i ^ bit) for i in range(size)])


def body(snapshots, sketch_matrix):
    rows_all = snapshots.shape[0]
    rank = sketch_matrix.shape[1]
    samp = lax.axis_size("samp")
    node = lax.axis_size("node")
    total = rows_all * node
    quarter = rows_all // samp
    me_s = lax.axis_index("samp").astype(jnp.int32)
    me_n = lax.axis_index("node").astype(jnp.int32)
    w_t = sketch_matrix.T
    last = samp // 2
    near = range(1, last)
    starts, sizes = (0, UNIT), (UNIT, quarter - UNIT)
    blocks = [(last, 0), (last, 1), (0, 0), (0, 1)]

    def block_of(base, c):
        return (me_s ^ base) * (quarter // UNIT) + starts[c] // UNIT

    borrowed = {b: [] for b in blocks}
    ws, w_at = [w_t], 0

    def borrow(chosen, after, w=None):
        out = ()
        for d in near:
            out = lend(jnp.stack([block_of(b[0] ^ d, b[1]) for b in chosen]), snapshots, UNIT, w, after)
            for b, v in zip(chosen, out):
                borrowed[b].append(swap(v, "samp", samp, d))
            after = tuple(out[:1])
        return after

    done = borrow(blocks[:1], (), w_t)
    for v in borrowed[blocks[0]]:
        w_at = v.shape[0] - rank
        ws.append(v)
    borrow(blocks[1:], done)

    pairs, arrived, done = {}, {}, ()
    ids = jnp.stack([block_of(*b) for b in blocks] + [me_n])
    slot = {b: k for k, b in enumerate(blocks)}
    for k, b in enumerate(blocks):
        later = ()
        numbers = [block_of(*b)] + [block_of(o[0] ^ d, o[1]) for o in later for d in near]
        out = sketch(jnp.stack(numbers), snapshots, ws, borrowed[b], UNIT, w_at, done)
        pairs[b], high = out[:2]
        done = (high,)
        if k + 1 < len(blocks):
            arrived[b[0] ^ last, b[1]] = swap(high, "samp", samp, last)
        for o in later:
            borrowed[o] = [swap(v, "samp", samp, d) for d, v in zip(near, out[2:])]
    own = [pairs[0, c] for c in range(2)]
    got_high = [arrived[0, c] for c in range(2)]

    def parts(chosen):
        return [(pairs[b], arrived[b], slot[b], borrowed[b]) for b in chosen]

    gram = own_gram(own[0], got_high[0], None, None)
    gram = own_gram(own[1], got_high[1], gram, 1.0 / total, done)
    t = project(ids, parts([(0, 0), (0, 1)]), snapshots, None, [gram])
    final = blocks[-1]
    late = [(final[0] ^ last, final[1])]
    high, t = lax.optimization_barrier((high, t))
    arrived[late[0]] = swap(high, "samp", samp, last)
    gram = gram + swap(gram, "samp", samp, last)
    got_low = []
    for c in range(2):
        low, _ = lax.optimization_barrier((pairs[last, c][rank:], gram))
        got_low.append(swap(low, "samp", samp, last))
    bit = last // 2
    while bit:
        gram = gram + swap(gram, "samp", samp, bit)
        bit //= 2
    rounds = node.bit_length() - 1
    before = gram
    for k in range(rounds):
        if k == min(PLACE[0], rounds - 1):
            t = project(ids, parts([(last, 0)]), snapshots, t, [gram])
            gram, t = lax.optimization_barrier((gram, t))
        before = gram
        gram = gram + swap(gram, "node", node, 1 << k)

    per_node = P1 // node
    width_cols = P2 // samp
    tall = rank // folding(rank, per_node * width_cols)
    messages = project(
        ids, parts(late), snapshots, t, [before],
        functools.partial(tail, node, samp, per_node, width_cols),
        [jax.ShapeDtypeStruct((node * tall, 128), F32)] * last,
        [pltpu.VMEM((node, tall, 128), F32)])
    if PLACE[1]:
        *messages, gram = lax.optimization_barrier((*messages, gram))

    pieces = messages[0]
    for d in near:
        pieces = pieces + swap(messages[d], "samp", samp, d)
    inverse = factor_inverse(gram, rank, (pieces,))
    for k in range(rounds):
        if k == min(PLACE[2], rounds - 1):
            pieces, inverse = lax.optimization_barrier((pieces, inverse))
        for c in range(2):
            if k == PLACE[3 + c]:
                pieces, got_low[c] = lax.optimization_barrier((pieces, got_low[c]))
        edge = pieces.shape[0] // 2
        pieces = pieces[:edge] + swap(pieces[edge:], "node", node, 1 << k)
    spread = node // samp
    route = [
        (n * samp + s, (s * spread + n // samp) * samp + n % samp) for n in range(node) for s in range(samp)
    ]
    piece = lax.ppermute(pieces, ("node", "samp"), route)
    core, coef = finish(inverse, piece, own, got_high, got_low, 1.0 / total, per_node, width_cols)
    return (core.T, coef.T)


def solution(mesh):
    placed = (P("node", "samp"), P("samp", None))
    return jax.shard_map(
        body,
        mesh=mesh,
        in_specs=placed,
        out_specs=(P(("node", "samp"), None), P("node", "samp")),
        check_vma=False,
    )
```

```python
import functools
import jax
import jax.numpy as jnp
import numpy as np
from jax import lax
from jax.experimental import pallas as pl
from jax.experimental.pallas import tpu as pltpu
from jax.sharding import PartitionSpec as P

P1 = 64
P2 = 32
BAND = 32
UNIT = 1024
LEND_PARTS = 4
PROJECT_ROWS = 512
PLACE = (-1, True, 1, -1, 1, True)
SKETCH_STEPS = 1
FACTOR_COST = 6e9
COST_CUT = 1
F32 = jnp.float32
BF16 = jnp.bfloat16
HI = lax.Precision.HIGHEST
UNREAD = pl.BlockSpec(memory_space=pl.ANY)
HELD = pl.BlockSpec(memory_space=pltpu.VMEM)
VMEM_LIMIT = 48 * 1024 * 1024


def iota(shape, dim):
    return lax.broadcasted_iota(jnp.int32, shape, dim)


def dot(a, b, dims, precision=None):
    return lax.dot_general(a, b, (dims, ((), ())), precision=precision, preferred_element_type=F32)


def params():
    return pltpu.CompilerParams(vmem_limit_bytes=VMEM_LIMIT)


def cost(flops, moved):
    return pl.CostEstimate(flops=int(flops) // COST_CUT, bytes_accessed=int(moved) // COST_CUT, transcendentals=0)


def lend_kernel(size, stride, at, ids_ref, x_ref, *refs):
    count = ids_ref.shape[0]
    extra = 1 if at is not None else 0
    outs, sems = refs[-1 - count:-1], refs[-1]
    copies = []
    for k in range(count):
        first = pl.multiple_of(ids_ref[k] * size, size)
        for part in range(size // stride):
            copies.append(pltpu.make_async_copy(
                x_ref.at[pl.ds(first + part * stride, stride)],
                outs[k].at[pl.ds(part * stride, stride)],
                sems.at[len(copies)]))
    if extra:
        copies.append(pltpu.make_async_copy(
            refs[0], outs[0].at[pl.ds(at, refs[0].shape[0])], sems.at[len(copies)]))
    for copy in copies:
        copy.start()
    for copy in copies:
        copy.wait()


def lend(ids, x, size, w=None, after=()):
    count = ids.shape[0]
    depth = x.shape[1]
    stride = size // LEND_PARTS
    at, height = None, size
    if w is not None:
        rank = w.shape[0]
        at = -(-size // rank) * rank
        height = at + rank
    more = [] if w is None else [w]
    return pl.pallas_call(
        functools.partial(lend_kernel, size, stride, at),
        in_specs=[pl.BlockSpec(memory_space=pltpu.SMEM)] + [UNREAD] * (1 + len(more) + len(after)),
        out_specs=[HELD] * count,
        out_shape=[jax.ShapeDtypeStruct((height, depth), BF16)] * count,
        scratch_shapes=[pltpu.SemaphoreType.DMA((LEND_PARTS * count + len(more),))],
        compiler_params=params(),
        cost_estimate=cost(0, 4 * count * height * depth),
        name="lend",
    )(ids, x, *more, *after)


def sketch_kernel(count, lent, ids_ref, x_ref, *refs):
    w_refs, x_refs = refs[:count], (x_ref,) + refs[count:2 * count - 1]
    both_ref, high_ref = refs[len(refs) - lent - 2:len(refs) - lent]
    rank = high_ref.shape[0]
    for k in range(lent):
        refs[len(refs) - lent + k][...] = refs[2 * count - 1 + k][...]
    s = None
    for w_ref, ref in zip(w_refs, x_refs):
        term = dot(w_ref[...], ref[...], ((1,), (1,)))
        s = term if s is None else s + term
    high = s.astype(BF16)
    high_ref[...] = high
    both_ref[:rank, :] = high
    both_ref[rank:, :] = (s - high.astype(F32)).astype(BF16)


def sketch(ids, x, ws, extra, size, w_at, after=()):
    rank, depth = ws[0].shape
    count = len(ws)
    lent = ids.shape[0] - 1
    steps = SKETCH_STEPS
    rows = size // steps
    return pl.pallas_call(
        functools.partial(sketch_kernel, count, lent),
        grid_spec=pltpu.PrefetchScalarGridSpec(
            num_scalar_prefetch=1,
            grid=(steps,),
            in_specs=[pl.BlockSpec((rows, depth), lambda i, ids: (ids[0] * steps + i, 0))]
            + [pl.BlockSpec((rank, depth), lambda i, ids: (0, 0))]
            + [pl.BlockSpec((rank, depth), lambda i, ids: (w_at // rank, 0))] * (count - 1)
            + [pl.BlockSpec((rows, depth), lambda i, ids: (i, 0))] * (count - 1)
            + [pl.BlockSpec((rows, depth), lambda i, ids, k=k: (ids[1 + k] * steps + i, 0)) for k in range(lent)]
            + [UNREAD] * len(after),
            out_specs=[
                pl.BlockSpec((2 * rank, rows), lambda i, ids: (0, i)),
                pl.BlockSpec((rank, rows), lambda i, ids: (0, i)),
            ] + [pl.BlockSpec((rows, depth), lambda i, ids: (i, 0))] * lent,
        ),
        out_shape=[
            jax.ShapeDtypeStruct((2 * rank, size), BF16),
            jax.ShapeDtypeStruct((rank, size), BF16),
        ] + [jax.ShapeDtypeStruct((size, depth), BF16)] * lent,
        compiler_params=params(),
        cost_estimate=cost(
            2 * rank * depth * size * count, size * (depth * 2 * (count + 2 * lent) + rank * 6)),
        name="sketch",
    )(ids, x, *ws, *extra, *([x] * lent), *after)


def packing(rank):
    bands = rank // BAND
    pairs = [(i, j) for i in range(bands) for j in range(i, bands)]
    wide = 128 // BAND
    groups = -(-len(pairs) // wide)
    groups += groups % 2
    return pairs, wide, groups


def pack_gram(gram):
    pairs, wide, groups = packing(gram.shape[0])
    out = []
    for g in range(groups):
        chosen = pairs[g * wide:(g + 1) * wide]
        parts = [gram[i * BAND:(i + 1) * BAND, j * BAND:(j + 1) * BAND] for i, j in chosen]
        parts += [jnp.zeros((BAND, BAND), F32)] * (wide - len(chosen))
        out.append(jnp.concatenate(parts, axis=1))
    return jnp.concatenate(out, axis=0)


def fold_square(x, rank):
    return (x[:rank, :rank] + x[rank:, rank:]) + (x[:rank, rank:] + x[rank:, :rank])


def gram_kernel(scale, has_base, own_ref, got_ref, *refs):
    o_ref = refs[-1]
    rank = got_ref.shape[0]
    s = own_ref[:rank, :].astype(F32) + own_ref[rank:, :].astype(F32) + got_ref[...].astype(F32)
    high = s.astype(BF16)
    both = jnp.concatenate([high, (s - high.astype(F32)).astype(BF16)], axis=0)
    total = fold_square(dot(both, both, ((1,), (1,))), rank)
    if has_base:
        total = total + refs[0][...]
    o_ref[...] = total if scale is None else pack_gram(total * scale)


def own_gram(own, got, base, scale, after=()):
    rank, rows = got.shape
    bases = [] if base is None else [base]
    shape = (rank, rank) if scale is None else (packing(rank)[2] * BAND, 128)
    return pl.pallas_call(
        functools.partial(gram_kernel, scale, len(bases)),
        in_specs=[HELD] * (2 + len(bases)) + [UNREAD] * len(after),
        out_shape=jax.ShapeDtypeStruct(shape, F32),
        compiler_params=params(),
        cost_estimate=cost(8 * rank * rank * rows, 6 * rank * rows),
        name="gram",
    )(own, got, *bases, *after)


def wide_lanes(x, n):
    reps = -(-n // 128)
    return jnp.concatenate([x] * reps, axis=1)[:, :n] if reps > 1 else x[:, :n]


def band_rows(block, b):
    n = block.shape[1]
    count = BAND // 8
    part = [block[8 * i:8 * i + 8, :] for i in range(count)]
    sub = iota((8, n), 0)
    lane = iota((8, n), 1)
    for m in range(count):
        c0 = b * BAND + 8 * m
        live = count - m
        col = [
            [jnp.broadcast_to(part[m + i][:, c0 + k:c0 + k + 1], (8, 128)) for i in range(live)]
            for k in range(8)
        ]
        here = (lane >= c0) & (lane < c0 + 8)
        part[m] = jnp.where(here, jnp.where(lane - c0 == sub, 1.0, 0.0), part[m])
        for i in range(1, live):
            part[m + i] = jnp.where(here, 0.0, part[m + i])
        for j in range(8):
            inv_root = lax.rsqrt(jnp.broadcast_to(col[j][0][j:j + 1, :], (8, 128)))
            low = [x * inv_root for x in col[j]]
            for k in range(j + 1, 8):
                t = jnp.broadcast_to(low[0][k:k + 1, :], (8, 128))
                for i in range(live):
                    col[k][i] = col[k][i] - low[i] * t
            row = jnp.broadcast_to(part[m][j:j + 1, :], (8, n)) * wide_lanes(inv_root, n)
            for i in range(live):
                new = part[m + i] - wide_lanes(low[i], n) * row
                if i == 0:
                    new = jnp.where(sub > j, new, jnp.where(sub == j, row, part[m]))
                part[m + i] = new
    return jnp.concatenate(part, axis=0)


def factor_kernel(rank, g_ref, *refs):
    o_ref = refs[-1]
    pairs, wide, _ = packing(rank)
    o_ref[...] = jnp.zeros((rank, rank), F32)
    for at, (i, j) in enumerate(pairs):
        g, k = at // wide, at % wide
        o_ref[i * BAND:(i + 1) * BAND, j * BAND:(j + 1) * BAND] = g_ref[
            g * BAND:(g + 1) * BAND, k * BAND:(k + 1) * BAND]
    for b in range(rank // BAND):
        lo, hi = b * BAND, (b + 1) * BAND
        r = band_rows(o_ref[lo:hi, :], b)
        rows, cols = iota(r.shape, 0), iota(r.shape, 1)
        r = jnp.where((cols >= lo) & (cols < hi) & (cols - lo > rows), 0.0, r)
        o_ref[lo:hi, :] = jnp.where(cols < hi, r, 0.0)
        if hi < rank:
            left = jnp.where(cols >= hi, r, 0.0)
            update = dot(left, r, ((0,), (0,)), HI)
            kept = jnp.where(iota((rank - hi, rank), 1) // BAND == b, 0.0, o_ref[hi:, :])
            o_ref[hi:, :] = kept - update[hi:, :]


def factor_inverse(packed, rank, after=()):
    return pl.pallas_call(
        functools.partial(factor_kernel, rank),
        in_specs=[HELD] + [UNREAD] * len(after),
        out_shape=jax.ShapeDtypeStruct((rank, rank), F32),
        compiler_params=params(),
        cost_estimate=cost(FACTOR_COST, 4 * rank * rank),
        name="factor",
    )(packed, *after)


def project_kernel(count, wide, has_base, aside, finish, ids_ref, *refs):
    pair_refs, high_refs, x_refs = refs[:count], refs[count:2 * count], refs[2 * count:count * (2 + wide)]
    at = count * (2 + wide)
    beside = refs[at + has_base:at + has_base + aside]
    rest = refs[at + has_base + aside:]
    t_ref = rest[-1]
    rank = t_ref.shape[1]

    @pl.when(pl.program_id(0) == 0)
    def _():
        t_ref[...] = refs[at][...] if has_base else jnp.zeros_like(t_ref)

    sums = []
    for pair_ref, high_ref in zip(pair_refs, high_refs):
        s = pair_ref[:rank, :].astype(F32) + pair_ref[rank:, :].astype(F32) + high_ref[...].astype(F32)
        high = s.astype(BF16)
        sums.append(jnp.concatenate([high, (s - high.astype(F32)).astype(BF16)], axis=0))
    for w in range(wide):
        total = None
        for k in range(count):
            term = dot(sums[k], x_refs[w * count + k][...], ((1,), (0,)))
            total = term if total is None else total + term
        t_ref[w] += total[:rank] + total[rank:]
    if finish is not None:
        @pl.when(pl.program_id(0) == pl.num_programs(0) - 1)
        def _():
            finish(t_ref, ids_ref, beside, *rest[:-1])


def project(ids, work, x, base, beside=(), finish=None, outs=(), scratch=()):
    count = len(work)
    wide = 1 + len(work[0][3])
    rank, span = work[0][1].shape
    depth = x.shape[1]
    rows = min(span, PROJECT_ROWS)
    steps = span // rows
    bases = [] if base is None else [base]
    whole = pl.BlockSpec((wide, rank, depth), lambda i, ids: (0, 0, 0))
    t_shape = jax.ShapeDtypeStruct((wide, rank, depth), F32)
    if finish is None:
        out_specs, out_shape, scratch_shapes = whole, t_shape, []
    else:
        out_specs = [pl.BlockSpec(o.shape, lambda i, ids: (0, 0)) for o in outs]
        out_shape = list(outs)
        scratch_shapes = list(scratch) + [pltpu.VMEM((wide, rank, depth), F32)]
    return pl.pallas_call(
        functools.partial(project_kernel, count, wide, len(bases), len(beside), finish),
        grid_spec=pltpu.PrefetchScalarGridSpec(
            num_scalar_prefetch=1,
            grid=(steps,),
            in_specs=[pl.BlockSpec((2 * rank, rows), lambda i, ids: (0, i))] * count
            + [pl.BlockSpec((rank, rows), lambda i, ids: (0, i))] * count
            + [
                pl.BlockSpec((rows, depth), lambda i, ids, slot=w[2]: (ids[slot] * steps + i, 0))
                for w in work
            ]
            + [pl.BlockSpec((rows, depth), lambda i, ids: (i, 0))] * (count * (wide - 1))
            + [whole] * len(bases) + [pl.BlockSpec(v.shape, lambda i, ids: (0, 0)) for v in beside],
            out_specs=out_specs,
            scratch_shapes=scratch_shapes,
        ),
        out_shape=out_shape,
        compiler_params=params(),
        cost_estimate=cost(
            4 * rank * depth * span * count * wide, span * count * (depth * wide + 3 * rank) * 2),
        name="project",
    )(
        ids, *[w[0] for w in work], *[w[1] for w in work], *([x] * count),
        *[w[3][d] for d in range(wide - 1) for w in work], *bases, *beside)


def folding(rank, width):
    best = 1
    for f in range(1, rank + 1):
        if rank % f == 0 and (rank // f) % 8 == 0 and f * width <= 128:
            best = f
    return best


def reverse_bits(p, count):
    return sum(1 << (count - 1 - b) for b in range(count) if (p >> b) & 1)


def column_order(depth, samp, per_node, width_cols):
    width = per_node * width_cols
    dst = np.arange(depth)
    a, rest = dst // (samp * width), dst % (samp * width)
    s, rest = rest // width, rest % width
    src = (a * per_node + rest // width_cols) * (samp * width_cols) + s * width_cols + rest % width_cols
    return jnp.asarray(np.arange(depth)[:, None] == src[None, :], BF16)


def tail(pieces, per_node, width_cols, t_ref, ids_ref, beside, *refs):
    outs, hold = refs[:-1], refs[-1]
    wide, rank, depth = t_ref.shape
    width = per_node * width_cols
    fold = folding(rank, width)
    tall = rank // fold
    me_node = ids_ref[ids_ref.shape[0] - 1]
    move = beside[0][...]
    bits = pieces.bit_length() - 1
    for w in range(wide):
        t = t_ref[w]
        high = t.astype(BF16)
        mid = (t - high.astype(F32)).astype(BF16)
        low = (t - high.astype(F32) - mid.astype(F32)).astype(BF16)
        moved = dot(jnp.concatenate([high, mid, low], axis=0), move, ((1,), (0,)))
        moved = moved[:rank] + moved[rank:2 * rank] + moved[2 * rank:]
        for i in range(pieces):
            piece = moved[:, i * width:(i + 1) * width]
            parts = [piece[f * tall:(f + 1) * tall] for f in range(fold)]
            if fold * width < 128:
                parts.append(jnp.zeros((tall, 128 - fold * width), F32))
            hold[i] = jnp.concatenate(parts, axis=1)
        for p in range(pieces):
            outs[w][p * tall:(p + 1) * tall, :] = hold[me_node ^ reverse_bits(p, bits)]


def finish_kernel(scale, per_node, width_cols, count, inv_ref, piece_ref, *refs):
    both, high = refs[:count], refs[count:2 * count]
    low, core_ref, coef_ref = refs[2 * count:3 * count], refs[-2], refs[-1]
    rank = inv_ref.shape[0]
    inverse = inv_ref[...]
    at = 0
    for c in range(count):
        s = both[c][:rank, :].astype(F32) + both[c][rank:, :].astype(F32)
        rows = s.shape[1]
        s = s + (high[c][...].astype(F32) + low[c][...].astype(F32))
        core_ref[:, at:at + rows] = dot(inverse, s, ((1,), (0,)), HI)
        at += rows
    width = per_node * width_cols
    fold = folding(rank, width)
    total = piece_ref[...]
    total = jnp.concatenate([total[:, f * width:(f + 1) * width] for f in range(fold)], axis=0)
    out = dot(total, inverse, ((0,), (1,)), HI) * scale
    coef_ref[...] = jnp.concatenate(
        [out[p * width_cols:(p + 1) * width_cols, :] for p in range(per_node)], axis=1)


def finish(inverse, piece, both, high, low, scale, per_node, width_cols):
    rank = inverse.shape[0]
    count = len(both)
    rows = sum(v.shape[1] for v in high)
    return pl.pallas_call(
        functools.partial(finish_kernel, scale, per_node, width_cols, count),
        out_shape=(
            jax.ShapeDtypeStruct((rank, rows), F32),
            jax.ShapeDtypeStruct((width_cols, per_node * rank), F32),
        ),
        compiler_params=params(),
        cost_estimate=cost(12 * rank * rank * rows, 12 * rank * rows),
        name="finish",
    )(inverse, piece, *both, *high, *low)


def swap(value, axis, size, bit):
    return lax.ppermute(value, axis, [(i, i ^ bit) for i in range(size)])


def body(snapshots, sketch_matrix):
    rows_all = snapshots.shape[0]
    rank = sketch_matrix.shape[1]
    samp = lax.axis_size("samp")
    node = lax.axis_size("node")
    total = rows_all * node
    quarter = rows_all // samp
    me_s = lax.axis_index("samp").astype(jnp.int32)
    me_n = lax.axis_index("node").astype(jnp.int32)
    w_t = sketch_matrix.T
    last = samp // 2
    near = range(1, last)
    starts, sizes = (0, UNIT), (UNIT, quarter - UNIT)
    blocks = [(last, 0), (last, 1), (0, 0), (0, 1)]

    def block_of(base, c):
        return (me_s ^ base) * (quarter // UNIT) + starts[c] // UNIT

    borrowed = {b: [] for b in blocks}
    ws, w_at = [w_t], 0

    def borrow(chosen, after, w=None):
        out = ()
        for d in near:
            out = lend(jnp.stack([block_of(b[0] ^ d, b[1]) for b in chosen]), snapshots, UNIT, w, after)
            for b, v in zip(chosen, out):
                borrowed[b].append(swap(v, "samp", samp, d))
            after = tuple(out[:1])
        return after

    done = borrow(blocks[:1], (), w_t)
    for v in borrowed[blocks[0]]:
        w_at = v.shape[0] - rank
        ws.append(v)
    borrow(blocks[1:], done)

    pairs, arrived, done = {}, {}, ()
    ids = jnp.stack([block_of(*b) for b in blocks] + [me_n])
    slot = {b: k for k, b in enumerate(blocks)}
    for k, b in enumerate(blocks):
        later = ()
        numbers = [block_of(*b)] + [block_of(o[0] ^ d, o[1]) for o in later for d in near]
        out = sketch(jnp.stack(numbers), snapshots, ws, borrowed[b], UNIT, w_at, done)
        pairs[b], high = out[:2]
        done = (high,)
        if k + 1 < len(blocks):
            arrived[b[0] ^ last, b[1]] = swap(high, "samp", samp, last)
        for o in later:
            borrowed[o] = [swap(v, "samp", samp, d) for d, v in zip(near, out[2:])]
    own = [pairs[0, c] for c in range(2)]
    got_high = [arrived[0, c] for c in range(2)]

    def parts(chosen):
        return [(pairs[b], arrived[b], slot[b], borrowed[b]) for b in chosen]

    gram = own_gram(own[0], got_high[0], None, None)
    t = project(ids, parts([(0, 0)]), snapshots, None, [gram])
    if PLACE[5]:
        t, gram = lax.optimization_barrier((t, gram))
    gram = own_gram(own[1], got_high[1], gram, 1.0 / total, done)
    t = project(ids, parts([(0, 1)]), snapshots, t, [gram])
    final = blocks[-1]
    late = [(final[0] ^ last, final[1])]
    high, t = lax.optimization_barrier((high, t))
    arrived[late[0]] = swap(high, "samp", samp, last)
    gram = gram + swap(gram, "samp", samp, last)
    got_low = []
    for c in range(2):
        low, _ = lax.optimization_barrier((pairs[last, c][rank:], gram))
        got_low.append(swap(low, "samp", samp, last))
    if PLACE[0] < 0:
        t = project(ids, parts([(last, 0)]), snapshots, t)
        gram, t = lax.optimization_barrier((gram, t))
    bit = last // 2
    while bit:
        gram = gram + swap(gram, "samp", samp, bit)
        bit //= 2
    rounds = node.bit_length() - 1
    before = gram
    for k in range(rounds):
        if k == PLACE[0]:
            t = project(ids, parts([(last, 0)]), snapshots, t, [gram])
            gram, t = lax.optimization_barrier((gram, t))
        before = gram
        gram = gram + swap(gram, "node", node, 1 << k)

    per_node = P1 // node
    width_cols = P2 // samp
    tall = rank // folding(rank, per_node * width_cols)
    messages = project(
        ids, parts(late), snapshots, t, [column_order(snapshots.shape[1], samp, per_node, width_cols), before],
        functools.partial(tail, node, per_node, width_cols),
        [jax.ShapeDtypeStruct((node * tall, 128), F32)] * last,
        [pltpu.VMEM((node, tall, 128), F32)])
    if PLACE[1]:
        *messages, gram = lax.optimization_barrier((*messages, gram))
    for c in range(2):
        if PLACE[3 + c] < 0:
            *messages, got_low[c] = lax.optimization_barrier((*messages, got_low[c]))

    pieces = messages[0]
    for d in near:
        pieces = pieces + swap(messages[d], "samp", samp, d)
    inverse = factor_inverse(gram, rank, (pieces,))
    for k in range(rounds):
        if k == min(PLACE[2], rounds - 1):
            pieces, inverse = lax.optimization_barrier((pieces, inverse))
        for c in range(2):
            if k == PLACE[3 + c]:
                pieces, got_low[c] = lax.optimization_barrier((pieces, got_low[c]))
        edge = pieces.shape[0] // 2
        pieces = pieces[:edge] + swap(pieces[edge:], "node", node, 1 << k)
    spread = node // samp
    route = [
        (n * samp + s, (s * spread + n // samp) * samp + n % samp) for n in range(node) for s in range(samp)
    ]
    piece = lax.ppermute(pieces, ("node", "samp"), route)
    core, coef = finish(inverse, piece, own, got_high, got_low, 1.0 / total, per_node, width_cols)
    return (core.T, coef.T)


def solution(mesh):
    placed = (P("node", "samp"), P("samp", None))
    return jax.shard_map(
        body,
        mesh=mesh,
        in_specs=placed,
        out_specs=(P(("node", "samp"), None), P("node", "samp")),
        check_vma=False,
    )
```

```python
import functools
import jax
import jax.numpy as jnp
import numpy as np
from jax import lax
from jax.experimental import pallas as pl
from jax.experimental.pallas import tpu as pltpu
from jax.sharding import PartitionSpec as P

P1 = 64
P2 = 32
BAND = 32
UNIT = 1024
LEND_PARTS = 4
PROJECT_ROWS = 512
PLACE = (False, 1, -1, True, False)
SKETCH_STEPS = 1
FACTOR_COST = 6e9
COST_CUT = 1
F32 = jnp.float32
BF16 = jnp.bfloat16
HI = lax.Precision.HIGHEST
UNREAD = pl.BlockSpec(memory_space=pl.ANY)
HELD = pl.BlockSpec(memory_space=pltpu.VMEM)
VMEM_LIMIT = 48 * 1024 * 1024


def iota(shape, dim):
    return lax.broadcasted_iota(jnp.int32, shape, dim)


def dot(a, b, dims, precision=None):
    return lax.dot_general(a, b, (dims, ((), ())), precision=precision, preferred_element_type=F32)


def params():
    return pltpu.CompilerParams(vmem_limit_bytes=VMEM_LIMIT)


def cost(flops, moved):
    return pl.CostEstimate(flops=int(flops) // COST_CUT, bytes_accessed=int(moved) // COST_CUT, transcendentals=0)


def lend_kernel(size, stride, at, ids_ref, x_ref, *refs):
    count = ids_ref.shape[0]
    extra = 1 if at is not None else 0
    outs, sems = refs[-1 - count:-1], refs[-1]
    copies = []
    for k in range(count):
        first = pl.multiple_of(ids_ref[k] * size, size)
        for part in range(size // stride):
            copies.append(pltpu.make_async_copy(
                x_ref.at[pl.ds(first + part * stride, stride)],
                outs[k].at[pl.ds(part * stride, stride)],
                sems.at[len(copies)]))
    if extra:
        copies.append(pltpu.make_async_copy(
            refs[0], outs[0].at[pl.ds(at, refs[0].shape[0])], sems.at[len(copies)]))
    for copy in copies:
        copy.start()
    for copy in copies:
        copy.wait()


def lend(ids, x, size, w=None, after=()):
    count = ids.shape[0]
    depth = x.shape[1]
    stride = size // LEND_PARTS
    at, height = None, size
    if w is not None:
        rank = w.shape[0]
        at = -(-size // rank) * rank
        height = at + rank
    more = [] if w is None else [w]
    return pl.pallas_call(
        functools.partial(lend_kernel, size, stride, at),
        in_specs=[pl.BlockSpec(memory_space=pltpu.SMEM)] + [UNREAD] * (1 + len(more) + len(after)),
        out_specs=[HELD] * count,
        out_shape=[jax.ShapeDtypeStruct((height, depth), BF16)] * count,
        scratch_shapes=[pltpu.SemaphoreType.DMA((LEND_PARTS * count + len(more),))],
        compiler_params=params(),
        cost_estimate=cost(0, 4 * count * height * depth),
        name="lend",
    )(ids, x, *more, *after)


def sketch_kernel(count, lent, ids_ref, x_ref, *refs):
    w_refs, x_refs = refs[:count], (x_ref,) + refs[count:2 * count - 1]
    both_ref, high_ref = refs[len(refs) - lent - 2:len(refs) - lent]
    rank = high_ref.shape[0]
    for k in range(lent):
        refs[len(refs) - lent + k][...] = refs[2 * count - 1 + k][...]
    s = None
    for w_ref, ref in zip(w_refs, x_refs):
        term = dot(w_ref[...], ref[...], ((1,), (1,)))
        s = term if s is None else s + term
    high = s.astype(BF16)
    high_ref[...] = high
    both_ref[:rank, :] = high
    both_ref[rank:, :] = (s - high.astype(F32)).astype(BF16)


def sketch(ids, x, ws, extra, size, w_at, after=()):
    rank, depth = ws[0].shape
    count = len(ws)
    lent = ids.shape[0] - 1
    steps = SKETCH_STEPS
    rows = size // steps
    return pl.pallas_call(
        functools.partial(sketch_kernel, count, lent),
        grid_spec=pltpu.PrefetchScalarGridSpec(
            num_scalar_prefetch=1,
            grid=(steps,),
            in_specs=[pl.BlockSpec((rows, depth), lambda i, ids: (ids[0] * steps + i, 0))]
            + [pl.BlockSpec((rank, depth), lambda i, ids: (0, 0))]
            + [pl.BlockSpec((rank, depth), lambda i, ids: (w_at // rank, 0))] * (count - 1)
            + [pl.BlockSpec((rows, depth), lambda i, ids: (i, 0))] * (count - 1)
            + [pl.BlockSpec((rows, depth), lambda i, ids, k=k: (ids[1 + k] * steps + i, 0)) for k in range(lent)]
            + [UNREAD] * len(after),
            out_specs=[
                pl.BlockSpec((2 * rank, rows), lambda i, ids: (0, i)),
                pl.BlockSpec((rank, rows), lambda i, ids: (0, i)),
            ] + [pl.BlockSpec((rows, depth), lambda i, ids: (i, 0))] * lent,
        ),
        out_shape=[
            jax.ShapeDtypeStruct((2 * rank, size), BF16),
            jax.ShapeDtypeStruct((rank, size), BF16),
        ] + [jax.ShapeDtypeStruct((size, depth), BF16)] * lent,
        compiler_params=params(),
        cost_estimate=cost(
            2 * rank * depth * size * count, size * (depth * 2 * (count + 2 * lent) + rank * 6)),
        name="sketch",
    )(ids, x, *ws, *extra, *([x] * lent), *after)


def packing(rank):
    bands = rank // BAND
    pairs = [(i, j) for i in range(bands) for j in range(i, bands)]
    wide = 128 // BAND
    groups = -(-len(pairs) // wide)
    groups += groups % 2
    return pairs, wide, groups


def pack_gram(gram):
    pairs, wide, groups = packing(gram.shape[0])
    out = []
    for g in range(groups):
        chosen = pairs[g * wide:(g + 1) * wide]
        parts = [gram[i * BAND:(i + 1) * BAND, j * BAND:(j + 1) * BAND] for i, j in chosen]
        parts += [jnp.zeros((BAND, BAND), F32)] * (wide - len(chosen))
        out.append(jnp.concatenate(parts, axis=1))
    return jnp.concatenate(out, axis=0)


def fold_square(x, rank):
    return (x[:rank, :rank] + x[rank:, rank:]) + (x[:rank, rank:] + x[rank:, :rank])


def gram_kernel(scale, has_base, own_ref, got_ref, *refs):
    o_ref = refs[-1]
    rank = got_ref.shape[0]
    s = own_ref[:rank, :].astype(F32) + own_ref[rank:, :].astype(F32) + got_ref[...].astype(F32)
    high = s.astype(BF16)
    both = jnp.concatenate([high, (s - high.astype(F32)).astype(BF16)], axis=0)
    total = fold_square(dot(both, both, ((1,), (1,))), rank)
    if has_base:
        total = total + refs[0][...]
    o_ref[...] = total if scale is None else pack_gram(total * scale)


def own_gram(own, got, base, scale, after=()):
    rank, rows = got.shape
    bases = [] if base is None else [base]
    shape = (rank, rank) if scale is None else (packing(rank)[2] * BAND, 128)
    return pl.pallas_call(
        functools.partial(gram_kernel, scale, len(bases)),
        in_specs=[HELD] * (2 + len(bases)) + [UNREAD] * len(after),
        out_shape=jax.ShapeDtypeStruct(shape, F32),
        compiler_params=params(),
        cost_estimate=cost(8 * rank * rank * rows, 6 * rank * rows),
        name="gram",
    )(own, got, *bases, *after)


def wide_lanes(x, n):
    reps = -(-n // 128)
    return jnp.concatenate([x] * reps, axis=1)[:, :n] if reps > 1 else x[:, :n]


def band_rows(block, b):
    n = block.shape[1]
    count = BAND // 8
    part = [block[8 * i:8 * i + 8, :] for i in range(count)]
    sub = iota((8, n), 0)
    lane = iota((8, n), 1)
    for m in range(count):
        c0 = b * BAND + 8 * m
        live = count - m
        col = [
            [jnp.broadcast_to(part[m + i][:, c0 + k:c0 + k + 1], (8, 128)) for i in range(live)]
            for k in range(8)
        ]
        here = (lane >= c0) & (lane < c0 + 8)
        part[m] = jnp.where(here, jnp.where(lane - c0 == sub, 1.0, 0.0), part[m])
        for i in range(1, live):
            part[m + i] = jnp.where(here, 0.0, part[m + i])
        for j in range(8):
            inv_root = lax.rsqrt(jnp.broadcast_to(col[j][0][j:j + 1, :], (8, 128)))
            low = [x * inv_root for x in col[j]]
            for k in range(j + 1, 8):
                t = jnp.broadcast_to(low[0][k:k + 1, :], (8, 128))
                for i in range(live):
                    col[k][i] = col[k][i] - low[i] * t
            row = jnp.broadcast_to(part[m][j:j + 1, :], (8, n)) * wide_lanes(inv_root, n)
            for i in range(live):
                new = part[m + i] - wide_lanes(low[i], n) * row
                if i == 0:
                    new = jnp.where(sub > j, new, jnp.where(sub == j, row, part[m]))
                part[m + i] = new
    return jnp.concatenate(part, axis=0)


def factor_kernel(rank, g_ref, *refs):
    o_ref = refs[-1]
    pairs, wide, _ = packing(rank)
    o_ref[...] = jnp.zeros((rank, rank), F32)
    for at, (i, j) in enumerate(pairs):
        g, k = at // wide, at % wide
        o_ref[i * BAND:(i + 1) * BAND, j * BAND:(j + 1) * BAND] = g_ref[
            g * BAND:(g + 1) * BAND, k * BAND:(k + 1) * BAND]
    for b in range(rank // BAND):
        lo, hi = b * BAND, (b + 1) * BAND
        r = band_rows(o_ref[lo:hi, :], b)
        rows, cols = iota(r.shape, 0), iota(r.shape, 1)
        r = jnp.where((cols >= lo) & (cols < hi) & (cols - lo > rows), 0.0, r)
        o_ref[lo:hi, :] = jnp.where(cols < hi, r, 0.0)
        if hi < rank:
            left = jnp.where(cols >= hi, r, 0.0)
            update = dot(left, r, ((0,), (0,)), HI)
            kept = jnp.where(iota((rank - hi, rank), 1) // BAND == b, 0.0, o_ref[hi:, :])
            o_ref[hi:, :] = kept - update[hi:, :]


def factor_inverse(packed, rank, after=()):
    return pl.pallas_call(
        functools.partial(factor_kernel, rank),
        in_specs=[HELD] + [UNREAD] * len(after),
        out_shape=jax.ShapeDtypeStruct((rank, rank), F32),
        compiler_params=params(),
        cost_estimate=cost(FACTOR_COST, 4 * rank * rank),
        name="factor",
    )(packed, *after)


def project_kernel(count, wide, has_base, aside, finish, ids_ref, *refs):
    pair_refs, high_refs, x_refs = refs[:count], refs[count:2 * count], refs[2 * count:count * (2 + wide)]
    at = count * (2 + wide)
    beside = refs[at + has_base:at + has_base + aside]
    rest = refs[at + has_base + aside:]
    t_ref = rest[-1]
    rank = t_ref.shape[1]

    @pl.when(pl.program_id(0) == 0)
    def _():
        t_ref[...] = refs[at][...] if has_base else jnp.zeros_like(t_ref)

    sums = []
    for pair_ref, high_ref in zip(pair_refs, high_refs):
        s = pair_ref[:rank, :].astype(F32) + pair_ref[rank:, :].astype(F32) + high_ref[...].astype(F32)
        high = s.astype(BF16)
        sums.append(jnp.concatenate([high, (s - high.astype(F32)).astype(BF16)], axis=0))
    for w in range(wide):
        total = None
        for k in range(count):
            term = dot(sums[k], x_refs[w * count + k][...], ((1,), (0,)))
            total = term if total is None else total + term
        t_ref[w] += total[:rank] + total[rank:]
    if finish is not None:
        @pl.when(pl.program_id(0) == pl.num_programs(0) - 1)
        def _():
            finish(t_ref, ids_ref, beside, *rest[:-1])


def project(ids, work, x, base, beside=(), finish=None, outs=(), scratch=()):
    count = len(work)
    wide = 1 + len(work[0][3])
    rank, span = work[0][1].shape
    depth = x.shape[1]
    rows = min(span, PROJECT_ROWS)
    steps = span // rows
    bases = [] if base is None else [base]
    whole = pl.BlockSpec((wide, rank, depth), lambda i, ids: (0, 0, 0))
    t_shape = jax.ShapeDtypeStruct((wide, rank, depth), F32)
    if finish is None:
        out_specs, out_shape, scratch_shapes = whole, t_shape, []
    else:
        out_specs = [pl.BlockSpec(o.shape, lambda i, ids: (0, 0)) for o in outs]
        out_shape = list(outs)
        scratch_shapes = list(scratch) + [pltpu.VMEM((wide, rank, depth), F32)]
    return pl.pallas_call(
        functools.partial(project_kernel, count, wide, len(bases), len(beside), finish),
        grid_spec=pltpu.PrefetchScalarGridSpec(
            num_scalar_prefetch=1,
            grid=(steps,),
            in_specs=[pl.BlockSpec((2 * rank, rows), lambda i, ids: (0, i))] * count
            + [pl.BlockSpec((rank, rows), lambda i, ids: (0, i))] * count
            + [
                pl.BlockSpec((rows, depth), lambda i, ids, slot=w[2]: (ids[slot] * steps + i, 0))
                for w in work
            ]
            + [pl.BlockSpec((rows, depth), lambda i, ids: (i, 0))] * (count * (wide - 1))
            + [whole] * len(bases) + [pl.BlockSpec(v.shape, lambda i, ids: (0, 0)) for v in beside],
            out_specs=out_specs,
            scratch_shapes=scratch_shapes,
        ),
        out_shape=out_shape,
        compiler_params=params(),
        cost_estimate=cost(
            4 * rank * depth * span * count * wide, span * count * (depth * wide + 3 * rank) * 2),
        name="project",
    )(
        ids, *[w[0] for w in work], *[w[1] for w in work], *([x] * count),
        *[w[3][d] for d in range(wide - 1) for w in work], *bases, *beside)


def folding(rank, width):
    best = 1
    for f in range(1, rank + 1):
        if rank % f == 0 and (rank // f) % 8 == 0 and f * width <= 128:
            best = f
    return best


def reverse_bits(p, count):
    return sum(1 << (count - 1 - b) for b in range(count) if (p >> b) & 1)


def column_order(depth, samp, per_node, width_cols):
    width = per_node * width_cols
    dst = np.arange(depth)
    a, rest = dst // (samp * width), dst % (samp * width)
    s, rest = rest // width, rest % width
    src = (a * per_node + rest // width_cols) * (samp * width_cols) + s * width_cols + rest % width_cols
    return jnp.asarray(np.arange(depth)[:, None] == src[None, :], BF16)


def tail(pieces, per_node, width_cols, t_ref, ids_ref, beside, *refs):
    outs, hold = refs[:-1], refs[-1]
    wide, rank, depth = t_ref.shape
    width = per_node * width_cols
    fold = folding(rank, width)
    tall = rank // fold
    me_node = ids_ref[ids_ref.shape[0] - 1]
    move = beside[0][...]
    bits = pieces.bit_length() - 1
    for w in range(wide):
        t = t_ref[w]
        high = t.astype(BF16)
        mid = (t - high.astype(F32)).astype(BF16)
        low = (t - high.astype(F32) - mid.astype(F32)).astype(BF16)
        moved = dot(jnp.concatenate([high, mid, low], axis=0), move, ((1,), (0,)))
        moved = moved[:rank] + moved[rank:2 * rank] + moved[2 * rank:]
        for i in range(pieces):
            piece = moved[:, i * width:(i + 1) * width]
            parts = [piece[f * tall:(f + 1) * tall] for f in range(fold)]
            if fold * width < 128:
                parts.append(jnp.zeros((tall, 128 - fold * width), F32))
            hold[i] = jnp.concatenate(parts, axis=1)
        for p in range(pieces):
            outs[w][p * tall:(p + 1) * tall, :] = hold[me_node ^ reverse_bits(p, bits)]


def finish_kernel(scale, per_node, width_cols, count, inv_ref, piece_ref, *refs):
    both, high = refs[:count], refs[count:2 * count]
    low, core_ref, coef_ref = refs[2 * count:3 * count], refs[-2], refs[-1]
    rank = inv_ref.shape[0]
    inverse = inv_ref[...]
    at = 0
    for c in range(count):
        s = both[c][:rank, :].astype(F32) + both[c][rank:, :].astype(F32)
        rows = s.shape[1]
        s = s + (high[c][...].astype(F32) + low[c][...].astype(F32))
        core_ref[:, at:at + rows] = dot(inverse, s, ((1,), (0,)), HI)
        at += rows
    width = per_node * width_cols
    fold = folding(rank, width)
    total = piece_ref[...]
    total = jnp.concatenate([total[:, f * width:(f + 1) * width] for f in range(fold)], axis=0)
    out = dot(total, inverse, ((0,), (1,)), HI) * scale
    coef_ref[...] = jnp.concatenate(
        [out[p * width_cols:(p + 1) * width_cols, :] for p in range(per_node)], axis=1)


def finish(inverse, piece, both, high, low, scale, per_node, width_cols):
    rank = inverse.shape[0]
    count = len(both)
    rows = sum(v.shape[1] for v in high)
    return pl.pallas_call(
        functools.partial(finish_kernel, scale, per_node, width_cols, count),
        out_shape=(
            jax.ShapeDtypeStruct((rank, rows), F32),
            jax.ShapeDtypeStruct((width_cols, per_node * rank), F32),
        ),
        compiler_params=params(),
        cost_estimate=cost(12 * rank * rank * rows, 12 * rank * rows),
        name="finish",
    )(inverse, piece, *both, *high, *low)


def swap(value, axis, size, bit):
    return lax.ppermute(value, axis, [(i, i ^ bit) for i in range(size)])


def body(snapshots, sketch_matrix):
    rows_all = snapshots.shape[0]
    rank = sketch_matrix.shape[1]
    samp = lax.axis_size("samp")
    node = lax.axis_size("node")
    total = rows_all * node
    quarter = rows_all // samp
    me_s = lax.axis_index("samp").astype(jnp.int32)
    me_n = lax.axis_index("node").astype(jnp.int32)
    w_t = sketch_matrix.T
    last = samp // 2
    near = range(1, last)
    starts, sizes = (0, UNIT), (UNIT, quarter - UNIT)
    blocks = [(last, 0), (last, 1), (0, 0), (0, 1)]

    def block_of(base, c):
        return (me_s ^ base) * (quarter // UNIT) + starts[c] // UNIT

    borrowed = {b: [] for b in blocks}
    ws, w_at = [w_t], 0

    def borrow(chosen, after, w=None):
        out = ()
        for d in near:
            out = lend(jnp.stack([block_of(b[0] ^ d, b[1]) for b in chosen]), snapshots, UNIT, w, after)
            for b, v in zip(chosen, out):
                borrowed[b].append(swap(v, "samp", samp, d))
            after = tuple(out[:1])
        return after

    done = borrow(blocks[:1], (), w_t)
    for v in borrowed[blocks[0]]:
        w_at = v.shape[0] - rank
        ws.append(v)
    borrow(blocks[1:], done)

    pairs, arrived, done = {}, {}, ()
    ids = jnp.stack([block_of(*b) for b in blocks] + [me_n])
    slot = {b: k for k, b in enumerate(blocks)}
    for k, b in enumerate(blocks):
        later = ()
        numbers = [block_of(*b)] + [block_of(o[0] ^ d, o[1]) for o in later for d in near]
        out = sketch(jnp.stack(numbers), snapshots, ws, borrowed[b], UNIT, w_at, done)
        pairs[b], high = out[:2]
        done = (high,)
        if k + 1 < len(blocks):
            arrived[b[0] ^ last, b[1]] = swap(high, "samp", samp, last)
        for o in later:
            borrowed[o] = [swap(v, "samp", samp, d) for d, v in zip(near, out[2:])]
    own = [pairs[0, c] for c in range(2)]
    got_high = [arrived[0, c] for c in range(2)]

    def parts(chosen):
        return [(pairs[b], arrived[b], slot[b], borrowed[b]) for b in chosen]

    gram = own_gram(own[0], got_high[0], None, None)
    t = project(ids, parts([(0, 0)]), snapshots, None, [gram])
    if PLACE[3]:
        t, gram = lax.optimization_barrier((t, gram))
    gram = own_gram(own[1], got_high[1], gram, 1.0 / total, done)
    t = project(ids, parts([(0, 1)]), snapshots, t, [gram])
    final = blocks[-1]
    late = [(final[0] ^ last, final[1])]
    high, t = lax.optimization_barrier((high, t))
    arrived[late[0]] = swap(high, "samp", samp, last)
    gram = gram + swap(gram, "samp", samp, last)
    got_low = []
    for c in range(2):
        low, _ = lax.optimization_barrier((pairs[last, c][rank:], gram))
        got_low.append(swap(low, "samp", samp, last))
    t = project(ids, parts([(last, 0)]), snapshots, t, [gram] if PLACE[4] else ())
    gram, t = lax.optimization_barrier((gram, t))
    bit = last // 2
    while bit:
        gram = gram + swap(gram, "samp", samp, bit)
        bit //= 2
    per_node = P1 // node
    width_cols = P2 // samp
    tall = rank // folding(rank, per_node * width_cols)
    messages = project(
        ids, parts(late), snapshots, t, [column_order(snapshots.shape[1], samp, per_node, width_cols)] + ([gram] if PLACE[0] else []),
        functools.partial(tail, node, per_node, width_cols),
        [jax.ShapeDtypeStruct((node * tall, 128), F32)] * last,
        [pltpu.VMEM((node, tall, 128), F32)])

    pieces = messages[0]
    for d in near:
        pieces = pieces + swap(messages[d], "samp", samp, d)
    for k in range(node.bit_length() - 1):
        for c in range(2):
            if k == PLACE[1 + c]:
                pieces, got_low[c] = lax.optimization_barrier((pieces, got_low[c]))
        edge = pieces.shape[0] // 2
        got = swap(jnp.concatenate([pieces[edge:], gram], axis=0), "node", node, 1 << k)
        pieces, gram = pieces[:edge] + got[:edge], gram + got[edge:]
    spread = node // samp
    route = [
        (n * samp + s, (s * spread + n // samp) * samp + n % samp) for n in range(node) for s in range(samp)
    ]
    piece = lax.ppermute(pieces, ("node", "samp"), route)
    inverse = factor_inverse(gram, rank)
    core, coef = finish(inverse, piece, own, got_high, got_low, 1.0 / total, per_node, width_cols)
    return (core.T, coef.T)


def solution(mesh):
    placed = (P("node", "samp"), P("samp", None))
    return jax.shard_map(
        body,
        mesh=mesh,
        in_specs=placed,
        out_specs=(P(("node", "samp"), None), P("node", "samp")),
        check_vma=False,
    )
```

```python
import functools
import jax
import jax.numpy as jnp
import numpy as np
from jax import lax
from jax.experimental import pallas as pl
from jax.experimental.pallas import tpu as pltpu
from jax.sharding import PartitionSpec as P

P1 = 64
P2 = 32
BAND = 32
UNIT = 1024
LEND_STEPS = 2
PROJECT_ROWS = 512
PLACE = (False, 1, -1, True, False)
SKETCH_STEPS = 1
FACTOR_COST = 6e9
COST_CUT = 1
F32 = jnp.float32
BF16 = jnp.bfloat16
HI = lax.Precision.HIGHEST
UNREAD = pl.BlockSpec(memory_space=pl.ANY)
HELD = pl.BlockSpec(memory_space=pltpu.VMEM)
VMEM_LIMIT = 48 * 1024 * 1024


def iota(shape, dim):
    return lax.broadcasted_iota(jnp.int32, shape, dim)


def dot(a, b, dims, precision=None):
    return lax.dot_general(a, b, (dims, ((), ())), precision=precision, preferred_element_type=F32)


def params():
    return pltpu.CompilerParams(vmem_limit_bytes=VMEM_LIMIT)


def cost(flops, moved):
    return pl.CostEstimate(flops=int(flops) // COST_CUT, bytes_accessed=int(moved) // COST_CUT, transcendentals=0)


def lend_kernel(count, at, ids_ref, *refs):
    outs = refs[-count:]
    rows = refs[0].shape[0]
    for k in range(count):
        outs[k][:rows, :] = refs[k][...]
    if at is not None:
        outs[0][at:, :] = refs[count][...]


def lend(ids, x, size, w=None, after=()):
    count = ids.shape[0]
    depth = x.shape[1]
    steps = LEND_STEPS if w is None else 1
    rows = size // steps
    at, height, more, shapes = None, size, [], (rows, depth)
    if w is not None:
        rank = w.shape[0]
        at = -(-size // rank) * rank
        height = at + rank
        more, shapes = [w], (height, depth)
    return pl.pallas_call(
        functools.partial(lend_kernel, count, at),
        grid_spec=pltpu.PrefetchScalarGridSpec(
            num_scalar_prefetch=1,
            grid=(steps,),
            in_specs=[
                pl.BlockSpec((rows, depth), lambda i, ids, k=k: (ids[k] * steps + i, 0))
                for k in range(count)
            ] + [pl.BlockSpec(v.shape, lambda i, ids: (0, 0)) for v in more] + [UNREAD] * len(after),
            out_specs=[pl.BlockSpec(shapes, lambda i, ids: (i, 0))] * count,
        ),
        out_shape=[jax.ShapeDtypeStruct((height, depth), BF16)] * count,
        compiler_params=params(),
        cost_estimate=cost(0, 4 * count * height * depth),
        name="lend",
    )(ids, *([x] * count), *more, *after)


def sketch_kernel(count, lent, ids_ref, x_ref, *refs):
    w_refs, x_refs = refs[:count], (x_ref,) + refs[count:2 * count - 1]
    both_ref, high_ref = refs[len(refs) - lent - 2:len(refs) - lent]
    rank = high_ref.shape[0]
    for k in range(lent):
        refs[len(refs) - lent + k][...] = refs[2 * count - 1 + k][...]
    s = None
    for w_ref, ref in zip(w_refs, x_refs):
        term = dot(w_ref[...], ref[...], ((1,), (1,)))
        s = term if s is None else s + term
    high = s.astype(BF16)
    high_ref[...] = high
    both_ref[:rank, :] = high
    both_ref[rank:, :] = (s - high.astype(F32)).astype(BF16)


def sketch(ids, x, ws, extra, size, w_at, after=()):
    rank, depth = ws[0].shape
    count = len(ws)
    lent = ids.shape[0] - 1
    steps = SKETCH_STEPS
    rows = size // steps
    return pl.pallas_call(
        functools.partial(sketch_kernel, count, lent),
        grid_spec=pltpu.PrefetchScalarGridSpec(
            num_scalar_prefetch=1,
            grid=(steps,),
            in_specs=[pl.BlockSpec((rows, depth), lambda i, ids: (ids[0] * steps + i, 0))]
            + [pl.BlockSpec((rank, depth), lambda i, ids: (0, 0))]
            + [pl.BlockSpec((rank, depth), lambda i, ids: (w_at // rank, 0))] * (count - 1)
            + [pl.BlockSpec((rows, depth), lambda i, ids: (i, 0))] * (count - 1)
            + [pl.BlockSpec((rows, depth), lambda i, ids, k=k: (ids[1 + k] * steps + i, 0)) for k in range(lent)]
            + [UNREAD] * len(after),
            out_specs=[
                pl.BlockSpec((2 * rank, rows), lambda i, ids: (0, i)),
                pl.BlockSpec((rank, rows), lambda i, ids: (0, i)),
            ] + [pl.BlockSpec((rows, depth), lambda i, ids: (i, 0))] * lent,
        ),
        out_shape=[
            jax.ShapeDtypeStruct((2 * rank, size), BF16),
            jax.ShapeDtypeStruct((rank, size), BF16),
        ] + [jax.ShapeDtypeStruct((size, depth), BF16)] * lent,
        compiler_params=params(),
        cost_estimate=cost(
            2 * rank * depth * size * count, size * (depth * 2 * (count + 2 * lent) + rank * 6)),
        name="sketch",
    )(ids, x, *ws, *extra, *([x] * lent), *after)


def packing(rank):
    bands = rank // BAND
    pairs = [(i, j) for i in range(bands) for j in range(i, bands)]
    wide = 128 // BAND
    groups = -(-len(pairs) // wide)
    groups += groups % 2
    return pairs, wide, groups


def pack_gram(gram):
    pairs, wide, groups = packing(gram.shape[0])
    out = []
    for g in range(groups):
        chosen = pairs[g * wide:(g + 1) * wide]
        parts = [gram[i * BAND:(i + 1) * BAND, j * BAND:(j + 1) * BAND] for i, j in chosen]
        parts += [jnp.zeros((BAND, BAND), F32)] * (wide - len(chosen))
        out.append(jnp.concatenate(parts, axis=1))
    return jnp.concatenate(out, axis=0)


def fold_square(x, rank):
    return (x[:rank, :rank] + x[rank:, rank:]) + (x[:rank, rank:] + x[rank:, :rank])


def gram_kernel(scale, has_base, own_ref, got_ref, *refs):
    o_ref = refs[-1]
    rank = got_ref.shape[0]
    s = own_ref[:rank, :].astype(F32) + own_ref[rank:, :].astype(F32) + got_ref[...].astype(F32)
    high = s.astype(BF16)
    both = jnp.concatenate([high, (s - high.astype(F32)).astype(BF16)], axis=0)
    total = fold_square(dot(both, both, ((1,), (1,))), rank)
    if has_base:
        total = total + refs[0][...]
    o_ref[...] = total if scale is None else pack_gram(total * scale)


def own_gram(own, got, base, scale, after=()):
    rank, rows = got.shape
    bases = [] if base is None else [base]
    shape = (rank, rank) if scale is None else (packing(rank)[2] * BAND, 128)
    return pl.pallas_call(
        functools.partial(gram_kernel, scale, len(bases)),
        in_specs=[HELD] * (2 + len(bases)) + [UNREAD] * len(after),
        out_shape=jax.ShapeDtypeStruct(shape, F32),
        compiler_params=params(),
        cost_estimate=cost(8 * rank * rank * rows, 6 * rank * rows),
        name="gram",
    )(own, got, *bases, *after)


def wide_lanes(x, n):
    reps = -(-n // 128)
    return jnp.concatenate([x] * reps, axis=1)[:, :n] if reps > 1 else x[:, :n]


def band_rows(block, b):
    n = block.shape[1]
    count = BAND // 8
    part = [block[8 * i:8 * i + 8, :] for i in range(count)]
    sub = iota((8, n), 0)
    lane = iota((8, n), 1)
    for m in range(count):
        c0 = b * BAND + 8 * m
        live = count - m
        col = [
            [jnp.broadcast_to(part[m + i][:, c0 + k:c0 + k + 1], (8, 128)) for i in range(live)]
            for k in range(8)
        ]
        here = (lane >= c0) & (lane < c0 + 8)
        part[m] = jnp.where(here, jnp.where(lane - c0 == sub, 1.0, 0.0), part[m])
        for i in range(1, live):
            part[m + i] = jnp.where(here, 0.0, part[m + i])
        for j in range(8):
            inv_root = lax.rsqrt(jnp.broadcast_to(col[j][0][j:j + 1, :], (8, 128)))
            low = [x * inv_root for x in col[j]]
            for k in range(j + 1, 8):
                t = jnp.broadcast_to(low[0][k:k + 1, :], (8, 128))
                for i in range(live):
                    col[k][i] = col[k][i] - low[i] * t
            row = jnp.broadcast_to(part[m][j:j + 1, :], (8, n)) * wide_lanes(inv_root, n)
            for i in range(live):
                new = part[m + i] - wide_lanes(low[i], n) * row
                if i == 0:
                    new = jnp.where(sub > j, new, jnp.where(sub == j, row, part[m]))
                part[m + i] = new
    return jnp.concatenate(part, axis=0)


def factor_kernel(rank, g_ref, *refs):
    o_ref = refs[-1]
    pairs, wide, _ = packing(rank)
    o_ref[...] = jnp.zeros((rank, rank), F32)
    for at, (i, j) in enumerate(pairs):
        g, k = at // wide, at % wide
        o_ref[i * BAND:(i + 1) * BAND, j * BAND:(j + 1) * BAND] = g_ref[
            g * BAND:(g + 1) * BAND, k * BAND:(k + 1) * BAND]
    for b in range(rank // BAND):
        lo, hi = b * BAND, (b + 1) * BAND
        r = band_rows(o_ref[lo:hi, :], b)
        rows, cols = iota(r.shape, 0), iota(r.shape, 1)
        r = jnp.where((cols >= lo) & (cols < hi) & (cols - lo > rows), 0.0, r)
        o_ref[lo:hi, :] = jnp.where(cols < hi, r, 0.0)
        if hi < rank:
            left = jnp.where(cols >= hi, r, 0.0)
            update = dot(left, r, ((0,), (0,)), HI)
            kept = jnp.where(iota((rank - hi, rank), 1) // BAND == b, 0.0, o_ref[hi:, :])
            o_ref[hi:, :] = kept - update[hi:, :]


def factor_inverse(packed, rank, after=()):
    return pl.pallas_call(
        functools.partial(factor_kernel, rank),
        in_specs=[HELD] + [UNREAD] * len(after),
        out_shape=jax.ShapeDtypeStruct((rank, rank), F32),
        compiler_params=params(),
        cost_estimate=cost(FACTOR_COST, 4 * rank * rank),
        name="factor",
    )(packed, *after)


def project_kernel(count, wide, has_base, aside, finish, ids_ref, *refs):
    pair_refs, high_refs, x_refs = refs[:count], refs[count:2 * count], refs[2 * count:count * (2 + wide)]
    at = count * (2 + wide)
    beside = refs[at + has_base:at + has_base + aside]
    rest = refs[at + has_base + aside:]
    t_ref = rest[-1]
    rank = t_ref.shape[1]

    @pl.when(pl.program_id(0) == 0)
    def _():
        t_ref[...] = refs[at][...] if has_base else jnp.zeros_like(t_ref)

    sums = []
    for pair_ref, high_ref in zip(pair_refs, high_refs):
        s = pair_ref[:rank, :].astype(F32) + pair_ref[rank:, :].astype(F32) + high_ref[...].astype(F32)
        high = s.astype(BF16)
        sums.append(jnp.concatenate([high, (s - high.astype(F32)).astype(BF16)], axis=0))
    for w in range(wide):
        total = None
        for k in range(count):
            term = dot(sums[k], x_refs[w * count + k][...], ((1,), (0,)))
            total = term if total is None else total + term
        t_ref[w] += total[:rank] + total[rank:]
    if finish is not None:
        @pl.when(pl.program_id(0) == pl.num_programs(0) - 1)
        def _():
            finish(t_ref, ids_ref, beside, *rest[:-1])


def project(ids, work, x, base, beside=(), finish=None, outs=(), scratch=()):
    count = len(work)
    wide = 1 + len(work[0][3])
    rank, span = work[0][1].shape
    depth = x.shape[1]
    rows = min(span, PROJECT_ROWS)
    steps = span // rows
    bases = [] if base is None else [base]
    whole = pl.BlockSpec((wide, rank, depth), lambda i, ids: (0, 0, 0))
    t_shape = jax.ShapeDtypeStruct((wide, rank, depth), F32)
    if finish is None:
        out_specs, out_shape, scratch_shapes = whole, t_shape, []
    else:
        out_specs = [pl.BlockSpec(o.shape, lambda i, ids: (0, 0)) for o in outs]
        out_shape = list(outs)
        scratch_shapes = list(scratch) + [pltpu.VMEM((wide, rank, depth), F32)]
    return pl.pallas_call(
        functools.partial(project_kernel, count, wide, len(bases), len(beside), finish),
        grid_spec=pltpu.PrefetchScalarGridSpec(
            num_scalar_prefetch=1,
            grid=(steps,),
            in_specs=[pl.BlockSpec((2 * rank, rows), lambda i, ids: (0, i))] * count
            + [pl.BlockSpec((rank, rows), lambda i, ids: (0, i))] * count
            + [
                pl.BlockSpec((rows, depth), lambda i, ids, slot=w[2]: (ids[slot] * steps + i, 0))
                for w in work
            ]
            + [pl.BlockSpec((rows, depth), lambda i, ids: (i, 0))] * (count * (wide - 1))
            + [whole] * len(bases) + [pl.BlockSpec(v.shape, lambda i, ids: (0, 0)) for v in beside],
            out_specs=out_specs,
            scratch_shapes=scratch_shapes,
        ),
        out_shape=out_shape,
        compiler_params=params(),
        cost_estimate=cost(
            4 * rank * depth * span * count * wide, span * count * (depth * wide + 3 * rank) * 2),
        name="project",
    )(
        ids, *[w[0] for w in work], *[w[1] for w in work], *([x] * count),
        *[w[3][d] for d in range(wide - 1) for w in work], *bases, *beside)


def folding(rank, width):
    best = 1
    for f in range(1, rank + 1):
        if rank % f == 0 and (rank // f) % 8 == 0 and f * width <= 128:
            best = f
    return best


def reverse_bits(p, count):
    return sum(1 << (count - 1 - b) for b in range(count) if (p >> b) & 1)


def column_order(depth, samp, per_node, width_cols):
    width = per_node * width_cols
    dst = np.arange(depth)
    a, rest = dst // (samp * width), dst % (samp * width)
    s, rest = rest // width, rest % width
    src = (a * per_node + rest // width_cols) * (samp * width_cols) + s * width_cols + rest % width_cols
    return jnp.asarray(np.arange(depth)[:, None] == src[None, :], BF16)


def tail(pieces, per_node, width_cols, t_ref, ids_ref, beside, *refs):
    outs, hold = refs[:-1], refs[-1]
    wide, rank, depth = t_ref.shape
    width = per_node * width_cols
    fold = folding(rank, width)
    tall = rank // fold
    me_node = ids_ref[ids_ref.shape[0] - 1]
    move = beside[0][...]
    bits = pieces.bit_length() - 1
    for w in range(wide):
        t = t_ref[w]
        high = t.astype(BF16)
        mid = (t - high.astype(F32)).astype(BF16)
        low = (t - high.astype(F32) - mid.astype(F32)).astype(BF16)
        moved = dot(jnp.concatenate([high, mid, low], axis=0), move, ((1,), (0,)))
        moved = moved[:rank] + moved[rank:2 * rank] + moved[2 * rank:]
        for i in range(pieces):
            piece = moved[:, i * width:(i + 1) * width]
            parts = [piece[f * tall:(f + 1) * tall] for f in range(fold)]
            if fold * width < 128:
                parts.append(jnp.zeros((tall, 128 - fold * width), F32))
            hold[i] = jnp.concatenate(parts, axis=1)
        for p in range(pieces):
            outs[w][p * tall:(p + 1) * tall, :] = hold[me_node ^ reverse_bits(p, bits)]


def finish_kernel(scale, per_node, width_cols, count, inv_ref, piece_ref, *refs):
    both, high = refs[:count], refs[count:2 * count]
    low, core_ref, coef_ref = refs[2 * count:3 * count], refs[-2], refs[-1]
    rank = inv_ref.shape[0]
    inverse = inv_ref[...]
    at = 0
    for c in range(count):
        s = both[c][:rank, :].astype(F32) + both[c][rank:, :].astype(F32)
        rows = s.shape[1]
        s = s + (high[c][...].astype(F32) + low[c][...].astype(F32))
        core_ref[:, at:at + rows] = dot(inverse, s, ((1,), (0,)), HI)
        at += rows
    width = per_node * width_cols
    fold = folding(rank, width)
    total = piece_ref[...]
    total = jnp.concatenate([total[:, f * width:(f + 1) * width] for f in range(fold)], axis=0)
    out = dot(total, inverse, ((0,), (1,)), HI) * scale
    coef_ref[...] = jnp.concatenate(
        [out[p * width_cols:(p + 1) * width_cols, :] for p in range(per_node)], axis=1)


def finish(inverse, piece, both, high, low, scale, per_node, width_cols):
    rank = inverse.shape[0]
    count = len(both)
    rows = sum(v.shape[1] for v in high)
    return pl.pallas_call(
        functools.partial(finish_kernel, scale, per_node, width_cols, count),
        out_shape=(
            jax.ShapeDtypeStruct((rank, rows), F32),
            jax.ShapeDtypeStruct((width_cols, per_node * rank), F32),
        ),
        compiler_params=params(),
        cost_estimate=cost(12 * rank * rank * rows, 12 * rank * rows),
        name="finish",
    )(inverse, piece, *both, *high, *low)


def swap(value, axis, size, bit):
    return lax.ppermute(value, axis, [(i, i ^ bit) for i in range(size)])


def body(snapshots, sketch_matrix):
    rows_all = snapshots.shape[0]
    rank = sketch_matrix.shape[1]
    samp = lax.axis_size("samp")
    node = lax.axis_size("node")
    total = rows_all * node
    quarter = rows_all // samp
    me_s = lax.axis_index("samp").astype(jnp.int32)
    me_n = lax.axis_index("node").astype(jnp.int32)
    w_t = sketch_matrix.T
    last = samp // 2
    near = range(1, last)
    starts, sizes = (0, UNIT), (UNIT, quarter - UNIT)
    blocks = [(last, 0), (last, 1), (0, 0), (0, 1)]

    def block_of(base, c):
        return (me_s ^ base) * (quarter // UNIT) + starts[c] // UNIT

    borrowed = {b: [] for b in blocks}
    ws, w_at = [w_t], 0

    def borrow(chosen, after, w=None):
        out = ()
        for d in near:
            out = lend(jnp.stack([block_of(b[0] ^ d, b[1]) for b in chosen]), snapshots, UNIT, w, after)
            for b, v in zip(chosen, out):
                borrowed[b].append(swap(v, "samp", samp, d))
            after = tuple(out[:1])
        return after

    done = borrow(blocks[:1], (), w_t)
    for v in borrowed[blocks[0]]:
        w_at = v.shape[0] - rank
        ws.append(v)
    borrow(blocks[1:], done)

    pairs, arrived, done = {}, {}, ()
    ids = jnp.stack([block_of(*b) for b in blocks] + [me_n])
    slot = {b: k for k, b in enumerate(blocks)}
    for k, b in enumerate(blocks):
        later = ()
        numbers = [block_of(*b)] + [block_of(o[0] ^ d, o[1]) for o in later for d in near]
        out = sketch(jnp.stack(numbers), snapshots, ws, borrowed[b], UNIT, w_at, done)
        pairs[b], high = out[:2]
        done = (high,)
        if k + 1 < len(blocks):
            arrived[b[0] ^ last, b[1]] = swap(high, "samp", samp, last)
        for o in later:
            borrowed[o] = [swap(v, "samp", samp, d) for d, v in zip(near, out[2:])]
    own = [pairs[0, c] for c in range(2)]
    got_high = [arrived[0, c] for c in range(2)]

    def parts(chosen):
        return [(pairs[b], arrived[b], slot[b], borrowed[b]) for b in chosen]

    gram = own_gram(own[0], got_high[0], None, None)
    t = project(ids, parts([(0, 0)]), snapshots, None, [gram])
    if PLACE[3]:
        t, gram = lax.optimization_barrier((t, gram))
    gram = own_gram(own[1], got_high[1], gram, 1.0 / total, done)
    t = project(ids, parts([(0, 1)]), snapshots, t, [gram])
    final = blocks[-1]
    late = [(final[0] ^ last, final[1])]
    high, t = lax.optimization_barrier((high, t))
    arrived[late[0]] = swap(high, "samp", samp, last)
    gram = gram + swap(gram, "samp", samp, last)
    got_low = []
    for c in range(2):
        low, _ = lax.optimization_barrier((pairs[last, c][rank:], gram))
        got_low.append(swap(low, "samp", samp, last))
    t = project(ids, parts([(last, 0)]), snapshots, t, [gram] if PLACE[4] else ())
    gram, t = lax.optimization_barrier((gram, t))
    bit = last // 2
    while bit:
        gram = gram + swap(gram, "samp", samp, bit)
        bit //= 2
    per_node = P1 // node
    width_cols = P2 // samp
    tall = rank // folding(rank, per_node * width_cols)
    messages = project(
        ids, parts(late), snapshots, t, [column_order(snapshots.shape[1], samp, per_node, width_cols)] + ([gram] if PLACE[0] else []),
        functools.partial(tail, node, per_node, width_cols),
        [jax.ShapeDtypeStruct((node * tall, 128), F32)] * last,
        [pltpu.VMEM((node, tall, 128), F32)])

    pieces = messages[0]
    for d in near:
        pieces = pieces + swap(messages[d], "samp", samp, d)
    for k in range(node.bit_length() - 1):
        for c in range(2):
            if k == PLACE[1 + c]:
                pieces, got_low[c] = lax.optimization_barrier((pieces, got_low[c]))
        edge = pieces.shape[0] // 2
        got = swap(jnp.concatenate([pieces[edge:], gram], axis=0), "node", node, 1 << k)
        pieces, gram = pieces[:edge] + got[:edge], gram + got[edge:]
    spread = node // samp
    route = [
        (n * samp + s, (s * spread + n // samp) * samp + n % samp) for n in range(node) for s in range(samp)
    ]
    piece = lax.ppermute(pieces, ("node", "samp"), route)
    inverse = factor_inverse(gram, rank)
    core, coef = finish(inverse, piece, own, got_high, got_low, 1.0 / total, per_node, width_cols)
    return (core.T, coef.T)


def solution(mesh):
    placed = (P("node", "samp"), P("samp", None))
    return jax.shard_map(
        body,
        mesh=mesh,
        in_specs=placed,
        out_specs=(P(("node", "samp"), None), P("node", "samp")),
        check_vma=False,
    )
```

```python
import functools
import jax
import jax.numpy as jnp
import numpy as np
from jax import lax
from jax.experimental import pallas as pl
from jax.experimental.pallas import tpu as pltpu
from jax.sharding import PartitionSpec as P

P1 = 64
P2 = 32
BAND = 32
UNIT = 1024
LEND_STEPS = 2
PROJECT_ROWS = 512
PLACE = (False, 1, -1, True, False)
SKETCH_STEPS = 2
FACTOR_COST = 6e9
COST_CUT = 1
F32 = jnp.float32
BF16 = jnp.bfloat16
HI = lax.Precision.HIGHEST
UNREAD = pl.BlockSpec(memory_space=pl.ANY)
HELD = pl.BlockSpec(memory_space=pltpu.VMEM)
VMEM_LIMIT = 48 * 1024 * 1024


def iota(shape, dim):
    return lax.broadcasted_iota(jnp.int32, shape, dim)


def dot(a, b, dims, precision=None):
    return lax.dot_general(a, b, (dims, ((), ())), precision=precision, preferred_element_type=F32)


def params():
    return pltpu.CompilerParams(vmem_limit_bytes=VMEM_LIMIT)


def cost(flops, moved):
    return pl.CostEstimate(flops=int(flops) // COST_CUT, bytes_accessed=int(moved) // COST_CUT, transcendentals=0)


def lend_kernel(count, at, ids_ref, *refs):
    outs = refs[-count:]
    rows = refs[0].shape[0]
    for k in range(count):
        outs[k][:rows, :] = refs[k][...]
    if at is not None:
        outs[0][at:, :] = refs[count][...]


def lend(ids, x, size, w=None, after=()):
    count = ids.shape[0]
    depth = x.shape[1]
    steps = LEND_STEPS if w is None else 1
    rows = size // steps
    at, height, more, shapes = None, size, [], (rows, depth)
    if w is not None:
        rank = w.shape[0]
        at = -(-size // rank) * rank
        height = at + rank
        more, shapes = [w], (height, depth)
    return pl.pallas_call(
        functools.partial(lend_kernel, count, at),
        grid_spec=pltpu.PrefetchScalarGridSpec(
            num_scalar_prefetch=1,
            grid=(steps,),
            in_specs=[
                pl.BlockSpec((rows, depth), lambda i, ids, k=k: (ids[k] * steps + i, 0))
                for k in range(count)
            ] + [pl.BlockSpec(v.shape, lambda i, ids: (0, 0)) for v in more] + [UNREAD] * len(after),
            out_specs=[pl.BlockSpec(shapes, lambda i, ids: (i, 0))] * count,
        ),
        out_shape=[jax.ShapeDtypeStruct((height, depth), BF16)] * count,
        compiler_params=params(),
        cost_estimate=cost(0, 4 * count * height * depth),
        name="lend",
    )(ids, *([x] * count), *more, *after)


def sketch_kernel(count, lent, ids_ref, x_ref, *refs):
    w_refs, x_refs = refs[:count], (x_ref,) + refs[count:2 * count - 1]
    both_ref, high_ref = refs[len(refs) - lent - 2:len(refs) - lent]
    rank = high_ref.shape[0]
    for k in range(lent):
        refs[len(refs) - lent + k][...] = refs[2 * count - 1 + k][...]
    s = None
    for w_ref, ref in zip(w_refs, x_refs):
        term = dot(w_ref[...], ref[...], ((1,), (1,)))
        s = term if s is None else s + term
    high = s.astype(BF16)
    high_ref[...] = high
    both_ref[:rank, :] = high
    both_ref[rank:, :] = (s - high.astype(F32)).astype(BF16)


def sketch(ids, x, ws, extra, size, w_at, after=()):
    rank, depth = ws[0].shape
    count = len(ws)
    lent = ids.shape[0] - 1
    steps = SKETCH_STEPS
    rows = size // steps
    return pl.pallas_call(
        functools.partial(sketch_kernel, count, lent),
        grid_spec=pltpu.PrefetchScalarGridSpec(
            num_scalar_prefetch=1,
            grid=(steps,),
            in_specs=[pl.BlockSpec((rows, depth), lambda i, ids: (ids[0] * steps + i, 0))]
            + [pl.BlockSpec((rank, depth), lambda i, ids: (0, 0))]
            + [pl.BlockSpec((rank, depth), lambda i, ids: (w_at // rank, 0))] * (count - 1)
            + [pl.BlockSpec((rows, depth), lambda i, ids: (i, 0))] * (count - 1)
            + [pl.BlockSpec((rows, depth), lambda i, ids, k=k: (ids[1 + k] * steps + i, 0)) for k in range(lent)]
            + [UNREAD] * len(after),
            out_specs=[
                pl.BlockSpec((2 * rank, rows), lambda i, ids: (0, i)),
                pl.BlockSpec((rank, rows), lambda i, ids: (0, i)),
            ] + [pl.BlockSpec((rows, depth), lambda i, ids: (i, 0))] * lent,
        ),
        out_shape=[
            jax.ShapeDtypeStruct((2 * rank, size), BF16),
            jax.ShapeDtypeStruct((rank, size), BF16),
        ] + [jax.ShapeDtypeStruct((size, depth), BF16)] * lent,
        compiler_params=params(),
        cost_estimate=cost(
            2 * rank * depth * size * count, size * (depth * 2 * (count + 2 * lent) + rank * 6)),
        name="sketch",
    )(ids, x, *ws, *extra, *([x] * lent), *after)


def packing(rank):
    bands = rank // BAND
    pairs = [(i, j) for i in range(bands) for j in range(i, bands)]
    wide = 128 // BAND
    groups = -(-len(pairs) // wide)
    groups += groups % 2
    return pairs, wide, groups


def pack_gram(gram):
    pairs, wide, groups = packing(gram.shape[0])
    out = []
    for g in range(groups):
        chosen = pairs[g * wide:(g + 1) * wide]
        parts = [gram[i * BAND:(i + 1) * BAND, j * BAND:(j + 1) * BAND] for i, j in chosen]
        parts += [jnp.zeros((BAND, BAND), F32)] * (wide - len(chosen))
        out.append(jnp.concatenate(parts, axis=1))
    return jnp.concatenate(out, axis=0)


def fold_square(x, rank):
    return (x[:rank, :rank] + x[rank:, rank:]) + (x[:rank, rank:] + x[rank:, :rank])


def gram_kernel(scale, has_base, own_ref, got_ref, *refs):
    o_ref = refs[-1]
    rank = got_ref.shape[0]
    s = own_ref[:rank, :].astype(F32) + own_ref[rank:, :].astype(F32) + got_ref[...].astype(F32)
    high = s.astype(BF16)
    both = jnp.concatenate([high, (s - high.astype(F32)).astype(BF16)], axis=0)
    total = fold_square(dot(both, both, ((1,), (1,))), rank)
    if has_base:
        total = total + refs[0][...]
    o_ref[...] = total if scale is None else pack_gram(total * scale)


def own_gram(own, got, base, scale, after=()):
    rank, rows = got.shape
    bases = [] if base is None else [base]
    shape = (rank, rank) if scale is None else (packing(rank)[2] * BAND, 128)
    return pl.pallas_call(
        functools.partial(gram_kernel, scale, len(bases)),
        in_specs=[HELD] * (2 + len(bases)) + [UNREAD] * len(after),
        out_shape=jax.ShapeDtypeStruct(shape, F32),
        compiler_params=params(),
        cost_estimate=cost(8 * rank * rank * rows, 6 * rank * rows),
        name="gram",
    )(own, got, *bases, *after)


def wide_lanes(x, n):
    reps = -(-n // 128)
    return jnp.concatenate([x] * reps, axis=1)[:, :n] if reps > 1 else x[:, :n]


def band_rows(block, b):
    n = block.shape[1]
    count = BAND // 8
    part = [block[8 * i:8 * i + 8, :] for i in range(count)]
    sub = iota((8, n), 0)
    lane = iota((8, n), 1)
    for m in range(count):
        c0 = b * BAND + 8 * m
        live = count - m
        col = [
            [jnp.broadcast_to(part[m + i][:, c0 + k:c0 + k + 1], (8, 128)) for i in range(live)]
            for k in range(8)
        ]
        here = (lane >= c0) & (lane < c0 + 8)
        part[m] = jnp.where(here, jnp.where(lane - c0 == sub, 1.0, 0.0), part[m])
        for i in range(1, live):
            part[m + i] = jnp.where(here, 0.0, part[m + i])
        for j in range(8):
            inv_root = lax.rsqrt(jnp.broadcast_to(col[j][0][j:j + 1, :], (8, 128)))
            low = [x * inv_root for x in col[j]]
            for k in range(j + 1, 8):
                t = jnp.broadcast_to(low[0][k:k + 1, :], (8, 128))
                for i in range(live):
                    col[k][i] = col[k][i] - low[i] * t
            row = jnp.broadcast_to(part[m][j:j + 1, :], (8, n)) * wide_lanes(inv_root, n)
            for i in range(live):
                new = part[m + i] - wide_lanes(low[i], n) * row
                if i == 0:
                    new = jnp.where(sub > j, new, jnp.where(sub == j, row, part[m]))
                part[m + i] = new
    return jnp.concatenate(part, axis=0)


def factor_kernel(rank, g_ref, *refs):
    o_ref = refs[-1]
    pairs, wide, _ = packing(rank)
    o_ref[...] = jnp.zeros((rank, rank), F32)
    for at, (i, j) in enumerate(pairs):
        g, k = at // wide, at % wide
        o_ref[i * BAND:(i + 1) * BAND, j * BAND:(j + 1) * BAND] = g_ref[
            g * BAND:(g + 1) * BAND, k * BAND:(k + 1) * BAND]
    for b in range(rank // BAND):
        lo, hi = b * BAND, (b + 1) * BAND
        r = band_rows(o_ref[lo:hi, :], b)
        rows, cols = iota(r.shape, 0), iota(r.shape, 1)
        r = jnp.where((cols >= lo) & (cols < hi) & (cols - lo > rows), 0.0, r)
        o_ref[lo:hi, :] = jnp.where(cols < hi, r, 0.0)
        if hi < rank:
            left = jnp.where(cols >= hi, r, 0.0)
            update = dot(left, r, ((0,), (0,)), HI)
            kept = jnp.where(iota((rank - hi, rank), 1) // BAND == b, 0.0, o_ref[hi:, :])
            o_ref[hi:, :] = kept - update[hi:, :]


def factor_inverse(packed, rank, after=()):
    return pl.pallas_call(
        functools.partial(factor_kernel, rank),
        in_specs=[HELD] + [UNREAD] * len(after),
        out_shape=jax.ShapeDtypeStruct((rank, rank), F32),
        compiler_params=params(),
        cost_estimate=cost(FACTOR_COST, 4 * rank * rank),
        name="factor",
    )(packed, *after)


def project_kernel(count, wide, has_base, aside, finish, ids_ref, *refs):
    pair_refs, high_refs, x_refs = refs[:count], refs[count:2 * count], refs[2 * count:count * (2 + wide)]
    at = count * (2 + wide)
    beside = refs[at + has_base:at + has_base + aside]
    rest = refs[at + has_base + aside:]
    t_ref = rest[-1]
    rank = t_ref.shape[1]

    @pl.when(pl.program_id(0) == 0)
    def _():
        t_ref[...] = refs[at][...] if has_base else jnp.zeros_like(t_ref)

    sums = []
    for pair_ref, high_ref in zip(pair_refs, high_refs):
        s = pair_ref[:rank, :].astype(F32) + pair_ref[rank:, :].astype(F32) + high_ref[...].astype(F32)
        high = s.astype(BF16)
        sums.append(jnp.concatenate([high, (s - high.astype(F32)).astype(BF16)], axis=0))
    for w in range(wide):
        total = None
        for k in range(count):
            term = dot(sums[k], x_refs[w * count + k][...], ((1,), (0,)))
            total = term if total is None else total + term
        t_ref[w] += total[:rank] + total[rank:]
    if finish is not None:
        @pl.when(pl.program_id(0) == pl.num_programs(0) - 1)
        def _():
            finish(t_ref, ids_ref, beside, *rest[:-1])


def project(ids, work, x, base, beside=(), finish=None, outs=(), scratch=()):
    count = len(work)
    wide = 1 + len(work[0][3])
    rank, span = work[0][1].shape
    depth = x.shape[1]
    rows = min(span, PROJECT_ROWS)
    steps = span // rows
    bases = [] if base is None else [base]
    whole = pl.BlockSpec((wide, rank, depth), lambda i, ids: (0, 0, 0))
    t_shape = jax.ShapeDtypeStruct((wide, rank, depth), F32)
    if finish is None:
        out_specs, out_shape, scratch_shapes = whole, t_shape, []
    else:
        out_specs = [pl.BlockSpec(o.shape, lambda i, ids: (0, 0)) for o in outs]
        out_shape = list(outs)
        scratch_shapes = list(scratch) + [pltpu.VMEM((wide, rank, depth), F32)]
    return pl.pallas_call(
        functools.partial(project_kernel, count, wide, len(bases), len(beside), finish),
        grid_spec=pltpu.PrefetchScalarGridSpec(
            num_scalar_prefetch=1,
            grid=(steps,),
            in_specs=[pl.BlockSpec((2 * rank, rows), lambda i, ids: (0, i))] * count
            + [pl.BlockSpec((rank, rows), lambda i, ids: (0, i))] * count
            + [
                pl.BlockSpec((rows, depth), lambda i, ids, slot=w[2]: (ids[slot] * steps + i, 0))
                for w in work
            ]
            + [pl.BlockSpec((rows, depth), lambda i, ids: (i, 0))] * (count * (wide - 1))
            + [whole] * len(bases) + [pl.BlockSpec(v.shape, lambda i, ids: (0, 0)) for v in beside],
            out_specs=out_specs,
            scratch_shapes=scratch_shapes,
        ),
        out_shape=out_shape,
        compiler_params=params(),
        cost_estimate=cost(
            4 * rank * depth * span * count * wide, span * count * (depth * wide + 3 * rank) * 2),
        name="project",
    )(
        ids, *[w[0] for w in work], *[w[1] for w in work], *([x] * count),
        *[w[3][d] for d in range(wide - 1) for w in work], *bases, *beside)


def folding(rank, width):
    best = 1
    for f in range(1, rank + 1):
        if rank % f == 0 and (rank // f) % 8 == 0 and f * width <= 128:
            best = f
    return best


def reverse_bits(p, count):
    return sum(1 << (count - 1 - b) for b in range(count) if (p >> b) & 1)


def column_order(depth, samp, per_node, width_cols):
    width = per_node * width_cols
    dst = np.arange(depth)
    a, rest = dst // (samp * width), dst % (samp * width)
    s, rest = rest // width, rest % width
    src = (a * per_node + rest // width_cols) * (samp * width_cols) + s * width_cols + rest % width_cols
    return jnp.asarray(np.arange(depth)[:, None] == src[None, :], BF16)


def tail(pieces, per_node, width_cols, t_ref, ids_ref, beside, *refs):
    outs, hold = refs[:-1], refs[-1]
    wide, rank, depth = t_ref.shape
    width = per_node * width_cols
    fold = folding(rank, width)
    tall = rank // fold
    me_node = ids_ref[ids_ref.shape[0] - 1]
    move = beside[0][...]
    bits = pieces.bit_length() - 1
    for w in range(wide):
        t = t_ref[w]
        high = t.astype(BF16)
        mid = (t - high.astype(F32)).astype(BF16)
        low = (t - high.astype(F32) - mid.astype(F32)).astype(BF16)
        moved = dot(jnp.concatenate([high, mid, low], axis=0), move, ((1,), (0,)))
        moved = moved[:rank] + moved[rank:2 * rank] + moved[2 * rank:]
        for i in range(pieces):
            piece = moved[:, i * width:(i + 1) * width]
            parts = [piece[f * tall:(f + 1) * tall] for f in range(fold)]
            if fold * width < 128:
                parts.append(jnp.zeros((tall, 128 - fold * width), F32))
            hold[i] = jnp.concatenate(parts, axis=1)
        for p in range(pieces):
            outs[w][p * tall:(p + 1) * tall, :] = hold[me_node ^ reverse_bits(p, bits)]


def finish_kernel(scale, per_node, width_cols, count, inv_ref, piece_ref, *refs):
    both, high = refs[:count], refs[count:2 * count]
    low, core_ref, coef_ref = refs[2 * count:3 * count], refs[-2], refs[-1]
    rank = inv_ref.shape[0]
    inverse = inv_ref[...]
    at = 0
    for c in range(count):
        s = both[c][:rank, :].astype(F32) + both[c][rank:, :].astype(F32)
        rows = s.shape[1]
        s = s + (high[c][...].astype(F32) + low[c][...].astype(F32))
        core_ref[:, at:at + rows] = dot(inverse, s, ((1,), (0,)), HI)
        at += rows
    width = per_node * width_cols
    fold = folding(rank, width)
    total = piece_ref[...]
    total = jnp.concatenate([total[:, f * width:(f + 1) * width] for f in range(fold)], axis=0)
    out = dot(total, inverse, ((0,), (1,)), HI) * scale
    coef_ref[...] = jnp.concatenate(
        [out[p * width_cols:(p + 1) * width_cols, :] for p in range(per_node)], axis=1)


def finish(inverse, piece, both, high, low, scale, per_node, width_cols):
    rank = inverse.shape[0]
    count = len(both)
    rows = sum(v.shape[1] for v in high)
    return pl.pallas_call(
        functools.partial(finish_kernel, scale, per_node, width_cols, count),
        out_shape=(
            jax.ShapeDtypeStruct((rank, rows), F32),
            jax.ShapeDtypeStruct((width_cols, per_node * rank), F32),
        ),
        compiler_params=params(),
        cost_estimate=cost(12 * rank * rank * rows, 12 * rank * rows),
        name="finish",
    )(inverse, piece, *both, *high, *low)


def swap(value, axis, size, bit):
    return lax.ppermute(value, axis, [(i, i ^ bit) for i in range(size)])


def body(snapshots, sketch_matrix):
    rows_all = snapshots.shape[0]
    rank = sketch_matrix.shape[1]
    samp = lax.axis_size("samp")
    node = lax.axis_size("node")
    total = rows_all * node
    quarter = rows_all // samp
    me_s = lax.axis_index("samp").astype(jnp.int32)
    me_n = lax.axis_index("node").astype(jnp.int32)
    w_t = sketch_matrix.T
    last = samp // 2
    near = range(1, last)
    starts, sizes = (0, UNIT), (UNIT, quarter - UNIT)
    blocks = [(last, 0), (last, 1), (0, 0), (0, 1)]

    def block_of(base, c):
        return (me_s ^ base) * (quarter // UNIT) + starts[c] // UNIT

    borrowed = {b: [] for b in blocks}
    ws, w_at = [w_t], 0

    def borrow(chosen, after, w=None):
        out = ()
        for d in near:
            out = lend(jnp.stack([block_of(b[0] ^ d, b[1]) for b in chosen]), snapshots, UNIT, w, after)
            for b, v in zip(chosen, out):
                borrowed[b].append(swap(v, "samp", samp, d))
            after = tuple(out[:1])
        return after

    done = borrow(blocks[:1], (), w_t)
    for v in borrowed[blocks[0]]:
        w_at = v.shape[0] - rank
        ws.append(v)
    borrow(blocks[1:3], done)

    pairs, arrived, done = {}, {}, ()
    ids = jnp.stack([block_of(*b) for b in blocks] + [me_n])
    slot = {b: k for k, b in enumerate(blocks)}
    for k, b in enumerate(blocks):
        later = blocks[3:] if k == 0 else ()
        numbers = [block_of(*b)] + [block_of(o[0] ^ d, o[1]) for o in later for d in near]
        out = sketch(jnp.stack(numbers), snapshots, ws, borrowed[b], UNIT, w_at, done)
        pairs[b], high = out[:2]
        done = (high,)
        if k + 1 < len(blocks):
            arrived[b[0] ^ last, b[1]] = swap(high, "samp", samp, last)
        for o in later:
            borrowed[o] = [swap(v, "samp", samp, d) for d, v in zip(near, out[2:])]
    own = [pairs[0, c] for c in range(2)]
    got_high = [arrived[0, c] for c in range(2)]

    def parts(chosen):
        return [(pairs[b], arrived[b], slot[b], borrowed[b]) for b in chosen]

    gram = own_gram(own[0], got_high[0], None, None)
    t = project(ids, parts([(0, 0)]), snapshots, None, [gram])
    if PLACE[3]:
        t, gram = lax.optimization_barrier((t, gram))
    gram = own_gram(own[1], got_high[1], gram, 1.0 / total, done)
    t = project(ids, parts([(0, 1)]), snapshots, t, [gram])
    final = blocks[-1]
    late = [(final[0] ^ last, final[1])]
    high, t = lax.optimization_barrier((high, t))
    arrived[late[0]] = swap(high, "samp", samp, last)
    gram = gram + swap(gram, "samp", samp, last)
    got_low = []
    for c in range(2):
        low, _ = lax.optimization_barrier((pairs[last, c][rank:], gram))
        got_low.append(swap(low, "samp", samp, last))
    t = project(ids, parts([(last, 0)]), snapshots, t, [gram] if PLACE[4] else ())
    gram, t = lax.optimization_barrier((gram, t))
    bit = last // 2
    while bit:
        gram = gram + swap(gram, "samp", samp, bit)
        bit //= 2
    per_node = P1 // node
    width_cols = P2 // samp
    tall = rank // folding(rank, per_node * width_cols)
    messages = project(
        ids, parts(late), snapshots, t, [column_order(snapshots.shape[1], samp, per_node, width_cols)] + ([gram] if PLACE[0] else []),
        functools.partial(tail, node, per_node, width_cols),
        [jax.ShapeDtypeStruct((node * tall, 128), F32)] * last,
        [pltpu.VMEM((node, tall, 128), F32)])

    pieces = messages[0]
    for d in near:
        pieces = pieces + swap(messages[d], "samp", samp, d)
    for k in range(node.bit_length() - 1):
        for c in range(2):
            if k == PLACE[1 + c]:
                pieces, got_low[c] = lax.optimization_barrier((pieces, got_low[c]))
        edge = pieces.shape[0] // 2
        got = swap(jnp.concatenate([pieces[edge:], gram], axis=0), "node", node, 1 << k)
        pieces, gram = pieces[:edge] + got[:edge], gram + got[edge:]
    spread = node // samp
    route = [
        (n * samp + s, (s * spread + n // samp) * samp + n % samp) for n in range(node) for s in range(samp)
    ]
    piece = lax.ppermute(pieces, ("node", "samp"), route)
    inverse = factor_inverse(gram, rank)
    core, coef = finish(inverse, piece, own, got_high, got_low, 1.0 / total, per_node, width_cols)
    return (core.T, coef.T)


def solution(mesh):
    placed = (P("node", "samp"), P("samp", None))
    return jax.shard_map(
        body,
        mesh=mesh,
        in_specs=placed,
        out_specs=(P(("node", "samp"), None), P("node", "samp")),
        check_vma=False,
    )
```

```python
import functools
import jax
import jax.numpy as jnp
import numpy as np
from jax import lax
from jax.experimental import pallas as pl
from jax.experimental.pallas import tpu as pltpu
from jax.sharding import PartitionSpec as P

P1 = 64
P2 = 32
BAND = 32
UNIT = 1024
LEND_STEPS = 2
PROJECT_ROWS = 512
PLACE = (False, 1, -1, True, False)
SKETCH_STEPS = 1
FACTOR_COST = 6e9
COST_CUT = 1
F32 = jnp.float32
BF16 = jnp.bfloat16
HI = lax.Precision.HIGHEST
UNREAD = pl.BlockSpec(memory_space=pl.ANY)
HELD = pl.BlockSpec(memory_space=pltpu.VMEM)
VMEM_LIMIT = 48 * 1024 * 1024


def iota(shape, dim):
    return lax.broadcasted_iota(jnp.int32, shape, dim)


def dot(a, b, dims, precision=None):
    return lax.dot_general(a, b, (dims, ((), ())), precision=precision, preferred_element_type=F32)


def params():
    return pltpu.CompilerParams(vmem_limit_bytes=VMEM_LIMIT)


def cost(flops, moved):
    return pl.CostEstimate(flops=int(flops) // COST_CUT, bytes_accessed=int(moved) // COST_CUT, transcendentals=0)


def lend_kernel(count, at, ids_ref, *refs):
    outs = refs[-count:]
    rows = refs[0].shape[0]
    for k in range(count):
        outs[k][:rows, :] = refs[k][...]
    if at is not None:
        outs[0][at:, :] = refs[count][...]


def lend(ids, x, size, w=None, after=()):
    count = ids.shape[0]
    depth = x.shape[1]
    steps = LEND_STEPS if w is None else 1
    rows = size // steps
    at, height, more, shapes = None, size, [], (rows, depth)
    if w is not None:
        rank = w.shape[0]
        at = -(-size // rank) * rank
        height = at + rank
        more, shapes = [w], (height, depth)
    return pl.pallas_call(
        functools.partial(lend_kernel, count, at),
        grid_spec=pltpu.PrefetchScalarGridSpec(
            num_scalar_prefetch=1,
            grid=(steps,),
            in_specs=[
                pl.BlockSpec((rows, depth), lambda i, ids, k=k: (ids[k] * steps + i, 0))
                for k in range(count)
            ] + [pl.BlockSpec(v.shape, lambda i, ids: (0, 0)) for v in more] + [UNREAD] * len(after),
            out_specs=[pl.BlockSpec(shapes, lambda i, ids: (i, 0))] * count,
        ),
        out_shape=[jax.ShapeDtypeStruct((height, depth), BF16)] * count,
        compiler_params=params(),
        cost_estimate=cost(0, 4 * count * height * depth),
        name="lend",
    )(ids, *([x] * count), *more, *after)


def sketch_kernel(count, lent, ids_ref, x_ref, *refs):
    w_refs, x_refs = refs[:count], (x_ref,) + refs[count:2 * count - 1]
    both_ref, high_ref = refs[len(refs) - lent - 2:len(refs) - lent]
    rank = high_ref.shape[0]
    for k in range(lent):
        refs[len(refs) - lent + k][...] = refs[2 * count - 1 + k][...]
    s = None
    for w_ref, ref in zip(w_refs, x_refs):
        term = dot(w_ref[...], ref[...], ((1,), (1,)))
        s = term if s is None else s + term
    high = s.astype(BF16)
    high_ref[...] = high
    both_ref[:rank, :] = high
    both_ref[rank:, :] = (s - high.astype(F32)).astype(BF16)


def sketch(ids, x, ws, extra, size, w_at, after=()):
    rank, depth = ws[0].shape
    count = len(ws)
    lent = ids.shape[0] - 1
    steps = SKETCH_STEPS
    rows = size // steps
    return pl.pallas_call(
        functools.partial(sketch_kernel, count, lent),
        grid_spec=pltpu.PrefetchScalarGridSpec(
            num_scalar_prefetch=1,
            grid=(steps,),
            in_specs=[pl.BlockSpec((rows, depth), lambda i, ids: (ids[0] * steps + i, 0))]
            + [pl.BlockSpec((rank, depth), lambda i, ids: (0, 0))]
            + [pl.BlockSpec((rank, depth), lambda i, ids: (w_at // rank, 0))] * (count - 1)
            + [pl.BlockSpec((rows, depth), lambda i, ids: (i, 0))] * (count - 1)
            + [pl.BlockSpec((rows, depth), lambda i, ids, k=k: (ids[1 + k] * steps + i, 0)) for k in range(lent)]
            + [UNREAD] * len(after),
            out_specs=[
                pl.BlockSpec((2 * rank, rows), lambda i, ids: (0, i)),
                pl.BlockSpec((rank, rows), lambda i, ids: (0, i)),
            ] + [pl.BlockSpec((rows, depth), lambda i, ids: (i, 0))] * lent,
        ),
        out_shape=[
            jax.ShapeDtypeStruct((2 * rank, size), BF16),
            jax.ShapeDtypeStruct((rank, size), BF16),
        ] + [jax.ShapeDtypeStruct((size, depth), BF16)] * lent,
        compiler_params=params(),
        cost_estimate=cost(
            2 * rank * depth * size * count, size * (depth * 2 * (count + 2 * lent) + rank * 6)),
        name="sketch",
    )(ids, x, *ws, *extra, *([x] * lent), *after)


def packing(rank):
    bands = rank // BAND
    pairs = [(i, j) for i in range(bands) for j in range(i, bands)]
    wide = 128 // BAND
    groups = -(-len(pairs) // wide)
    groups += groups % 2
    return pairs, wide, groups


def pack_gram(gram):
    pairs, wide, groups = packing(gram.shape[0])
    out = []
    for g in range(groups):
        chosen = pairs[g * wide:(g + 1) * wide]
        parts = [gram[i * BAND:(i + 1) * BAND, j * BAND:(j + 1) * BAND] for i, j in chosen]
        parts += [jnp.zeros((BAND, BAND), F32)] * (wide - len(chosen))
        out.append(jnp.concatenate(parts, axis=1))
    return jnp.concatenate(out, axis=0)


def fold_square(x, rank):
    return (x[:rank, :rank] + x[rank:, rank:]) + (x[:rank, rank:] + x[rank:, :rank])


def gram_kernel(scale, has_base, own_ref, got_ref, *refs):
    o_ref = refs[-1]
    rank = got_ref.shape[0]
    s = own_ref[:rank, :].astype(F32) + own_ref[rank:, :].astype(F32) + got_ref[...].astype(F32)
    high = s.astype(BF16)
    both = jnp.concatenate([high, (s - high.astype(F32)).astype(BF16)], axis=0)
    total = fold_square(dot(both, both, ((1,), (1,))), rank)
    if has_base:
        total = total + refs[0][...]
    o_ref[...] = total if scale is None else pack_gram(total * scale)


def own_gram(own, got, base, scale, after=()):
    rank, rows = got.shape
    bases = [] if base is None else [base]
    shape = (rank, rank) if scale is None else (packing(rank)[2] * BAND, 128)
    return pl.pallas_call(
        functools.partial(gram_kernel, scale, len(bases)),
        in_specs=[HELD] * (2 + len(bases)) + [UNREAD] * len(after),
        out_shape=jax.ShapeDtypeStruct(shape, F32),
        compiler_params=params(),
        cost_estimate=cost(8 * rank * rank * rows, 6 * rank * rows),
        name="gram",
    )(own, got, *bases, *after)


def wide_lanes(x, n):
    reps = -(-n // 128)
    return jnp.concatenate([x] * reps, axis=1)[:, :n] if reps > 1 else x[:, :n]


def band_rows(block, b):
    n = block.shape[1]
    count = BAND // 8
    part = [block[8 * i:8 * i + 8, :] for i in range(count)]
    sub = iota((8, n), 0)
    lane = iota((8, n), 1)
    for m in range(count):
        c0 = b * BAND + 8 * m
        live = count - m
        col = [
            [jnp.broadcast_to(part[m + i][:, c0 + k:c0 + k + 1], (8, 128)) for i in range(live)]
            for k in range(8)
        ]
        here = (lane >= c0) & (lane < c0 + 8)
        part[m] = jnp.where(here, jnp.where(lane - c0 == sub, 1.0, 0.0), part[m])
        for i in range(1, live):
            part[m + i] = jnp.where(here, 0.0, part[m + i])
        for j in range(8):
            inv_root = lax.rsqrt(jnp.broadcast_to(col[j][0][j:j + 1, :], (8, 128)))
            low = [x * inv_root for x in col[j]]
            for k in range(j + 1, 8):
                t = jnp.broadcast_to(low[0][k:k + 1, :], (8, 128))
                for i in range(live):
                    col[k][i] = col[k][i] - low[i] * t
            row = jnp.broadcast_to(part[m][j:j + 1, :], (8, n)) * wide_lanes(inv_root, n)
            for i in range(live):
                new = part[m + i] - wide_lanes(low[i], n) * row
                if i == 0:
                    new = jnp.where(sub > j, new, jnp.where(sub == j, row, part[m]))
                part[m + i] = new
    return jnp.concatenate(part, axis=0)


def factor_kernel(rank, g_ref, *refs):
    o_ref = refs[-1]
    pairs, wide, _ = packing(rank)
    o_ref[...] = jnp.zeros((rank, rank), F32)
    for at, (i, j) in enumerate(pairs):
        g, k = at // wide, at % wide
        o_ref[i * BAND:(i + 1) * BAND, j * BAND:(j + 1) * BAND] = g_ref[
            g * BAND:(g + 1) * BAND, k * BAND:(k + 1) * BAND]
    for b in range(rank // BAND):
        lo, hi = b * BAND, (b + 1) * BAND
        r = band_rows(o_ref[lo:hi, :], b)
        rows, cols = iota(r.shape, 0), iota(r.shape, 1)
        r = jnp.where((cols >= lo) & (cols < hi) & (cols - lo > rows), 0.0, r)
        o_ref[lo:hi, :] = jnp.where(cols < hi, r, 0.0)
        if hi < rank:
            left = jnp.where(cols >= hi, r, 0.0)
            update = dot(left, r, ((0,), (0,)), HI)
            kept = jnp.where(iota((rank - hi, rank), 1) // BAND == b, 0.0, o_ref[hi:, :])
            o_ref[hi:, :] = kept - update[hi:, :]


def factor_inverse(packed, rank, after=()):
    return pl.pallas_call(
        functools.partial(factor_kernel, rank),
        in_specs=[HELD] + [UNREAD] * len(after),
        out_shape=jax.ShapeDtypeStruct((rank, rank), F32),
        compiler_params=params(),
        cost_estimate=cost(FACTOR_COST, 4 * rank * rank),
        name="factor",
    )(packed, *after)


def project_kernel(count, wide, has_base, aside, finish, ids_ref, *refs):
    pair_refs, high_refs, x_refs = refs[:count], refs[count:2 * count], refs[2 * count:count * (2 + wide)]
    at = count * (2 + wide)
    beside = refs[at + has_base:at + has_base + aside]
    rest = refs[at + has_base + aside:]
    t_ref = rest[-1]
    rank = t_ref.shape[1]

    @pl.when(pl.program_id(0) == 0)
    def _():
        t_ref[...] = refs[at][...] if has_base else jnp.zeros_like(t_ref)

    sums = []
    for pair_ref, high_ref in zip(pair_refs, high_refs):
        s = pair_ref[:rank, :].astype(F32) + pair_ref[rank:, :].astype(F32) + high_ref[...].astype(F32)
        high = s.astype(BF16)
        sums.append(jnp.concatenate([high, (s - high.astype(F32)).astype(BF16)], axis=0))
    for w in range(wide):
        total = None
        for k in range(count):
            term = dot(sums[k], x_refs[w * count + k][...], ((1,), (0,)))
            total = term if total is None else total + term
        t_ref[w] += total[:rank] + total[rank:]
    if finish is not None:
        @pl.when(pl.program_id(0) == pl.num_programs(0) - 1)
        def _():
            finish(t_ref, ids_ref, beside, *rest[:-1])


def project(ids, work, x, base, beside=(), finish=None, outs=(), scratch=()):
    count = len(work)
    wide = 1 + len(work[0][3])
    rank, span = work[0][1].shape
    depth = x.shape[1]
    rows = min(span, PROJECT_ROWS)
    steps = span // rows
    bases = [] if base is None else [base]
    whole = pl.BlockSpec((wide, rank, depth), lambda i, ids: (0, 0, 0))
    t_shape = jax.ShapeDtypeStruct((wide, rank, depth), F32)
    if finish is None:
        out_specs, out_shape, scratch_shapes = whole, t_shape, []
    else:
        out_specs = [pl.BlockSpec(o.shape, lambda i, ids: (0, 0)) for o in outs]
        out_shape = list(outs)
        scratch_shapes = list(scratch) + [pltpu.VMEM((wide, rank, depth), F32)]
    return pl.pallas_call(
        functools.partial(project_kernel, count, wide, len(bases), len(beside), finish),
        grid_spec=pltpu.PrefetchScalarGridSpec(
            num_scalar_prefetch=1,
            grid=(steps,),
            in_specs=[pl.BlockSpec((2 * rank, rows), lambda i, ids: (0, i))] * count
            + [pl.BlockSpec((rank, rows), lambda i, ids: (0, i))] * count
            + [
                pl.BlockSpec((rows, depth), lambda i, ids, slot=w[2]: (ids[slot] * steps + i, 0))
                for w in work
            ]
            + [pl.BlockSpec((rows, depth), lambda i, ids: (i, 0))] * (count * (wide - 1))
            + [whole] * len(bases) + [pl.BlockSpec(v.shape, lambda i, ids: (0, 0)) for v in beside],
            out_specs=out_specs,
            scratch_shapes=scratch_shapes,
        ),
        out_shape=out_shape,
        compiler_params=params(),
        cost_estimate=cost(
            4 * rank * depth * span * count * wide, span * count * (depth * wide + 3 * rank) * 2),
        name="project",
    )(
        ids, *[w[0] for w in work], *[w[1] for w in work], *([x] * count),
        *[w[3][d] for d in range(wide - 1) for w in work], *bases, *beside)


def folding(rank, width):
    best = 1
    for f in range(1, rank + 1):
        if rank % f == 0 and (rank // f) % 8 == 0 and f * width <= 128:
            best = f
    return best


def reverse_bits(p, count):
    return sum(1 << (count - 1 - b) for b in range(count) if (p >> b) & 1)


def column_order(depth, samp, per_node, width_cols):
    width = per_node * width_cols
    dst = np.arange(depth)
    a, rest = dst // (samp * width), dst % (samp * width)
    s, rest = rest // width, rest % width
    src = (a * per_node + rest // width_cols) * (samp * width_cols) + s * width_cols + rest % width_cols
    return jnp.asarray(np.arange(depth)[:, None] == src[None, :], BF16)


def tail(pieces, per_node, width_cols, t_ref, ids_ref, beside, *refs):
    outs, hold = refs[:-1], refs[-1]
    wide, rank, depth = t_ref.shape
    width = per_node * width_cols
    fold = folding(rank, width)
    tall = rank // fold
    me_node = ids_ref[ids_ref.shape[0] - 1]
    move = beside[0][...]
    bits = pieces.bit_length() - 1
    for w in range(wide):
        t = t_ref[w]
        high = t.astype(BF16)
        mid = (t - high.astype(F32)).astype(BF16)
        low = (t - high.astype(F32) - mid.astype(F32)).astype(BF16)
        moved = dot(jnp.concatenate([high, mid, low], axis=0), move, ((1,), (0,)))
        moved = moved[:rank] + moved[rank:2 * rank] + moved[2 * rank:]
        for i in range(pieces):
            piece = moved[:, i * width:(i + 1) * width]
            parts = [piece[f * tall:(f + 1) * tall] for f in range(fold)]
            if fold * width < 128:
                parts.append(jnp.zeros((tall, 128 - fold * width), F32))
            hold[i] = jnp.concatenate(parts, axis=1)
        for p in range(pieces):
            outs[w][p * tall:(p + 1) * tall, :] = hold[me_node ^ reverse_bits(p, bits)]


def finish_kernel(scale, per_node, width_cols, count, inv_ref, piece_ref, piece2_ref, *refs):
    both, high = refs[:count], refs[count:2 * count]
    low, core_ref, coef_ref = refs[2 * count:3 * count], refs[-2], refs[-1]
    rank = inv_ref.shape[0]
    inverse = inv_ref[...]
    at = 0
    for c in range(count):
        s = both[c][:rank, :].astype(F32) + both[c][rank:, :].astype(F32)
        rows = s.shape[1]
        s = s + (high[c][...].astype(F32) + low[c][...].astype(F32))
        core_ref[:, at:at + rows] = dot(inverse, s, ((1,), (0,)), HI)
        at += rows
    width = per_node * width_cols
    fold = folding(rank, width)
    total = piece_ref[...] + piece2_ref[...]
    total = jnp.concatenate([total[:, f * width:(f + 1) * width] for f in range(fold)], axis=0)
    out = dot(total, inverse, ((0,), (1,)), HI) * scale
    coef_ref[...] = jnp.concatenate(
        [out[p * width_cols:(p + 1) * width_cols, :] for p in range(per_node)], axis=1)


def finish(inverse, pieces, both, high, low, scale, per_node, width_cols):
    rank = inverse.shape[0]
    count = len(both)
    rows = sum(v.shape[1] for v in high)
    return pl.pallas_call(
        functools.partial(finish_kernel, scale, per_node, width_cols, count),
        out_shape=(
            jax.ShapeDtypeStruct((rank, rows), F32),
            jax.ShapeDtypeStruct((width_cols, per_node * rank), F32),
        ),
        compiler_params=params(),
        cost_estimate=cost(12 * rank * rank * rows, 12 * rank * rows),
        name="finish",
    )(inverse, *pieces, *both, *high, *low)


def swap(value, axis, size, bit):
    return lax.ppermute(value, axis, [(i, i ^ bit) for i in range(size)])


def body(snapshots, sketch_matrix):
    rows_all = snapshots.shape[0]
    rank = sketch_matrix.shape[1]
    samp = lax.axis_size("samp")
    node = lax.axis_size("node")
    total = rows_all * node
    quarter = rows_all // samp
    me_s = lax.axis_index("samp").astype(jnp.int32)
    me_n = lax.axis_index("node").astype(jnp.int32)
    w_t = sketch_matrix.T
    last = samp // 2
    near = range(1, last)
    starts, sizes = (0, UNIT), (UNIT, quarter - UNIT)
    blocks = [(last, 0), (last, 1), (0, 0), (0, 1)]

    def block_of(base, c):
        return (me_s ^ base) * (quarter // UNIT) + starts[c] // UNIT

    borrowed = {b: [] for b in blocks}
    ws, w_at = [w_t], 0

    def borrow(chosen, after, w=None):
        out = ()
        for d in near:
            out = lend(jnp.stack([block_of(b[0] ^ d, b[1]) for b in chosen]), snapshots, UNIT, w, after)
            for b, v in zip(chosen, out):
                borrowed[b].append(swap(v, "samp", samp, d))
            after = tuple(out[:1])
        return after

    done = borrow(blocks[:1], (), w_t)
    for v in borrowed[blocks[0]]:
        w_at = v.shape[0] - rank
        ws.append(v)
    borrow(blocks[1:], done)

    pairs, arrived, done = {}, {}, ()
    ids = jnp.stack([block_of(*b) for b in blocks] + [me_n])
    slot = {b: k for k, b in enumerate(blocks)}
    for k, b in enumerate(blocks):
        later = ()
        numbers = [block_of(*b)] + [block_of(o[0] ^ d, o[1]) for o in later for d in near]
        out = sketch(jnp.stack(numbers), snapshots, ws, borrowed[b], UNIT, w_at, done)
        pairs[b], high = out[:2]
        done = (high,)
        if k + 1 < len(blocks):
            arrived[b[0] ^ last, b[1]] = swap(high, "samp", samp, last)
        for o in later:
            borrowed[o] = [swap(v, "samp", samp, d) for d, v in zip(near, out[2:])]
    own = [pairs[0, c] for c in range(2)]
    got_high = [arrived[0, c] for c in range(2)]

    def parts(chosen):
        return [(pairs[b], arrived[b], slot[b], borrowed[b]) for b in chosen]

    gram = own_gram(own[0], got_high[0], None, None)
    t = project(ids, parts([(0, 0)]), snapshots, None, [gram])
    if PLACE[3]:
        t, gram = lax.optimization_barrier((t, gram))
    gram = own_gram(own[1], got_high[1], gram, 1.0 / total, done)
    t = project(ids, parts([(0, 1)]), snapshots, t, [gram])
    final = blocks[-1]
    late = [(final[0] ^ last, final[1])]
    high, t = lax.optimization_barrier((high, t))
    arrived[late[0]] = swap(high, "samp", samp, last)
    gram = gram + swap(gram, "samp", samp, last)
    got_low = []
    for c in range(2):
        low, _ = lax.optimization_barrier((pairs[last, c][rank:], gram))
        got_low.append(swap(low, "samp", samp, last))
    t = project(ids, parts([(last, 0)]), snapshots, t, [gram] if PLACE[4] else ())
    gram, t = lax.optimization_barrier((gram, t))
    bit = last // 2
    while bit:
        gram = gram + swap(gram, "samp", samp, bit)
        bit //= 2
    per_node = P1 // node
    width_cols = P2 // samp
    tall = rank // folding(rank, per_node * width_cols)
    messages = project(
        ids, parts(late), snapshots, t, [column_order(snapshots.shape[1], samp, per_node, width_cols)] + ([gram] if PLACE[0] else []),
        functools.partial(tail, node, per_node, width_cols),
        [jax.ShapeDtypeStruct((node * tall, 128), F32)] * last,
        [pltpu.VMEM((node, tall, 128), F32)])

    pieces = messages[0]
    for d in near:
        pieces = pieces + swap(messages[d], "samp", samp, d)
    bit = 1
    for k in range(node.bit_length() - 2):
        for c in range(2):
            if k == PLACE[1 + c]:
                pieces, got_low[c] = lax.optimization_barrier((pieces, got_low[c]))
        edge = pieces.shape[0] // 2
        got = swap(jnp.concatenate([pieces[edge:], gram], axis=0), "node", node, bit)
        pieces, gram = pieces[:edge] + got[:edge], gram + got[edge:]
        bit *= 2

    gram = gram + swap(gram, "node", node, bit)
    spread = node // samp
    landed = []
    for k, value in ((0, pieces[:tall]), (bit, pieces[tall:])):
        route = []
        for n in range(node):
            a, s_to = (n ^ k) // samp, (n ^ k) % samp
            for s_from in range(samp):
                route.append((n * samp + s_from, (s_from * spread + a) * samp + s_to))
        landed.append(lax.ppermute(value, ("node", "samp"), route))
    inverse = factor_inverse(gram, rank)
    core, coef = finish(inverse, landed, own, got_high, got_low, 1.0 / total, per_node, width_cols)
    return (core.T, coef.T)


def solution(mesh):
    placed = (P("node", "samp"), P("samp", None))
    return jax.shard_map(
        body,
        mesh=mesh,
        in_specs=placed,
        out_specs=(P(("node", "samp"), None), P("node", "samp")),
        check_vma=False,
    )
```

```python
import functools
import jax
import jax.numpy as jnp
import numpy as np
from jax import lax
from jax.experimental import pallas as pl
from jax.experimental.pallas import tpu as pltpu
from jax.sharding import PartitionSpec as P

P1 = 64
P2 = 32
BAND = 32
UNIT = 1024
LEND_STEPS = 2
PROJECT_ROWS = 512
PLACE = (False, -1, -1, True, False)
SKETCH_STEPS = 1
FACTOR_COST = 6e9
COST_CUT = 1
F32 = jnp.float32
BF16 = jnp.bfloat16
HI = lax.Precision.HIGHEST
UNREAD = pl.BlockSpec(memory_space=pl.ANY)
HELD = pl.BlockSpec(memory_space=pltpu.VMEM)
VMEM_LIMIT = 48 * 1024 * 1024


def iota(shape, dim):
    return lax.broadcasted_iota(jnp.int32, shape, dim)


def dot(a, b, dims, precision=None):
    return lax.dot_general(a, b, (dims, ((), ())), precision=precision, preferred_element_type=F32)


def params():
    return pltpu.CompilerParams(vmem_limit_bytes=VMEM_LIMIT)


def cost(flops, moved):
    return pl.CostEstimate(flops=int(flops) // COST_CUT, bytes_accessed=int(moved) // COST_CUT, transcendentals=0)


def lend_kernel(count, at, ids_ref, *refs):
    outs = refs[-count:]
    rows = refs[0].shape[0]
    for k in range(count):
        outs[k][:rows, :] = refs[k][...]
    if at is not None:
        outs[0][at:, :] = refs[count][...]


def lend(ids, x, size, w=None, after=()):
    count = ids.shape[0]
    depth = x.shape[1]
    steps = LEND_STEPS if w is None else 1
    rows = size // steps
    at, height, more, shapes = None, size, [], (rows, depth)
    if w is not None:
        rank = w.shape[0]
        at = -(-size // rank) * rank
        height = at + rank
        more, shapes = [w], (height, depth)
    return pl.pallas_call(
        functools.partial(lend_kernel, count, at),
        grid_spec=pltpu.PrefetchScalarGridSpec(
            num_scalar_prefetch=1,
            grid=(steps,),
            in_specs=[
                pl.BlockSpec((rows, depth), lambda i, ids, k=k: (ids[k] * steps + i, 0))
                for k in range(count)
            ] + [pl.BlockSpec(v.shape, lambda i, ids: (0, 0)) for v in more] + [UNREAD] * len(after),
            out_specs=[pl.BlockSpec(shapes, lambda i, ids: (i, 0))] * count,
        ),
        out_shape=[jax.ShapeDtypeStruct((height, depth), BF16)] * count,
        compiler_params=params(),
        cost_estimate=cost(0, 4 * count * height * depth),
        name="lend",
    )(ids, *([x] * count), *more, *after)


def sketch_kernel(count, lent, ids_ref, x_ref, *refs):
    w_refs, x_refs = refs[:count], (x_ref,) + refs[count:2 * count - 1]
    both_ref, high_ref = refs[len(refs) - lent - 2:len(refs) - lent]
    rank = high_ref.shape[0]
    for k in range(lent):
        refs[len(refs) - lent + k][...] = refs[2 * count - 1 + k][...]
    s = None
    for w_ref, ref in zip(w_refs, x_refs):
        term = dot(w_ref[...], ref[...], ((1,), (1,)))
        s = term if s is None else s + term
    high = s.astype(BF16)
    high_ref[...] = high
    both_ref[:rank, :] = high
    both_ref[rank:, :] = (s - high.astype(F32)).astype(BF16)


def sketch(ids, x, ws, extra, size, w_at, after=()):
    rank, depth = ws[0].shape
    count = len(ws)
    lent = ids.shape[0] - 1
    steps = SKETCH_STEPS
    rows = size // steps
    return pl.pallas_call(
        functools.partial(sketch_kernel, count, lent),
        grid_spec=pltpu.PrefetchScalarGridSpec(
            num_scalar_prefetch=1,
            grid=(steps,),
            in_specs=[pl.BlockSpec((rows, depth), lambda i, ids: (ids[0] * steps + i, 0))]
            + [pl.BlockSpec((rank, depth), lambda i, ids: (0, 0))]
            + [pl.BlockSpec((rank, depth), lambda i, ids: (w_at // rank, 0))] * (count - 1)
            + [pl.BlockSpec((rows, depth), lambda i, ids: (i, 0))] * (count - 1)
            + [pl.BlockSpec((rows, depth), lambda i, ids, k=k: (ids[1 + k] * steps + i, 0)) for k in range(lent)]
            + [UNREAD] * len(after),
            out_specs=[
                pl.BlockSpec((2 * rank, rows), lambda i, ids: (0, i)),
                pl.BlockSpec((rank, rows), lambda i, ids: (0, i)),
            ] + [pl.BlockSpec((rows, depth), lambda i, ids: (i, 0))] * lent,
        ),
        out_shape=[
            jax.ShapeDtypeStruct((2 * rank, size), BF16),
            jax.ShapeDtypeStruct((rank, size), BF16),
        ] + [jax.ShapeDtypeStruct((size, depth), BF16)] * lent,
        compiler_params=params(),
        cost_estimate=cost(
            2 * rank * depth * size * count, size * (depth * 2 * (count + 2 * lent) + rank * 6)),
        name="sketch",
    )(ids, x, *ws, *extra, *([x] * lent), *after)


def packing(rank):
    bands = rank // BAND
    pairs = [(i, j) for i in range(bands) for j in range(i, bands)]
    wide = 128 // BAND
    groups = -(-len(pairs) // wide)
    groups += groups % 2
    return pairs, wide, groups


def pack_gram(gram):
    pairs, wide, groups = packing(gram.shape[0])
    out = []
    for g in range(groups):
        chosen = pairs[g * wide:(g + 1) * wide]
        parts = [gram[i * BAND:(i + 1) * BAND, j * BAND:(j + 1) * BAND] for i, j in chosen]
        parts += [jnp.zeros((BAND, BAND), F32)] * (wide - len(chosen))
        out.append(jnp.concatenate(parts, axis=1))
    return jnp.concatenate(out, axis=0)


def fold_square(x, rank):
    return (x[:rank, :rank] + x[rank:, rank:]) + (x[:rank, rank:] + x[rank:, :rank])


def gram_kernel(scale, has_base, own_ref, got_ref, *refs):
    o_ref = refs[-1]
    rank = got_ref.shape[0]
    s = own_ref[:rank, :].astype(F32) + own_ref[rank:, :].astype(F32) + got_ref[...].astype(F32)
    high = s.astype(BF16)
    both = jnp.concatenate([high, (s - high.astype(F32)).astype(BF16)], axis=0)
    total = fold_square(dot(both, both, ((1,), (1,))), rank)
    if has_base:
        total = total + refs[0][...]
    o_ref[...] = total if scale is None else pack_gram(total * scale)


def own_gram(own, got, base, scale, after=()):
    rank, rows = got.shape
    bases = [] if base is None else [base]
    shape = (rank, rank) if scale is None else (packing(rank)[2] * BAND, 128)
    return pl.pallas_call(
        functools.partial(gram_kernel, scale, len(bases)),
        in_specs=[HELD] * (2 + len(bases)) + [UNREAD] * len(after),
        out_shape=jax.ShapeDtypeStruct(shape, F32),
        compiler_params=params(),
        cost_estimate=cost(8 * rank * rank * rows, 6 * rank * rows),
        name="gram",
    )(own, got, *bases, *after)


def wide_lanes(x, n):
    reps = -(-n // 128)
    return jnp.concatenate([x] * reps, axis=1)[:, :n] if reps > 1 else x[:, :n]


def band_rows(block, b):
    n = block.shape[1]
    count = BAND // 8
    part = [block[8 * i:8 * i + 8, :] for i in range(count)]
    sub = iota((8, n), 0)
    lane = iota((8, n), 1)
    for m in range(count):
        c0 = b * BAND + 8 * m
        live = count - m
        col = [
            [jnp.broadcast_to(part[m + i][:, c0 + k:c0 + k + 1], (8, 128)) for i in range(live)]
            for k in range(8)
        ]
        here = (lane >= c0) & (lane < c0 + 8)
        part[m] = jnp.where(here, jnp.where(lane - c0 == sub, 1.0, 0.0), part[m])
        for i in range(1, live):
            part[m + i] = jnp.where(here, 0.0, part[m + i])
        for j in range(8):
            inv_root = lax.rsqrt(jnp.broadcast_to(col[j][0][j:j + 1, :], (8, 128)))
            low = [x * inv_root for x in col[j]]
            for k in range(j + 1, 8):
                t = jnp.broadcast_to(low[0][k:k + 1, :], (8, 128))
                for i in range(live):
                    col[k][i] = col[k][i] - low[i] * t
            row = jnp.broadcast_to(part[m][j:j + 1, :], (8, n)) * wide_lanes(inv_root, n)
            for i in range(live):
                new = part[m + i] - wide_lanes(low[i], n) * row
                if i == 0:
                    new = jnp.where(sub > j, new, jnp.where(sub == j, row, part[m]))
                part[m + i] = new
    return jnp.concatenate(part, axis=0)


def factor_kernel(rank, g_ref, *refs):
    o_ref = refs[-1]
    pairs, wide, _ = packing(rank)
    o_ref[...] = jnp.zeros((rank, rank), F32)
    for at, (i, j) in enumerate(pairs):
        g, k = at // wide, at % wide
        o_ref[i * BAND:(i + 1) * BAND, j * BAND:(j + 1) * BAND] = g_ref[
            g * BAND:(g + 1) * BAND, k * BAND:(k + 1) * BAND]
    for b in range(rank // BAND):
        lo, hi = b * BAND, (b + 1) * BAND
        r = band_rows(o_ref[lo:hi, :], b)
        rows, cols = iota(r.shape, 0), iota(r.shape, 1)
        r = jnp.where((cols >= lo) & (cols < hi) & (cols - lo > rows), 0.0, r)
        o_ref[lo:hi, :] = jnp.where(cols < hi, r, 0.0)
        if hi < rank:
            left = jnp.where(cols >= hi, r, 0.0)
            update = dot(left, r, ((0,), (0,)), HI)
            kept = jnp.where(iota((rank - hi, rank), 1) // BAND == b, 0.0, o_ref[hi:, :])
            o_ref[hi:, :] = kept - update[hi:, :]


def factor_inverse(packed, rank, after=()):
    return pl.pallas_call(
        functools.partial(factor_kernel, rank),
        in_specs=[HELD] + [UNREAD] * len(after),
        out_shape=jax.ShapeDtypeStruct((rank, rank), F32),
        compiler_params=params(),
        cost_estimate=cost(FACTOR_COST, 4 * rank * rank),
        name="factor",
    )(packed, *after)


def project_kernel(count, wide, has_base, aside, finish, ids_ref, *refs):
    pair_refs, high_refs, x_refs = refs[:count], refs[count:2 * count], refs[2 * count:count * (2 + wide)]
    at = count * (2 + wide)
    beside = refs[at + has_base:at + has_base + aside]
    rest = refs[at + has_base + aside:]
    t_ref = rest[-1]
    rank = t_ref.shape[1]

    @pl.when(pl.program_id(0) == 0)
    def _():
        t_ref[...] = refs[at][...] if has_base else jnp.zeros_like(t_ref)

    sums = []
    for pair_ref, high_ref in zip(pair_refs, high_refs):
        s = pair_ref[:rank, :].astype(F32) + pair_ref[rank:, :].astype(F32) + high_ref[...].astype(F32)
        high = s.astype(BF16)
        sums.append(jnp.concatenate([high, (s - high.astype(F32)).astype(BF16)], axis=0))
    for w in range(wide):
        total = None
        for k in range(count):
            term = dot(sums[k], x_refs[w * count + k][...], ((1,), (0,)))
            total = term if total is None else total + term
        t_ref[w] += total[:rank] + total[rank:]
    if finish is not None:
        @pl.when(pl.program_id(0) == pl.num_programs(0) - 1)
        def _():
            finish(t_ref, ids_ref, beside, *rest[:-1])


def project(ids, work, x, base, beside=(), finish=None, outs=(), scratch=()):
    count = len(work)
    wide = 1 + len(work[0][3])
    rank, span = work[0][1].shape
    depth = x.shape[1]
    rows = min(span, PROJECT_ROWS)
    steps = span // rows
    bases = [] if base is None else [base]
    whole = pl.BlockSpec((wide, rank, depth), lambda i, ids: (0, 0, 0))
    t_shape = jax.ShapeDtypeStruct((wide, rank, depth), F32)
    if finish is None:
        out_specs, out_shape, scratch_shapes = whole, t_shape, []
    else:
        out_specs = [pl.BlockSpec(o.shape, lambda i, ids: (0, 0)) for o in outs]
        out_shape = list(outs)
        scratch_shapes = list(scratch) + [pltpu.VMEM((wide, rank, depth), F32)]
    return pl.pallas_call(
        functools.partial(project_kernel, count, wide, len(bases), len(beside), finish),
        grid_spec=pltpu.PrefetchScalarGridSpec(
            num_scalar_prefetch=1,
            grid=(steps,),
            in_specs=[pl.BlockSpec((2 * rank, rows), lambda i, ids: (0, i))] * count
            + [pl.BlockSpec((rank, rows), lambda i, ids: (0, i))] * count
            + [
                pl.BlockSpec((rows, depth), lambda i, ids, slot=w[2]: (ids[slot] * steps + i, 0))
                for w in work
            ]
            + [pl.BlockSpec((rows, depth), lambda i, ids: (i, 0))] * (count * (wide - 1))
            + [whole] * len(bases) + [pl.BlockSpec(v.shape, lambda i, ids: (0, 0)) for v in beside],
            out_specs=out_specs,
            scratch_shapes=scratch_shapes,
        ),
        out_shape=out_shape,
        compiler_params=params(),
        cost_estimate=cost(
            4 * rank * depth * span * count * wide, span * count * (depth * wide + 3 * rank) * 2),
        name="project",
    )(
        ids, *[w[0] for w in work], *[w[1] for w in work], *([x] * count),
        *[w[3][d] for d in range(wide - 1) for w in work], *bases, *beside)


def folding(rank, width):
    best = 1
    for f in range(1, rank + 1):
        if rank % f == 0 and (rank // f) % 8 == 0 and f * width <= 128:
            best = f
    return best


def reverse_bits(p, count):
    return sum(1 << (count - 1 - b) for b in range(count) if (p >> b) & 1)


def column_order(depth, samp, per_node, width_cols):
    width = per_node * width_cols
    dst = np.arange(depth)
    a, rest = dst // (samp * width), dst % (samp * width)
    s, rest = rest // width, rest % width
    src = (a * per_node + rest // width_cols) * (samp * width_cols) + s * width_cols + rest % width_cols
    return jnp.asarray(np.arange(depth)[:, None] == src[None, :], BF16)


def tail(pieces, per_node, width_cols, t_ref, ids_ref, beside, *refs):
    outs, hold = refs[:-1], refs[-1]
    wide, rank, depth = t_ref.shape
    width = per_node * width_cols
    fold = folding(rank, width)
    tall = rank // fold
    me_node = ids_ref[ids_ref.shape[0] - 1]
    move = beside[0][...]
    bits = pieces.bit_length() - 1
    for w in range(wide):
        t = t_ref[w]
        high = t.astype(BF16)
        mid = (t - high.astype(F32)).astype(BF16)
        low = (t - high.astype(F32) - mid.astype(F32)).astype(BF16)
        moved = dot(jnp.concatenate([high, mid, low], axis=0), move, ((1,), (0,)))
        moved = moved[:rank] + moved[rank:2 * rank] + moved[2 * rank:]
        for i in range(pieces):
            piece = moved[:, i * width:(i + 1) * width]
            parts = [piece[f * tall:(f + 1) * tall] for f in range(fold)]
            if fold * width < 128:
                parts.append(jnp.zeros((tall, 128 - fold * width), F32))
            hold[i] = jnp.concatenate(parts, axis=1)
        for p in range(pieces):
            outs[w][p * tall:(p + 1) * tall, :] = hold[me_node ^ reverse_bits(p, bits)]


def finish_kernel(scale, per_node, width_cols, count, inv_ref, piece_ref, piece2_ref, *refs):
    both, high = refs[:count], refs[count:2 * count]
    low, core_ref, coef_ref = refs[2 * count:3 * count], refs[-2], refs[-1]
    rank = inv_ref.shape[0]
    inverse = inv_ref[...]
    at = 0
    for c in range(count):
        s = both[c][:rank, :].astype(F32) + both[c][rank:, :].astype(F32)
        rows = s.shape[1]
        s = s + (high[c][...].astype(F32) + low[c][...].astype(F32))
        core_ref[:, at:at + rows] = dot(inverse, s, ((1,), (0,)), HI)
        at += rows
    width = per_node * width_cols
    fold = folding(rank, width)
    total = piece_ref[...] + piece2_ref[...]
    total = jnp.concatenate([total[:, f * width:(f + 1) * width] for f in range(fold)], axis=0)
    out = dot(total, inverse, ((0,), (1,)), HI) * scale
    coef_ref[...] = jnp.concatenate(
        [out[p * width_cols:(p + 1) * width_cols, :] for p in range(per_node)], axis=1)


def finish(inverse, pieces, both, high, low, scale, per_node, width_cols):
    rank = inverse.shape[0]
    count = len(both)
    rows = sum(v.shape[1] for v in high)
    return pl.pallas_call(
        functools.partial(finish_kernel, scale, per_node, width_cols, count),
        out_shape=(
            jax.ShapeDtypeStruct((rank, rows), F32),
            jax.ShapeDtypeStruct((width_cols, per_node * rank), F32),
        ),
        compiler_params=params(),
        cost_estimate=cost(12 * rank * rank * rows, 12 * rank * rows),
        name="finish",
    )(inverse, *pieces, *both, *high, *low)


def swap(value, axis, size, bit):
    return lax.ppermute(value, axis, [(i, i ^ bit) for i in range(size)])


def body(snapshots, sketch_matrix):
    rows_all = snapshots.shape[0]
    rank = sketch_matrix.shape[1]
    samp = lax.axis_size("samp")
    node = lax.axis_size("node")
    total = rows_all * node
    quarter = rows_all // samp
    me_s = lax.axis_index("samp").astype(jnp.int32)
    me_n = lax.axis_index("node").astype(jnp.int32)
    w_t = sketch_matrix.T
    last = samp // 2
    near = range(1, last)
    starts, sizes = (0, UNIT), (UNIT, quarter - UNIT)
    blocks = [(last, 0), (last, 1), (0, 0), (0, 1)]

    def block_of(base, c):
        return (me_s ^ base) * (quarter // UNIT) + starts[c] // UNIT

    borrowed = {b: [] for b in blocks}
    ws, w_at = [w_t], 0

    def borrow(chosen, after, w=None):
        out = ()
        for d in near:
            out = lend(jnp.stack([block_of(b[0] ^ d, b[1]) for b in chosen]), snapshots, UNIT, w, after)
            for b, v in zip(chosen, out):
                borrowed[b].append(swap(v, "samp", samp, d))
            after = tuple(out[:1])
        return after

    done = borrow(blocks[:1], (), w_t)
    for v in borrowed[blocks[0]]:
        w_at = v.shape[0] - rank
        ws.append(v)
    borrow(blocks[1:], done)

    pairs, arrived, done = {}, {}, ()
    ids = jnp.stack([block_of(*b) for b in blocks] + [me_n])
    slot = {b: k for k, b in enumerate(blocks)}
    for k, b in enumerate(blocks):
        later = ()
        numbers = [block_of(*b)] + [block_of(o[0] ^ d, o[1]) for o in later for d in near]
        out = sketch(jnp.stack(numbers), snapshots, ws, borrowed[b], UNIT, w_at, done)
        pairs[b], high = out[:2]
        done = (high,)
        if k + 1 < len(blocks):
            arrived[b[0] ^ last, b[1]] = swap(high, "samp", samp, last)
        for o in later:
            borrowed[o] = [swap(v, "samp", samp, d) for d, v in zip(near, out[2:])]
    own = [pairs[0, c] for c in range(2)]
    got_high = [arrived[0, c] for c in range(2)]

    def parts(chosen):
        return [(pairs[b], arrived[b], slot[b], borrowed[b]) for b in chosen]

    gram = own_gram(own[0], got_high[0], None, None)
    t = project(ids, parts([(0, 0)]), snapshots, None, [gram])
    if PLACE[3]:
        t, gram = lax.optimization_barrier((t, gram))
    gram = own_gram(own[1], got_high[1], gram, 1.0 / total, done)
    t = project(ids, parts([(0, 1)]), snapshots, t, [gram])
    final = blocks[-1]
    late = [(final[0] ^ last, final[1])]
    high, t = lax.optimization_barrier((high, t))
    arrived[late[0]] = swap(high, "samp", samp, last)
    gram = gram + swap(gram, "samp", samp, last)
    got_low = []
    for c in range(2):
        low, _ = lax.optimization_barrier((pairs[last, c][rank:], gram))
        got_low.append(swap(low, "samp", samp, last))
    t = project(ids, parts([(last, 0)]), snapshots, t, [gram] if PLACE[4] else ())
    gram, t = lax.optimization_barrier((gram, t))
    bit = last // 2
    while bit:
        gram = gram + swap(gram, "samp", samp, bit)
        bit //= 2
    per_node = P1 // node
    width_cols = P2 // samp
    tall = rank // folding(rank, per_node * width_cols)
    messages = project(
        ids, parts(late), snapshots, t, [column_order(snapshots.shape[1], samp, per_node, width_cols)] + ([gram] if PLACE[0] else []),
        functools.partial(tail, node, per_node, width_cols),
        [jax.ShapeDtypeStruct((node * tall, 128), F32)] * last,
        [pltpu.VMEM((node, tall, 128), F32)])

    pieces = messages[0]
    for d in near:
        pieces = pieces + swap(messages[d], "samp", samp, d)
    bit = 1
    for k in range(node.bit_length() - 2):
        for c in range(2):
            if k == PLACE[1 + c]:
                pieces, got_low[c] = lax.optimization_barrier((pieces, got_low[c]))
        edge = pieces.shape[0] // 2
        got = swap(jnp.concatenate([pieces[edge:], gram], axis=0), "node", node, bit)
        pieces, gram = pieces[:edge] + got[:edge], gram + got[edge:]
        bit *= 2

    gram = gram + swap(gram, "node", node, bit)
    spread = node // samp
    landed = []
    for k, value in ((0, pieces[:tall]), (bit, pieces[tall:])):
        route = []
        for n in range(node):
            a, s_to = (n ^ k) // samp, (n ^ k) % samp
            for s_from in range(samp):
                route.append((n * samp + s_from, (s_from * spread + a) * samp + s_to))
        landed.append(lax.ppermute(value, ("node", "samp"), route))
    inverse = factor_inverse(gram, rank)
    core, coef = finish(inverse, landed, own, got_high, got_low, 1.0 / total, per_node, width_cols)
    return (core.T, coef.T)


def solution(mesh):
    placed = (P("node", "samp"), P("samp", None))
    return jax.shard_map(
        body,
        mesh=mesh,
        in_specs=placed,
        out_specs=(P(("node", "samp"), None), P("node", "samp")),
        check_vma=False,
    )
```

```python
import functools
import jax
import jax.numpy as jnp
import numpy as np
from jax import lax
from jax.experimental import pallas as pl
from jax.experimental.pallas import tpu as pltpu
from jax.sharding import PartitionSpec as P

P1 = 64
P2 = 32
BAND = 32
UNIT = 1024
LEND_STEPS = 2
PROJECT_ROWS = 512
PLACE = (False, -1, -1, True, False)
SKETCH_STEPS = 2
FACTOR_COST = 6e9
COST_CUT = 1
F32 = jnp.float32
BF16 = jnp.bfloat16
HI = lax.Precision.HIGHEST
UNREAD = pl.BlockSpec(memory_space=pl.ANY)
HELD = pl.BlockSpec(memory_space=pltpu.VMEM)
VMEM_LIMIT = 48 * 1024 * 1024


def iota(shape, dim):
    return lax.broadcasted_iota(jnp.int32, shape, dim)


def dot(a, b, dims, precision=None):
    return lax.dot_general(a, b, (dims, ((), ())), precision=precision, preferred_element_type=F32)


def params():
    return pltpu.CompilerParams(vmem_limit_bytes=VMEM_LIMIT)


def cost(flops, moved):
    return pl.CostEstimate(flops=int(flops) // COST_CUT, bytes_accessed=int(moved) // COST_CUT, transcendentals=0)


def lend_kernel(count, at, ids_ref, *refs):
    outs = refs[-count:]
    rows = refs[0].shape[0]
    for k in range(count):
        outs[k][:rows, :] = refs[k][...]
    if at is not None:
        outs[0][at:, :] = refs[count][...]


def lend(ids, x, size, w=None, after=()):
    count = ids.shape[0]
    depth = x.shape[1]
    steps = LEND_STEPS if w is None else 1
    rows = size // steps
    at, height, more, shapes = None, size, [], (rows, depth)
    if w is not None:
        rank = w.shape[0]
        at = -(-size // rank) * rank
        height = at + rank
        more, shapes = [w], (height, depth)
    return pl.pallas_call(
        functools.partial(lend_kernel, count, at),
        grid_spec=pltpu.PrefetchScalarGridSpec(
            num_scalar_prefetch=1,
            grid=(steps,),
            in_specs=[
                pl.BlockSpec((rows, depth), lambda i, ids, k=k: (ids[k] * steps + i, 0))
                for k in range(count)
            ] + [pl.BlockSpec(v.shape, lambda i, ids: (0, 0)) for v in more] + [UNREAD] * len(after),
            out_specs=[pl.BlockSpec(shapes, lambda i, ids: (i, 0))] * count,
        ),
        out_shape=[jax.ShapeDtypeStruct((height, depth), BF16)] * count,
        compiler_params=params(),
        cost_estimate=cost(0, 4 * count * height * depth),
        name="lend",
    )(ids, *([x] * count), *more, *after)


def sketch_kernel(count, lent, ids_ref, x_ref, *refs):
    w_refs, x_refs = refs[:count], (x_ref,) + refs[count:2 * count - 1]
    both_ref, high_ref = refs[len(refs) - lent - 2:len(refs) - lent]
    rank = high_ref.shape[0]
    for k in range(lent):
        refs[len(refs) - lent + k][...] = refs[2 * count - 1 + k][...]
    s = None
    for w_ref, ref in zip(w_refs, x_refs):
        term = dot(w_ref[...], ref[...], ((1,), (1,)))
        s = term if s is None else s + term
    high = s.astype(BF16)
    high_ref[...] = high
    both_ref[:rank, :] = high
    both_ref[rank:, :] = (s - high.astype(F32)).astype(BF16)


def sketch(ids, x, ws, extra, size, w_at, after=()):
    rank, depth = ws[0].shape
    count = len(ws)
    lent = ids.shape[0] - 1
    steps = SKETCH_STEPS
    rows = size // steps
    return pl.pallas_call(
        functools.partial(sketch_kernel, count, lent),
        grid_spec=pltpu.PrefetchScalarGridSpec(
            num_scalar_prefetch=1,
            grid=(steps,),
            in_specs=[pl.BlockSpec((rows, depth), lambda i, ids: (ids[0] * steps + i, 0))]
            + [pl.BlockSpec((rank, depth), lambda i, ids: (0, 0))]
            + [pl.BlockSpec((rank, depth), lambda i, ids: (w_at // rank, 0))] * (count - 1)
            + [pl.BlockSpec((rows, depth), lambda i, ids: (i, 0))] * (count - 1)
            + [pl.BlockSpec((rows, depth), lambda i, ids, k=k: (ids[1 + k] * steps + i, 0)) for k in range(lent)]
            + [UNREAD] * len(after),
            out_specs=[
                pl.BlockSpec((2 * rank, rows), lambda i, ids: (0, i)),
                pl.BlockSpec((rank, rows), lambda i, ids: (0, i)),
            ] + [pl.BlockSpec((rows, depth), lambda i, ids: (i, 0))] * lent,
        ),
        out_shape=[
            jax.ShapeDtypeStruct((2 * rank, size), BF16),
            jax.ShapeDtypeStruct((rank, size), BF16),
        ] + [jax.ShapeDtypeStruct((size, depth), BF16)] * lent,
        compiler_params=params(),
        cost_estimate=cost(
            2 * rank * depth * size * count, size * (depth * 2 * (count + 2 * lent) + rank * 6)),
        name="sketch",
    )(ids, x, *ws, *extra, *([x] * lent), *after)


def packing(rank):
    bands = rank // BAND
    pairs = [(i, j) for i in range(bands) for j in range(i, bands)]
    wide = 128 // BAND
    groups = -(-len(pairs) // wide)
    groups += groups % 2
    return pairs, wide, groups


def pack_gram(gram):
    pairs, wide, groups = packing(gram.shape[0])
    out = []
    for g in range(groups):
        chosen = pairs[g * wide:(g + 1) * wide]
        parts = [gram[i * BAND:(i + 1) * BAND, j * BAND:(j + 1) * BAND] for i, j in chosen]
        parts += [jnp.zeros((BAND, BAND), F32)] * (wide - len(chosen))
        out.append(jnp.concatenate(parts, axis=1))
    return jnp.concatenate(out, axis=0)


def fold_square(x, rank):
    return (x[:rank, :rank] + x[rank:, rank:]) + (x[:rank, rank:] + x[rank:, :rank])


def gram_kernel(scale, has_base, own_ref, got_ref, *refs):
    o_ref = refs[-1]
    rank = got_ref.shape[0]
    s = own_ref[:rank, :].astype(F32) + own_ref[rank:, :].astype(F32) + got_ref[...].astype(F32)
    high = s.astype(BF16)
    both = jnp.concatenate([high, (s - high.astype(F32)).astype(BF16)], axis=0)
    total = fold_square(dot(both, both, ((1,), (1,))), rank)
    if has_base:
        total = total + refs[0][...]
    o_ref[...] = total if scale is None else pack_gram(total * scale)


def own_gram(own, got, base, scale, after=()):
    rank, rows = got.shape
    bases = [] if base is None else [base]
    shape = (rank, rank) if scale is None else (packing(rank)[2] * BAND, 128)
    return pl.pallas_call(
        functools.partial(gram_kernel, scale, len(bases)),
        in_specs=[HELD] * (2 + len(bases)) + [UNREAD] * len(after),
        out_shape=jax.ShapeDtypeStruct(shape, F32),
        compiler_params=params(),
        cost_estimate=cost(8 * rank * rank * rows, 6 * rank * rows),
        name="gram",
    )(own, got, *bases, *after)


def wide_lanes(x, n):
    reps = -(-n // 128)
    return jnp.concatenate([x] * reps, axis=1)[:, :n] if reps > 1 else x[:, :n]


def band_rows(block, b):
    n = block.shape[1]
    count = BAND // 8
    part = [block[8 * i:8 * i + 8, :] for i in range(count)]
    sub = iota((8, n), 0)
    lane = iota((8, n), 1)
    for m in range(count):
        c0 = b * BAND + 8 * m
        live = count - m
        col = [
            [jnp.broadcast_to(part[m + i][:, c0 + k:c0 + k + 1], (8, 128)) for i in range(live)]
            for k in range(8)
        ]
        here = (lane >= c0) & (lane < c0 + 8)
        part[m] = jnp.where(here, jnp.where(lane - c0 == sub, 1.0, 0.0), part[m])
        for i in range(1, live):
            part[m + i] = jnp.where(here, 0.0, part[m + i])
        for j in range(8):
            inv_root = lax.rsqrt(jnp.broadcast_to(col[j][0][j:j + 1, :], (8, 128)))
            low = [x * inv_root for x in col[j]]
            for k in range(j + 1, 8):
                t = jnp.broadcast_to(low[0][k:k + 1, :], (8, 128))
                for i in range(live):
                    col[k][i] = col[k][i] - low[i] * t
            row = jnp.broadcast_to(part[m][j:j + 1, :], (8, n)) * wide_lanes(inv_root, n)
            for i in range(live):
                new = part[m + i] - wide_lanes(low[i], n) * row
                if i == 0:
                    new = jnp.where(sub > j, new, jnp.where(sub == j, row, part[m]))
                part[m + i] = new
    return jnp.concatenate(part, axis=0)


def factor_kernel(rank, g_ref, *refs):
    o_ref = refs[-1]
    pairs, wide, _ = packing(rank)
    o_ref[...] = jnp.zeros((rank, rank), F32)
    for at, (i, j) in enumerate(pairs):
        g, k = at // wide, at % wide
        o_ref[i * BAND:(i + 1) * BAND, j * BAND:(j + 1) * BAND] = g_ref[
            g * BAND:(g + 1) * BAND, k * BAND:(k + 1) * BAND]
    for b in range(rank // BAND):
        lo, hi = b * BAND, (b + 1) * BAND
        r = band_rows(o_ref[lo:hi, :], b)
        rows, cols = iota(r.shape, 0), iota(r.shape, 1)
        r = jnp.where((cols >= lo) & (cols < hi) & (cols - lo > rows), 0.0, r)
        o_ref[lo:hi, :] = jnp.where(cols < hi, r, 0.0)
        if hi < rank:
            left = jnp.where(cols >= hi, r, 0.0)
            update = dot(left, r, ((0,), (0,)), HI)
            kept = jnp.where(iota((rank - hi, rank), 1) // BAND == b, 0.0, o_ref[hi:, :])
            o_ref[hi:, :] = kept - update[hi:, :]


def factor_inverse(packed, rank, after=()):
    return pl.pallas_call(
        functools.partial(factor_kernel, rank),
        in_specs=[HELD] + [UNREAD] * len(after),
        out_shape=jax.ShapeDtypeStruct((rank, rank), F32),
        compiler_params=params(),
        cost_estimate=cost(FACTOR_COST, 4 * rank * rank),
        name="factor",
    )(packed, *after)


def project_kernel(count, wide, has_base, aside, finish, ids_ref, *refs):
    pair_refs, high_refs, x_refs = refs[:count], refs[count:2 * count], refs[2 * count:count * (2 + wide)]
    at = count * (2 + wide)
    beside = refs[at + has_base:at + has_base + aside]
    rest = refs[at + has_base + aside:]
    t_ref = rest[-1]
    rank = t_ref.shape[1]

    @pl.when(pl.program_id(0) == 0)
    def _():
        t_ref[...] = refs[at][...] if has_base else jnp.zeros_like(t_ref)

    sums = []
    for pair_ref, high_ref in zip(pair_refs, high_refs):
        s = pair_ref[:rank, :].astype(F32) + pair_ref[rank:, :].astype(F32) + high_ref[...].astype(F32)
        high = s.astype(BF16)
        sums.append(jnp.concatenate([high, (s - high.astype(F32)).astype(BF16)], axis=0))
    for w in range(wide):
        total = None
        for k in range(count):
            term = dot(sums[k], x_refs[w * count + k][...], ((1,), (0,)))
            total = term if total is None else total + term
        t_ref[w] += total[:rank] + total[rank:]
    if finish is not None:
        @pl.when(pl.program_id(0) == pl.num_programs(0) - 1)
        def _():
            finish(t_ref, ids_ref, beside, *rest[:-1])


def project(ids, work, x, base, beside=(), finish=None, outs=(), scratch=()):
    count = len(work)
    wide = 1 + len(work[0][3])
    rank, span = work[0][1].shape
    depth = x.shape[1]
    rows = min(span, PROJECT_ROWS)
    steps = span // rows
    bases = [] if base is None else [base]
    whole = pl.BlockSpec((wide, rank, depth), lambda i, ids: (0, 0, 0))
    t_shape = jax.ShapeDtypeStruct((wide, rank, depth), F32)
    if finish is None:
        out_specs, out_shape, scratch_shapes = whole, t_shape, []
    else:
        out_specs = [pl.BlockSpec(o.shape, lambda i, ids: (0, 0)) for o in outs]
        out_shape = list(outs)
        scratch_shapes = list(scratch) + [pltpu.VMEM((wide, rank, depth), F32)]
    return pl.pallas_call(
        functools.partial(project_kernel, count, wide, len(bases), len(beside), finish),
        grid_spec=pltpu.PrefetchScalarGridSpec(
            num_scalar_prefetch=1,
            grid=(steps,),
            in_specs=[pl.BlockSpec((2 * rank, rows), lambda i, ids: (0, i))] * count
            + [pl.BlockSpec((rank, rows), lambda i, ids: (0, i))] * count
            + [
                pl.BlockSpec((rows, depth), lambda i, ids, slot=w[2]: (ids[slot] * steps + i, 0))
                for w in work
            ]
            + [pl.BlockSpec((rows, depth), lambda i, ids: (i, 0))] * (count * (wide - 1))
            + [whole] * len(bases) + [pl.BlockSpec(v.shape, lambda i, ids: (0, 0)) for v in beside],
            out_specs=out_specs,
            scratch_shapes=scratch_shapes,
        ),
        out_shape=out_shape,
        compiler_params=params(),
        cost_estimate=cost(
            4 * rank * depth * span * count * wide, span * count * (depth * wide + 3 * rank) * 2),
        name="project",
    )(
        ids, *[w[0] for w in work], *[w[1] for w in work], *([x] * count),
        *[w[3][d] for d in range(wide - 1) for w in work], *bases, *beside)


def folding(rank, width):
    best = 1
    for f in range(1, rank + 1):
        if rank % f == 0 and (rank // f) % 8 == 0 and f * width <= 128:
            best = f
    return best


def reverse_bits(p, count):
    return sum(1 << (count - 1 - b) for b in range(count) if (p >> b) & 1)


def column_order(depth, samp, per_node, width_cols):
    width = per_node * width_cols
    dst = np.arange(depth)
    a, rest = dst // (samp * width), dst % (samp * width)
    s, rest = rest // width, rest % width
    src = (a * per_node + rest // width_cols) * (samp * width_cols) + s * width_cols + rest % width_cols
    return jnp.asarray(np.arange(depth)[:, None] == src[None, :], BF16)


def tail(pieces, per_node, width_cols, t_ref, ids_ref, beside, *refs):
    outs, hold = refs[:-1], refs[-1]
    wide, rank, depth = t_ref.shape
    width = per_node * width_cols
    fold = folding(rank, width)
    tall = rank // fold
    me_node = ids_ref[ids_ref.shape[0] - 1]
    move = beside[0][...]
    bits = pieces.bit_length() - 1
    for w in range(wide):
        t = t_ref[w]
        high = t.astype(BF16)
        mid = (t - high.astype(F32)).astype(BF16)
        low = (t - high.astype(F32) - mid.astype(F32)).astype(BF16)
        moved = dot(jnp.concatenate([high, mid, low], axis=0), move, ((1,), (0,)))
        moved = moved[:rank] + moved[rank:2 * rank] + moved[2 * rank:]
        for i in range(pieces):
            piece = moved[:, i * width:(i + 1) * width]
            parts = [piece[f * tall:(f + 1) * tall] for f in range(fold)]
            if fold * width < 128:
                parts.append(jnp.zeros((tall, 128 - fold * width), F32))
            hold[i] = jnp.concatenate(parts, axis=1)
        for p in range(pieces):
            outs[w][p * tall:(p + 1) * tall, :] = hold[me_node ^ reverse_bits(p, bits)]


def finish_kernel(scale, per_node, width_cols, count, inv_ref, piece_ref, piece2_ref, *refs):
    both, high = refs[:count], refs[count:2 * count]
    low, core_ref, coef_ref = refs[2 * count:3 * count], refs[-2], refs[-1]
    rank = inv_ref.shape[0]
    inverse = inv_ref[...]
    at = 0
    for c in range(count):
        s = both[c][:rank, :].astype(F32) + both[c][rank:, :].astype(F32)
        rows = s.shape[1]
        s = s + (high[c][...].astype(F32) + low[c][...].astype(F32))
        core_ref[:, at:at + rows] = dot(inverse, s, ((1,), (0,)), HI)
        at += rows
    width = per_node * width_cols
    fold = folding(rank, width)
    total = piece_ref[...] + piece2_ref[...]
    total = jnp.concatenate([total[:, f * width:(f + 1) * width] for f in range(fold)], axis=0)
    out = dot(total, inverse, ((0,), (1,)), HI) * scale
    coef_ref[...] = jnp.concatenate(
        [out[p * width_cols:(p + 1) * width_cols, :] for p in range(per_node)], axis=1)


def finish(inverse, pieces, both, high, low, scale, per_node, width_cols):
    rank = inverse.shape[0]
    count = len(both)
    rows = sum(v.shape[1] for v in high)
    return pl.pallas_call(
        functools.partial(finish_kernel, scale, per_node, width_cols, count),
        out_shape=(
            jax.ShapeDtypeStruct((rank, rows), F32),
            jax.ShapeDtypeStruct((width_cols, per_node * rank), F32),
        ),
        compiler_params=params(),
        cost_estimate=cost(12 * rank * rank * rows, 12 * rank * rows),
        name="finish",
    )(inverse, *pieces, *both, *high, *low)


def swap(value, axis, size, bit):
    return lax.ppermute(value, axis, [(i, i ^ bit) for i in range(size)])


def body(snapshots, sketch_matrix):
    rows_all = snapshots.shape[0]
    rank = sketch_matrix.shape[1]
    samp = lax.axis_size("samp")
    node = lax.axis_size("node")
    total = rows_all * node
    quarter = rows_all // samp
    me_s = lax.axis_index("samp").astype(jnp.int32)
    me_n = lax.axis_index("node").astype(jnp.int32)
    w_t = sketch_matrix.T
    last = samp // 2
    near = range(1, last)
    starts, sizes = (0, UNIT), (UNIT, quarter - UNIT)
    blocks = [(last, 0), (last, 1), (0, 0), (0, 1)]

    def block_of(base, c):
        return (me_s ^ base) * (quarter // UNIT) + starts[c] // UNIT

    borrowed = {b: [] for b in blocks}
    ws, w_at = [w_t], 0

    def borrow(chosen, after, w=None):
        out = ()
        for d in near:
            out = lend(jnp.stack([block_of(b[0] ^ d, b[1]) for b in chosen]), snapshots, UNIT, w, after)
            for b, v in zip(chosen, out):
                borrowed[b].append(swap(v, "samp", samp, d))
            after = tuple(out[:1])
        return after

    done = borrow(blocks[:1], (), w_t)
    for v in borrowed[blocks[0]]:
        w_at = v.shape[0] - rank
        ws.append(v)
    borrow(blocks[1:], done)

    pairs, arrived, done = {}, {}, ()
    ids = jnp.stack([block_of(*b) for b in blocks] + [me_n])
    slot = {b: k for k, b in enumerate(blocks)}
    for k, b in enumerate(blocks):
        later = ()
        numbers = [block_of(*b)] + [block_of(o[0] ^ d, o[1]) for o in later for d in near]
        out = sketch(jnp.stack(numbers), snapshots, ws, borrowed[b], UNIT, w_at, done)
        pairs[b], high = out[:2]
        done = (high,)
        if k + 1 < len(blocks):
            arrived[b[0] ^ last, b[1]] = swap(high, "samp", samp, last)
        for o in later:
            borrowed[o] = [swap(v, "samp", samp, d) for d, v in zip(near, out[2:])]
    own = [pairs[0, c] for c in range(2)]
    got_high = [arrived[0, c] for c in range(2)]

    def parts(chosen):
        return [(pairs[b], arrived[b], slot[b], borrowed[b]) for b in chosen]

    gram = own_gram(own[0], got_high[0], None, None)
    t = project(ids, parts([(0, 0)]), snapshots, None, [gram])
    if PLACE[3]:
        t, gram = lax.optimization_barrier((t, gram))
    gram = own_gram(own[1], got_high[1], gram, 1.0 / total, done)
    t = project(ids, parts([(0, 1)]), snapshots, t, [gram])
    final = blocks[-1]
    late = [(final[0] ^ last, final[1])]
    high, t = lax.optimization_barrier((high, t))
    arrived[late[0]] = swap(high, "samp", samp, last)
    gram = gram + swap(gram, "samp", samp, last)
    got_low = []
    for c in range(2):
        low, _ = lax.optimization_barrier((pairs[last, c][rank:], gram))
        got_low.append(swap(low, "samp", samp, last))
    t = project(ids, parts([(last, 0)]), snapshots, t, [gram] if PLACE[4] else ())
    gram, t = lax.optimization_barrier((gram, t))
    bit = last // 2
    while bit:
        gram = gram + swap(gram, "samp", samp, bit)
        bit //= 2
    per_node = P1 // node
    width_cols = P2 // samp
    tall = rank // folding(rank, per_node * width_cols)
    messages = project(
        ids, parts(late), snapshots, t, [column_order(snapshots.shape[1], samp, per_node, width_cols)] + ([gram] if PLACE[0] else []),
        functools.partial(tail, node, per_node, width_cols),
        [jax.ShapeDtypeStruct((node * tall, 128), F32)] * last,
        [pltpu.VMEM((node, tall, 128), F32)])

    pieces = messages[0]
    for d in near:
        pieces = pieces + swap(messages[d], "samp", samp, d)
    bit = 1
    for k in range(node.bit_length() - 2):
        for c in range(2):
            if k == PLACE[1 + c]:
                pieces, got_low[c] = lax.optimization_barrier((pieces, got_low[c]))
        edge = pieces.shape[0] // 2
        got = swap(jnp.concatenate([pieces[edge:], gram], axis=0), "node", node, bit)
        pieces, gram = pieces[:edge] + got[:edge], gram + got[edge:]
        bit *= 2

    gram = gram + swap(gram, "node", node, bit)
    spread = node // samp
    landed = []
    for k, value in ((0, pieces[:tall]), (bit, pieces[tall:])):
        route = []
        for n in range(node):
            a, s_to = (n ^ k) // samp, (n ^ k) % samp
            for s_from in range(samp):
                route.append((n * samp + s_from, (s_from * spread + a) * samp + s_to))
        landed.append(lax.ppermute(value, ("node", "samp"), route))
    inverse = factor_inverse(gram, rank)
    core, coef = finish(inverse, landed, own, got_high, got_low, 1.0 / total, per_node, width_cols)
    return (core.T, coef.T)


def solution(mesh):
    placed = (P("node", "samp"), P("samp", None))
    return jax.shard_map(
        body,
        mesh=mesh,
        in_specs=placed,
        out_specs=(P(("node", "samp"), None), P("node", "samp")),
        check_vma=False,
    )
```
